32 devices in a mesh: rep: 8 (over z, y), shard: 4 (over x, core).
Axes of the slice: x: 2, y: 2, z: 4, core: 2. Of those that a mesh axis runs over, the one named last changes fastest.
Arguments:
- block_input: bfloat16 [8, 1024, 1088], P('rep', 'shard'), may hold values from -6 to 6
- first_gain: bfloat16 [1088], P('shard'), may hold values from 0.5 to 1.5
- first_shift: bfloat16 [1088], P('shard'), may hold values from -4 to 4
- query_key_value_weight: bfloat16 [1088, 3264], P('shard'), may hold values from -0.1875 to 0.1875
- query_bias: bfloat16 [1088], P('shard'), may hold values from -4 to 4
- value_bias: bfloat16 [1088], P('shard'), may hold values from -4 to 4
- attention_output_weight: bfloat16 [1088, 1088], P('shard'), may hold values from -0.75 to 0.75
- attention_output_bias: bfloat16 [1088], P('shard'), may hold values from -4 to 4
- second_gain: bfloat16 [1088], P('shard'), may hold values from 0.5 to 1.5
- second_shift: bfloat16 [1088], P('shard'), may hold values from -4 to 4
- up_weight: bfloat16 [1088, 4352], P('shard'), may hold values from -0.1875 to 0.1875
- up_bias: bfloat16 [4352], P('shard'), may hold values from -6 to 6
- down_weight: bfloat16 [4352, 1088], P('shard'), may hold values from -0.09375 to 0.09375
- down_bias: bfloat16 [1088], P('shard'), may hold values from -4 to 4
- cotangent: float32 [8, 1024, 1088], P('rep', 'shard'), may hold values from -8 to 8
Outputs:
- block_output: float32 [8, 1024, 1088], P('rep', 'shard')
- input_grad: float32 [8, 1024, 1088], P('rep', 'shard')
- first_gain_grad: float32 [1088], P('shard')
- first_shift_grad: float32 [1088], P('shard')
- input_weight_grad: float32 [1088, 3264], P('shard')
- query_bias_grad: float32 [1088], P('shard')
- value_bias_grad: float32 [1088], P('shard')
- output_weight_grad: float32 [1088, 1088], P('shard')
- output_bias_grad: float32 [1088], P('shard')
- second_gain_grad: float32 [1088], P('shard')
- second_shift_grad: float32 [1088], P('shard')
- up_weight_grad: float32 [1088, 4352], P('shard')
- up_bias_grad: float32 [4352], P('shard')
- down_weight_grad: float32 [4352, 1088], P('shard')
- down_bias_grad: float32 [1088], P('shard')
The draws below stay inside these ranges and needn't reach their ends.
All inputs are finite; a program needn't handle non-finite values.
Results may differ from the reference program's by a relative error of at most 0.017.
Values may be sent and summed in bfloat16 or wider, within the bound.
No kernel may reach another device: no remote copies, remote signals or barrier semaphores. Data moves between devices by JAX's collectives and lax.ppermute only.
A program may use at most 192 MiB of HBM per device.

```python
import math
import jax
import jax.numpy as jnp
from jax import lax

HEADS = 17
HEAD_DIM = 64
D = 1088
FF = 4352
LENGTH = 1024
BATCH = 8


def draw_cotangent(key, part):
    key = jax.random.fold_in(key, 7)
    sample = jnp.clip(jax.random.normal(key, (BATCH, LENGTH, D), jnp.float32), -4.0, 4.0)
    rising = 3.0 ** (jnp.arange(BATCH, dtype=jnp.float32) / max(BATCH - 1, 1))
    return sample * (0.6 * rising)[:, None, None]


def block_levels(own_key, dims, shards, least, high):
    loudness, own = 1.0, jax.random.fold_in(own_key, 6)
    for axis_at, blocks in shards:
        heights = jnp.exp(jax.random.uniform(jax.random.fold_in(own, axis_at), (blocks,), jnp.float32, least / len(shards), high / len(shards)))
        loudness = loudness * jnp.repeat(heights, dims[axis_at] // blocks).reshape([-1 if axis == axis_at else 1 for axis in range(len(dims))])
    return loudness


def noise(rng, dims, deviation, reach, split=(), held_as=jnp.bfloat16):
    array = jax.random.normal(rng, dims, jnp.float32) * deviation
    if len(split) > 0:
        array = block_levels(rng, dims, split, -0.22, 0.18) * array
    return jnp.clip(array, min=-reach, max=reach).astype(held_as)


def setup_inputs(seed: int = 0) -> dict:
    seeds = jax.random.split(jax.random.key(seed), 16)
    return {
        "block_input": noise(seeds[0], (BATCH, LENGTH, D), 1.0, 6.0, ((0, 8), (1, 4))),
        "first_gain": jnp.clip(1.0 + 0.1 * jax.random.normal(seeds[1], (D,), jnp.float32), 0.5, 1.5).astype(jnp.bfloat16),
        "first_shift": noise(seeds[2], (D,), 0.3, 4.0, ((0, 4),)),
        "query_key_value_weight": noise(seeds[3], (D, 3 * D), D ** -0.5, 0.1875, ((0, 4),)),
        "query_bias": noise(seeds[4], (D,), 0.3, 4.0, ((0, 4),)),
        "value_bias": noise(seeds[5], (D,), 0.3, 4.0, ((0, 4),)),
        "attention_output_weight": noise(seeds[6], (D, D), (D // 16) ** -0.5, 0.75, ((0, 4),)),
        "attention_output_bias": noise(seeds[7], (D,), 0.3, 4.0, ((0, 4),)),
        "second_gain": jnp.clip(1.0 + 0.1 * jax.random.normal(seeds[8], (D,), jnp.float32), 0.5, 1.5).astype(jnp.bfloat16),
        "second_shift": noise(seeds[9], (D,), 0.3, 4.0, ((0, 4),)),
        "up_weight": noise(seeds[10], (D, FF), D ** -0.5, 0.1875, ((0, 4),)),
        "up_bias": noise(seeds[11], (FF,), 0.5, 6.0, ((0, 4),)),
        "down_weight": noise(seeds[12], (FF, D), FF ** -0.5, 0.09375, ((0, 4),)),
        "down_bias": noise(seeds[13], (D,), 0.3, 4.0, ((0, 4),)),
        "cotangent": draw_cotangent(jax.random.fold_in(seeds[15], 71), 0),
    }


@jax.custom_vjp
def low(v):
    return lax.optimization_barrier(v.astype(jnp.bfloat16)).astype(jnp.float32)

@jax.custom_vjp
def low_back(v):
    return v

def low_keep(v):
    return (low(v), None)

def low_pass(kept, grad):
    return (grad,)

def back_keep(v):
    return (v, None)

def back_low(kept, grad):
    return (low(grad),)
low.defvjp(low_keep, low_pass)
low_back.defvjp(back_keep, back_low)

def layer_norm(values, gain, shift):
    centre = lax.optimization_barrier(jnp.mean(values, axis=-1, keepdims=True))
    centred = values - centre
    variance = lax.optimization_barrier(jnp.mean(centred * centred, axis=-1, keepdims=True))
    return centred * lax.rsqrt(variance + 1e-05) * gain + shift

def attend(parts):
    queries, keys, values = parts
    length = queries.shape[0]
    head_query = queries.reshape(length, HEADS, HEAD_DIM)
    head_key = keys.reshape(length, HEADS, HEAD_DIM)
    head_value = values.reshape(length, HEADS, HEAD_DIM)
    raw_scores = jnp.einsum('ihe,jhe->hij', head_query, head_key, precision=lax.Precision.HIGHEST) * 0.125
    scores = low_back(raw_scores)
    position = jnp.arange(length)
    causal = position[:, None] >= position[None, :]
    scores = jnp.where(causal[None], scores, -jnp.inf)
    log_total = jax.nn.logsumexp(scores, axis=-1, keepdims=True)
    weights_low = low(jnp.exp(scores - log_total))
    mixed = jnp.einsum('hij,jhe->ihe', weights_low, head_value, precision=lax.Precision.HIGHEST)
    return mixed.reshape(length, HEADS * HEAD_DIM)

def block(layer_input, params):
    first_gain, first_shift, query_key_value_weight, query_bias, value_bias, attention_output_weight, attention_output_bias, second_gain, second_shift, up_weight, up_bias, down_weight, down_bias = params
    precision_highest = lax.Precision.HIGHEST
    first_residual = low(layer_norm(layer_input, first_gain, first_shift))
    attention_projected = jnp.einsum('ias,sm->iam', first_residual, query_key_value_weight, precision=precision_highest)
    queries = low_back(low(attention_projected[..., :D] + query_bias))
    keys = low_back(low(attention_projected[..., D:2 * D]))
    values = low_back(low(attention_projected[..., 2 * D:] + value_bias))
    attention_context = lax.map(jax.checkpoint(attend), (queries, keys, values))
    attention_context = low_back(low(attention_context))
    residual_middle = layer_input + low_back(jnp.einsum('ias,sm->iam', attention_context, attention_output_weight, precision=precision_highest) + attention_output_bias)
    hidden_two = low(layer_norm(residual_middle, second_gain, second_shift))
    before = low_back(jnp.einsum('gld,df->glf', hidden_two, up_weight, precision=precision_highest) + up_bias)
    activated = low(jax.nn.gelu(before, approximate=False))
    return residual_middle + low_back(jnp.einsum('glf,fd->gld', activated, down_weight, precision=precision_highest) + down_bias)

def reference(block_input, first_gain, first_shift, query_key_value_weight, query_bias, value_bias, attention_output_weight, attention_output_bias, second_gain, second_shift, up_weight, up_bias, down_weight, down_bias, cotangent):
    params = tuple((p.astype(jnp.float32) for p in (first_gain, first_shift, query_key_value_weight, query_bias, value_bias, attention_output_weight, attention_output_bias, second_gain, second_shift, up_weight, up_bias, down_weight, down_bias)))
    per_map = math.gcd(BATCH, max(1, 4096 // LENGTH))
    grouped = block_input.astype(jnp.float32).reshape(BATCH // per_map, per_map, LENGTH, D)

    def forward(grouped_in, weights):

        def one_group(piece):
            return jax.checkpoint(block)(piece, weights)
        return lax.map(one_group, grouped_in)
    result, pullback = jax.vjp(forward, grouped, params)
    grad_in, grads = pullback(cotangent.astype(jnp.float32).reshape(BATCH // per_map, per_map, LENGTH, D))
    return (result.reshape(BATCH, LENGTH, D), grad_in.reshape(BATCH, LENGTH, D), grads[0], grads[1], grads[2], grads[3], grads[4], grads[5], grads[6], grads[7], grads[8], grads[9], grads[10], grads[11], grads[12])
```

```python
import functools

import jax
import jax.numpy as jnp
from jax import lax
from jax.experimental import pallas as pl
from jax.experimental.pallas import tpu as pltpu
from jax.sharding import PartitionSpec as P

HEADS = 17

epsilon = 1e-05
score_scale = 0.125
low = jnp.bfloat16
f32 = jnp.float32


def normalize(values):
    centre = jnp.mean(values, axis=-1, keepdims=True)
    centred = values - centre
    inverse = lax.rsqrt(jnp.mean(centred * centred, axis=-1, keepdims=True) + epsilon)
    return (centred * inverse, inverse)


def norm_back(grad, normed, inverse, gain):
    scaled = grad * gain
    first = jnp.mean(scaled, axis=-1, keepdims=True)
    second = jnp.mean(scaled * normed, axis=-1, keepdims=True)
    return inverse * (scaled - first - normed * second)


def gelu_parts(values):
    cumulative = 0.5 * (1.0 + lax.erf(values * 0.7071067811865476))
    density = jnp.exp(-0.5 * values * values) * 0.3989422804014327
    return values * cumulative, cumulative + values * density


def contract(left, right, left_dim, right_dim):
    return lax.dot_general(
        left, right, (((left_dim,), (right_dim,)), ((), ())), preferred_element_type=f32
    )


def swap(values, bit):
    size = lax.axis_size("shard")
    return lax.ppermute(values, "shard", [(i, i ^ bit) for i in range(size)])


def bits_far_first():
    bit = lax.axis_size("shard") // 2
    bits = []
    while bit:
        bits.append(bit)
        bit //= 2
    return bits


def relative_order():
    order = [0]
    for bit in bits_far_first():
        order = order + [o ^ bit for o in order]
    return order


def gather_relative(block):
    stack = block[None]
    for bit in bits_far_first():
        stack = jnp.concatenate([stack, swap(stack, bit)], axis=0)
    return stack


def gather_absolute(block):
    index = lax.axis_index("shard")
    stack = block[None]
    for bit in bits_far_first():
        other = swap(stack, bit)
        upper = (index & bit) != 0
        pair = jnp.stack(
            [jnp.where(upper, other, stack), jnp.where(upper, stack, other)], axis=1
        )
        stack = pair.reshape((2 * stack.shape[0],) + block.shape)
    return stack


def scatter_relative(parts):
    for bit in reversed(bits_far_first()):
        half = parts.shape[0] // 2
        other = swap(parts[half:].astype(low), bit)
        parts = parts[:half] + other.astype(f32)
    return parts[0]


def exchange(blocks):
    size = lax.axis_size("shard")
    index = lax.axis_index("shard")
    result = jnp.zeros_like(blocks)
    for offset in range(size):
        peer = index ^ offset
        piece = lax.dynamic_index_in_dim(blocks, peer, 0, keepdims=True)
        if offset:
            piece = swap(piece, offset)
        result = lax.dynamic_update_slice_in_dim(result, piece, peer, 0)
    return result


def visible_part(scores, top, block, fill):
    rows = lax.broadcasted_iota(jnp.int32, (block, block), 0)
    cols = lax.broadcasted_iota(jnp.int32, (block, block), 1)
    last = jnp.where(rows <= cols, scores[top:], fill)
    if top == 0:
        return last
    return jnp.concatenate([scores[:top], last], axis=0)


def turn(values):
    return values.astype(f32).T


def forward_kernel(blocks, block, place, q_ref, k_ref, v_ref, o_ref, low_ref, log_ref, k_rows, v_cols):
    for i in range(blocks):
        here = pl.ds(pl.multiple_of(place[i] * block, block), block)
        there = pl.ds(i * block, block)
        k_rows[there, :] = turn(k_ref[:, here]).astype(low)
        v_cols[:, there] = v_ref[:, here]
    for i in range(blocks):
        here = pl.ds(pl.multiple_of(place[i] * block, block), block)
        top = i * block
        count = top + block
        q_cols = q_ref[:, here] * jnp.asarray(score_scale, low)
        scores = contract(k_rows[:count, :], q_cols, 1, 0)
        scores = visible_part(scores, top, block, -jnp.inf)
        peak = jnp.max(scores, axis=0, keepdims=True)
        weights = jnp.exp(scores - peak)
        total = jnp.sum(weights, axis=0, keepdims=True)
        mixed = contract(v_cols[:, :count], weights.astype(low), 1, 0) / total
        o_ref[:, here] = mixed
        low_ref[:, here] = mixed.astype(low)
        log_ref[0, :, here] = peak + jnp.log(total)


def backward_kernel(
    blocks,
    block,
    place,
    q_ref,
    k_ref,
    v_ref,
    g_ref,
    o_ref,
    log_ref,
    dq_ref,
    dk_ref,
    dv_ref,
    k_rows,
    v_rows,
    k_cols,
    dk_rows,
    dv_rows,
):
    for i in range(blocks):
        here = pl.ds(pl.multiple_of(place[i] * block, block), block)
        there = pl.ds(i * block, block)
        k_rows[there, :] = turn(k_ref[:, here]).astype(low)
        v_rows[there, :] = turn(v_ref[:, here]).astype(low)
        k_cols[:, there] = k_ref[:, here]
    for i in reversed(range(blocks)):
        here = pl.ds(pl.multiple_of(place[i] * block, block), block)
        top = i * block
        count = top + block
        q_cols = q_ref[:, here] * jnp.asarray(score_scale, low)
        g_cols = g_ref[:, here]
        q_rows = turn(q_cols).astype(low)
        g_rows = turn(g_cols).astype(low)
        correction = jnp.sum(g_cols.astype(f32) * o_ref[:, here], axis=0, keepdims=True)
        scores = contract(k_rows[:count, :], q_cols, 1, 0)
        probs = jnp.exp(scores - log_ref[0, :, here])
        probs = visible_part(probs, top, block, 0.0)
        grad_probs = contract(v_rows[:count, :], g_cols, 1, 0)
        grad_scores = (probs * (grad_probs - correction)).astype(low)
        dv_part = contract(probs.astype(low), g_rows, 1, 0)
        dk_part = contract(grad_scores, q_rows, 1, 0)
        if i == blocks - 1:
            dv_rows[:count, :] = dv_part
            dk_rows[:count, :] = dk_part
        else:
            dv_rows[:count, :] += dv_part
            dk_rows[:count, :] += dk_part
        dq = contract(k_cols[:, :count], grad_scores, 1, 0) * score_scale
        dq_ref[:, here] = dq.astype(low)
    for i in range(blocks):
        here = pl.ds(pl.multiple_of(place[i] * block, block), block)
        there = pl.ds(i * block, block)
        dk_ref[:, here] = dk_rows[there, :].T.astype(low)
        dv_ref[:, here] = dv_rows[there, :].T.astype(low)


def head_spec(size, length, first):
    return pl.BlockSpec((size, length), lambda h, place: (first + h, 0))


def attend_forward(place, projected, heads, block):
    size = projected.shape[0] // (3 * heads)
    length = projected.shape[1]
    blocks = length // block
    row = pl.BlockSpec((1, 1, length), lambda h, place: (h, 0, 0))
    return pl.pallas_call(
        functools.partial(forward_kernel, blocks, block),
        grid_spec=pltpu.PrefetchScalarGridSpec(
            num_scalar_prefetch=1,
            grid=(heads,),
            in_specs=[
                head_spec(size, length, 0),
                head_spec(size, length, heads),
                head_spec(size, length, 2 * heads),
            ],
            out_specs=[head_spec(size, length, 0), head_spec(size, length, 0), row],
            scratch_shapes=[
                pltpu.VMEM((length, size), low),
                pltpu.VMEM((size, length), low),
            ],
        ),
        out_shape=[
            jax.ShapeDtypeStruct((heads * size, length), f32),
            jax.ShapeDtypeStruct((heads * size, length), low),
            jax.ShapeDtypeStruct((heads, 1, length), f32),
        ],
        cost_estimate=pl.CostEstimate(
            flops=4 * heads * length * length * size,
            bytes_accessed=heads * length * size * 12,
            transcendentals=heads * length * length,
        ),
        compiler_params=pltpu.CompilerParams(vmem_limit_bytes=32 * 1024 * 1024),
        name="attend_forward",
    )(place, projected, projected, projected)


def attend_backward(place, projected, grad, mixed, log_total, heads, block):
    size = projected.shape[0] // (3 * heads)
    length = projected.shape[1]
    blocks = length // block
    row = pl.BlockSpec((1, 1, length), lambda h, place: (h, 0, 0))
    out = jax.ShapeDtypeStruct((heads * size, length), low)
    return pl.pallas_call(
        functools.partial(backward_kernel, blocks, block),
        grid_spec=pltpu.PrefetchScalarGridSpec(
            num_scalar_prefetch=1,
            grid=(heads,),
            in_specs=[
                head_spec(size, length, 0),
                head_spec(size, length, heads),
                head_spec(size, length, 2 * heads),
                head_spec(size, length, 0),
                head_spec(size, length, 0),
                row,
            ],
            out_specs=[head_spec(size, length, 0)] * 3,
            scratch_shapes=[
                pltpu.VMEM((length, size), low),
                pltpu.VMEM((length, size), low),
                pltpu.VMEM((size, length), low),
                pltpu.VMEM((length, size), f32),
                pltpu.VMEM((length, size), f32),
            ],
        ),
        out_shape=[out, out, out],
        cost_estimate=pl.CostEstimate(
            flops=10 * heads * length * length * size,
            bytes_accessed=heads * length * size * 20,
            transcendentals=heads * length * length,
        ),
        compiler_params=pltpu.CompilerParams(vmem_limit_bytes=32 * 1024 * 1024),
        name="attend_backward",
    )(place, projected, projected, projected, grad, mixed, log_total)


def local(
    block_input,
    first_gain,
    first_shift,
    query_key_value_weight,
    query_bias,
    value_bias,
    attention_output_weight,
    attention_output_bias,
    second_gain,
    second_shift,
    up_weight,
    up_bias,
    down_weight,
    down_bias,
    cotangent,
):
    shards = lax.axis_size("shard")
    index = lax.axis_index("shard")
    seqs, span, width = block_input.shape
    size = width // HEADS
    own = width // shards
    hidden = up_bias.shape[0]
    starts = [d * own // size for d in range(shards)]
    heads = max(-(-(d + 1) * own // size) - starts[d] for d in range(shards))
    window = heads * size
    pad = window - own
    start = index * own // size
    skew = index * own - start * size
    order = relative_order()
    inverse_order = jnp.asarray([order.index(o) for o in range(shards)], jnp.int32)
    place = inverse_order[jnp.arange(shards, dtype=jnp.int32) ^ index]

    own_input = block_input.reshape(seqs * span, width)
    inputs_all = gather_relative(own_input)
    vectors = gather_absolute(
        jnp.stack(
            [
                first_gain,
                first_shift,
                query_bias,
                value_bias,
                attention_output_bias,
                second_gain,
                second_shift,
                down_bias,
            ]
        )
    )
    vectors = vectors.transpose(1, 0, 2).reshape(8, width)
    gain_one, shift_one, bias_query, bias_value, bias_out, gain_two, shift_two, bias_down = (
        vectors[i] for i in range(8)
    )
    weight_in = exchange(
        jnp.stack(
            [
                jnp.concatenate(
                    [
                        query_key_value_weight[
                            :, part * width + s * size : part * width + s * size + window
                        ]
                        for part in range(3)
                    ],
                    axis=1,
                )
                for s in starts
            ]
        )
    ).reshape(width, 3 * window)
    weight_up = exchange(
        up_weight.reshape(own, shards, hidden).transpose(1, 0, 2)
    ).reshape(width, hidden)
    to_right = [(i, i + 1) for i in range(shards - 1)]
    to_left = [(i + 1, i) for i in range(shards - 1)]
    weight_out_window = lax.dynamic_slice_in_dim(
        jnp.concatenate(
            [
                lax.ppermute(attention_output_weight[own - pad :], "shard", to_right),
                attention_output_weight,
                lax.ppermute(attention_output_weight[:pad], "shard", to_left),
            ],
            axis=0,
        ),
        pad - skew,
        window,
        0,
    )
    branch_all = gather_relative(cotangent.reshape(seqs * span, width).astype(low))
    grad_out = cotangent.reshape(seqs * span, width)

    def own_rows(values):
        return lax.dynamic_slice_in_dim(values, skew, own, 0)

    rows = shards * seqs * span
    normed_all, _ = normalize(inputs_all.reshape(rows, width).astype(f32))
    hidden_one = (normed_all * gain_one + shift_one).astype(low)
    bias_window = jnp.concatenate(
        [
            lax.dynamic_slice_in_dim(bias_query, start * size, window, 0),
            jnp.zeros((window,), low),
            lax.dynamic_slice_in_dim(bias_value, start * size, window, 0),
        ]
    ).astype(f32)
    projected = (contract(weight_in, hidden_one, 0, 1) + bias_window[:, None]).astype(low)

    def per_sequence(values):
        lead = values.shape[:-1]
        split = values.reshape(lead + (shards, seqs, span))
        return [split[..., :, s, :].reshape(lead + (shards * span,)) for s in range(seqs)]

    def join_sequences(parts):
        if seqs == 1:
            return parts[0]
        lead = parts[0].shape[:-1]
        joined = jnp.stack([p.reshape(lead + (shards, span)) for p in parts], axis=-2)
        return joined.reshape(lead + (rows,))

    projected_parts = per_sequence(projected) if seqs > 1 else [projected]
    forward_parts = [attend_forward(place, p, heads, span) for p in projected_parts]
    attended = own_rows(join_sequences([p[1] for p in forward_parts]))
    mixed_sum = scatter_relative(
        contract(attended, attention_output_weight, 0, 0).reshape(shards, seqs * span, width)
    )
    layer_input = own_input.astype(f32)
    middle = layer_input + mixed_sum + bias_out

    normed_two, inverse_two = normalize(middle)
    hidden_two = gather_relative((normed_two * gain_two + shift_two).astype(low)).reshape(
        rows, width
    )
    branch = branch_all.reshape(rows, width)
    before = contract(hidden_two, weight_up, 1, 0) + up_bias
    activated, slope = gelu_parts(before)
    activated = activated.astype(low)
    grad_before = (contract(branch, down_weight, 1, 1) * slope).astype(low)
    grad_hidden_two = scatter_relative(
        contract(grad_before, weight_up, 1, 1).reshape(shards, seqs * span, width)
    )
    down_weight_grad = lax.psum(contract(activated, branch, 0, 0).astype(low), "rep")
    up_weight_grad = exchange(
        contract(hidden_two, grad_before, 0, 0).astype(low).reshape(shards, own, hidden)
    )
    up_weight_grad = lax.psum(up_weight_grad, "rep")
    block_output = (
        middle
        + scatter_relative(
            contract(activated, down_weight, 1, 0).reshape(shards, seqs * span, width)
        )
        + bias_down
    )
    grad_middle = grad_out + norm_back(grad_hidden_two, normed_two, inverse_two, gain_two)

    grad_mixed = gather_relative(grad_middle.astype(low)).reshape(rows, width)
    grad_attended = contract(weight_out_window, grad_mixed, 1, 1).astype(low)
    grad_parts = per_sequence(grad_attended) if seqs > 1 else [grad_attended]
    backward_parts = [
        attend_backward(place, p, g, f[0], f[2], heads, span)
        for p, g, f in zip(projected_parts, grad_parts, forward_parts)
    ]
    grad_query, grad_key, grad_value = (
        join_sequences([p[i] for p in backward_parts]) for i in range(3)
    )
    own_query, own_key, own_value = (own_rows(g) for g in (grad_query, grad_key, grad_value))
    own_projected = jnp.concatenate([own_query, own_key, own_value], axis=0)
    line = jnp.arange(window)
    mine = ((line >= skew) & (line < skew + own))[:, None]
    grad_projected = jnp.concatenate(
        [jnp.where(mine, g, jnp.zeros_like(g)) for g in (grad_query, grad_key, grad_value)], axis=0
    )
    input_weight_grad = exchange(
        contract(hidden_one, own_projected, 0, 1).astype(low).reshape(shards, own, 3 * own)
    )
    input_weight_grad = lax.psum(input_weight_grad, "rep")
    output_weight_grad = lax.psum(contract(attended, grad_mixed, 1, 0).astype(low), "rep")
    grad_hidden_one = scatter_relative(
        contract(grad_projected, weight_in, 0, 1).reshape(shards, seqs * span, width)
    )
    normed_one, inverse_one = normalize(layer_input)
    input_grad = grad_middle + norm_back(grad_hidden_one, normed_one, inverse_one, gain_one)

    def own_part(values):
        return lax.dynamic_slice_in_dim(values, index * own, own, 0)

    partial = lax.psum(
        jnp.stack(
            [
                jnp.sum(grad_hidden_one * normed_one, axis=0),
                jnp.sum(grad_hidden_one, axis=0),
                jnp.sum(grad_hidden_two * normed_two, axis=0),
                jnp.sum(grad_hidden_two, axis=0),
            ]
        ),
        ("rep", "shard"),
    )
    first_gain_grad, first_shift_grad, second_gain_grad, second_shift_grad = (
        own_part(partial[i]) for i in range(4)
    )
    complete = lax.psum(
        jnp.concatenate(
            [
                jnp.sum(own_query.astype(f32), axis=1),
                jnp.sum(own_value.astype(f32), axis=1),
                own_part(jnp.sum(grad_mixed.astype(f32), axis=0)),
                own_part(jnp.sum(branch.astype(f32), axis=0)),
                jnp.sum(grad_before.astype(f32), axis=0),
            ]
        ),
        "rep",
    )
    query_bias_grad, value_bias_grad, output_bias_grad, down_bias_grad = (
        complete[i * own : (i + 1) * own] for i in range(4)
    )
    up_bias_grad = complete[4 * own :]
    return (
        block_output.reshape(seqs, span, width),
        input_grad.reshape(seqs, span, width),
        first_gain_grad,
        first_shift_grad,
        input_weight_grad.reshape(shards, own, 3, own)
        .transpose(1, 2, 0, 3)
        .reshape(own, 3 * width)
        .astype(f32),
        query_bias_grad,
        value_bias_grad,
        output_weight_grad.astype(f32),
        output_bias_grad,
        second_gain_grad,
        second_shift_grad,
        up_weight_grad.transpose(1, 0, 2).reshape(own, shards * hidden).astype(f32),
        up_bias_grad,
        down_weight_grad.astype(f32),
        down_bias_grad,
    )


def solution(mesh):
    matrix, vector, tokens = P("shard", None), P("shard"), P("rep", "shard", None)
    return jax.shard_map(
        local,
        mesh=mesh,
        in_specs=(
            tokens,
            vector,
            vector,
            matrix,
            vector,
            vector,
            matrix,
            vector,
            vector,
            vector,
            matrix,
            vector,
            matrix,
            vector,
            tokens,
        ),
        out_specs=(
            tokens,
            tokens,
            vector,
            vector,
            matrix,
            vector,
            vector,
            matrix,
            vector,
            vector,
            vector,
            matrix,
            vector,
            matrix,
            vector,
        ),
        check_vma=False,
    )
```

```python
import functools

import jax
import jax.numpy as jnp
from jax import lax
from jax.experimental import pallas as pl
from jax.experimental.pallas import tpu as pltpu
from jax.sharding import PartitionSpec as P

HEADS = 17

epsilon = 1e-05
score_scale = 0.125
low = jnp.bfloat16
f32 = jnp.float32


def normalize(values):
    centre = jnp.mean(values, axis=-1, keepdims=True)
    centred = values - centre
    inverse = lax.rsqrt(jnp.mean(centred * centred, axis=-1, keepdims=True) + epsilon)
    return (centred * inverse, inverse)


def norm_back(grad, normed, inverse, gain):
    scaled = grad * gain
    first = jnp.mean(scaled, axis=-1, keepdims=True)
    second = jnp.mean(scaled * normed, axis=-1, keepdims=True)
    return inverse * (scaled - first - normed * second)


def gelu_parts(values):
    cumulative = 0.5 * (1.0 + lax.erf(values * 0.7071067811865476))
    density = jnp.exp(-0.5 * values * values) * 0.3989422804014327
    return values * cumulative, cumulative + values * density


def contract(left, right, left_dim, right_dim):
    return lax.dot_general(
        left, right, (((left_dim,), (right_dim,)), ((), ())), preferred_element_type=f32
    )


def swap(values, bit):
    size = lax.axis_size("shard")
    return lax.ppermute(values, "shard", [(i, i ^ bit) for i in range(size)])


def bits_far_first():
    bit = lax.axis_size("shard") // 2
    bits = []
    while bit:
        bits.append(bit)
        bit //= 2
    return bits


def relative_order():
    order = [0]
    for bit in bits_far_first():
        order = order + [o ^ bit for o in order]
    return order


def gather_relative(block):
    for bit in bits_far_first():
        block = jnp.concatenate([block, swap(block, bit)], axis=0)
    return block


def gather_absolute(block):
    index = lax.axis_index("shard")
    stack = block[None]
    for bit in bits_far_first():
        other = swap(stack, bit)
        upper = (index & bit) != 0
        pair = jnp.stack(
            [jnp.where(upper, other, stack), jnp.where(upper, stack, other)], axis=1
        )
        stack = pair.reshape((2 * stack.shape[0],) + block.shape)
    return stack


def scatter_relative(parts):
    for bit in reversed(bits_far_first()):
        half = parts.shape[0] // 2
        other = swap(parts[half:].astype(low), bit)
        parts = parts[:half] + other.astype(f32)
    return parts


def swap_rep(values, bit):
    size = lax.axis_size("rep")
    return lax.ppermute(values, "rep", [(i, i ^ bit) for i in range(size)])


def rep_bits(turned):
    bits, bit = [], 1
    while bit < lax.axis_size("rep"):
        bits.append(bit)
        bit *= 2
    return bits[1:] + bits[:1] if turned else bits


def rep_sum(values, turned=False, halvings=None):
    bits = rep_bits(turned)
    halvings = len(bits) if halvings is None else halvings
    rows, cols = values.shape
    index = lax.axis_index("rep")
    total = values.reshape((2,) * halvings + (rows >> halvings, cols))
    for bit in bits[:halvings]:
        mine = (index // bit) % 2
        send = lax.dynamic_index_in_dim(total, 1 - mine, 0, keepdims=False)
        keep = lax.dynamic_index_in_dim(total, mine, 0, keepdims=False)
        total = (keep.astype(f32) + swap_rep(send, bit).astype(f32)).astype(low)
    for bit in bits[halvings:]:
        total = (total.astype(f32) + swap_rep(total, bit).astype(f32)).astype(low)
    total = lax.optimization_barrier(total)
    for bit in reversed(bits[:halvings]):
        upper = (index // bit) % 2 != 0
        other = swap_rep(total, bit)
        total = jnp.stack([jnp.where(upper, other, total), jnp.where(upper, total, other)])
    return total.reshape(rows, cols)


def exchange(blocks):
    size = lax.axis_size("shard")
    index = lax.axis_index("shard")
    result = jnp.zeros_like(blocks)
    for offset in range(size):
        peer = index ^ offset
        piece = lax.dynamic_index_in_dim(blocks, peer, 0, keepdims=True)
        if offset:
            piece = swap(piece, offset)
        result = lax.dynamic_update_slice_in_dim(result, piece, peer, 0)
    return result


def visible_part(scores, top, block, fill):
    rows = lax.broadcasted_iota(jnp.int32, (block, block), 0)
    cols = lax.broadcasted_iota(jnp.int32, (block, block), 1)
    last = jnp.where(rows <= cols, scores[top:], fill)
    if top == 0:
        return last
    return jnp.concatenate([scores[:top], last], axis=0)


def turn(values):
    return values.astype(f32).T


def forward_kernel(blocks, block, place, q_ref, k_ref, v_ref, o_ref, low_ref, log_ref, k_rows, v_cols):
    for i in range(blocks):
        here = pl.ds(pl.multiple_of(place[i] * block, block), block)
        there = pl.ds(i * block, block)
        k_rows[there, :] = turn(k_ref[:, here]).astype(low)
        v_cols[:, there] = v_ref[:, here]
    for i in range(blocks):
        here = pl.ds(pl.multiple_of(place[i] * block, block), block)
        top = i * block
        count = top + block
        q_cols = q_ref[:, here] * jnp.asarray(score_scale, low)
        scores = contract(k_rows[:count, :], q_cols, 1, 0)
        scores = visible_part(scores, top, block, -jnp.inf)
        peak = jnp.max(scores, axis=0, keepdims=True)
        weights = jnp.exp(scores - peak)
        total = jnp.sum(weights, axis=0, keepdims=True)
        mixed = contract(v_cols[:, :count], weights.astype(low), 1, 0) / total
        o_ref[:, here] = mixed
        low_ref[:, here] = mixed.astype(low)
        log_ref[0, :, here] = peak + jnp.log(total)


def backward_kernel(
    blocks,
    block,
    place,
    q_ref,
    k_ref,
    v_ref,
    g_ref,
    o_ref,
    log_ref,
    dq_ref,
    dk_ref,
    dv_ref,
    k_rows,
    v_rows,
    k_cols,
    dk_rows,
    dv_rows,
):
    for i in range(blocks):
        here = pl.ds(pl.multiple_of(place[i] * block, block), block)
        there = pl.ds(i * block, block)
        k_rows[there, :] = turn(k_ref[:, here]).astype(low)
        v_rows[there, :] = turn(v_ref[:, here]).astype(low)
        k_cols[:, there] = k_ref[:, here]
    for i in reversed(range(blocks)):
        here = pl.ds(pl.multiple_of(place[i] * block, block), block)
        top = i * block
        count = top + block
        q_cols = q_ref[:, here] * jnp.asarray(score_scale, low)
        g_cols = g_ref[:, here]
        q_rows = turn(q_cols).astype(low)
        g_rows = turn(g_cols).astype(low)
        correction = jnp.sum(g_cols.astype(f32) * o_ref[:, here], axis=0, keepdims=True)
        scores = contract(k_rows[:count, :], q_cols, 1, 0)
        probs = jnp.exp(scores - log_ref[0, :, here])
        probs = visible_part(probs, top, block, 0.0)
        grad_probs = contract(v_rows[:count, :], g_cols, 1, 0)
        grad_scores = (probs * (grad_probs - correction)).astype(low)
        dv_part = contract(probs.astype(low), g_rows, 1, 0)
        dk_part = contract(grad_scores, q_rows, 1, 0)
        if i == blocks - 1:
            dv_rows[:count, :] = dv_part
            dk_rows[:count, :] = dk_part
        else:
            dv_rows[:count, :] += dv_part
            dk_rows[:count, :] += dk_part
        dq = contract(k_cols[:, :count], grad_scores, 1, 0) * score_scale
        dq_ref[:, here] = dq.astype(low)
    for i in range(blocks):
        here = pl.ds(pl.multiple_of(place[i] * block, block), block)
        there = pl.ds(i * block, block)
        dk_ref[:, here] = dk_rows[there, :].T.astype(low)
        dv_ref[:, here] = dv_rows[there, :].T.astype(low)


def head_spec(size, length, first):
    return pl.BlockSpec((size, length), lambda h, place: (first + h, 0))


def attend_forward(place, projected, heads, block):
    size = projected.shape[0] // (3 * heads)
    length = projected.shape[1]
    blocks = length // block
    row = pl.BlockSpec((1, 1, length), lambda h, place: (h, 0, 0))
    return pl.pallas_call(
        functools.partial(forward_kernel, blocks, block),
        grid_spec=pltpu.PrefetchScalarGridSpec(
            num_scalar_prefetch=1,
            grid=(heads,),
            in_specs=[
                head_spec(size, length, 0),
                head_spec(size, length, heads),
                head_spec(size, length, 2 * heads),
            ],
            out_specs=[head_spec(size, length, 0), head_spec(size, length, 0), row],
            scratch_shapes=[
                pltpu.VMEM((length, size), low),
                pltpu.VMEM((size, length), low),
            ],
        ),
        out_shape=[
            jax.ShapeDtypeStruct((heads * size, length), f32),
            jax.ShapeDtypeStruct((heads * size, length), low),
            jax.ShapeDtypeStruct((heads, 1, length), f32),
        ],
        cost_estimate=pl.CostEstimate(
            flops=4 * heads * length * length * size,
            bytes_accessed=heads * length * size * 12,
            transcendentals=heads * length * length,
        ),
        compiler_params=pltpu.CompilerParams(vmem_limit_bytes=32 * 1024 * 1024),
        name="attend_forward",
    )(place, projected, projected, projected)


def attend_backward(place, projected, grad, mixed, log_total, heads, block):
    size = projected.shape[0] // (3 * heads)
    length = projected.shape[1]
    blocks = length // block
    row = pl.BlockSpec((1, 1, length), lambda h, place: (h, 0, 0))
    out = jax.ShapeDtypeStruct((heads * size, length), low)
    return pl.pallas_call(
        functools.partial(backward_kernel, blocks, block),
        grid_spec=pltpu.PrefetchScalarGridSpec(
            num_scalar_prefetch=1,
            grid=(heads,),
            in_specs=[
                head_spec(size, length, 0),
                head_spec(size, length, heads),
                head_spec(size, length, 2 * heads),
                head_spec(size, length, 0),
                head_spec(size, length, 0),
                row,
            ],
            out_specs=[head_spec(size, length, 0)] * 3,
            scratch_shapes=[
                pltpu.VMEM((length, size), low),
                pltpu.VMEM((length, size), low),
                pltpu.VMEM((size, length), low),
                pltpu.VMEM((length, size), f32),
                pltpu.VMEM((length, size), f32),
            ],
        ),
        out_shape=[out, out, out],
        cost_estimate=pl.CostEstimate(
            flops=10 * heads * length * length * size,
            bytes_accessed=heads * length * size * 20,
            transcendentals=heads * length * length,
        ),
        compiler_params=pltpu.CompilerParams(vmem_limit_bytes=32 * 1024 * 1024),
        name="attend_backward",
    )(place, projected, projected, projected, grad, mixed, log_total)


def local(
    block_input,
    first_gain,
    first_shift,
    query_key_value_weight,
    query_bias,
    value_bias,
    attention_output_weight,
    attention_output_bias,
    second_gain,
    second_shift,
    up_weight,
    up_bias,
    down_weight,
    down_bias,
    cotangent,
):
    shards = lax.axis_size("shard")
    index = lax.axis_index("shard")
    seqs, span, width = block_input.shape
    size = width // HEADS
    own = width // shards
    hidden = up_bias.shape[0]
    starts = [d * own // size for d in range(shards)]
    heads = max(-(-(d + 1) * own // size) - starts[d] for d in range(shards))
    window = heads * size
    pad = window - own
    start = index * own // size
    skew = index * own - start * size
    order = relative_order()
    inverse_order = jnp.asarray([order.index(o) for o in range(shards)], jnp.int32)
    place = inverse_order[jnp.arange(shards, dtype=jnp.int32) ^ index]

    own_input = block_input.reshape(seqs * span, width)
    inputs_all = gather_relative(own_input)
    vectors = gather_absolute(
        jnp.stack(
            [
                first_gain,
                first_shift,
                query_bias,
                value_bias,
                attention_output_bias,
                second_gain,
                second_shift,
                down_bias,
            ]
        )
    )
    vectors = vectors.transpose(1, 0, 2).reshape(8, width)
    gain_one, shift_one, bias_query, bias_value, bias_out, gain_two, shift_two, bias_down = (
        vectors[i] for i in range(8)
    )
    weight_in = exchange(
        jnp.stack(
            [
                jnp.concatenate(
                    [
                        query_key_value_weight[
                            :, part * width + s * size : part * width + s * size + window
                        ]
                        for part in range(3)
                    ],
                    axis=1,
                )
                for s in starts
            ]
        )
    ).reshape(width, 3 * window)
    weight_up = exchange(
        jnp.stack([up_weight[:, s * hidden : (s + 1) * hidden] for s in range(shards)])
    ).reshape(width, hidden)
    to_right = [(i, i + 1) for i in range(shards - 1)]
    to_left = [(i + 1, i) for i in range(shards - 1)]
    weight_out_window = lax.dynamic_slice_in_dim(
        jnp.concatenate(
            [
                lax.ppermute(attention_output_weight[own - pad :], "shard", to_right),
                attention_output_weight,
                lax.ppermute(attention_output_weight[:pad], "shard", to_left),
            ],
            axis=0,
        ),
        pad - skew,
        window,
        0,
    )
    branch = gather_relative(cotangent.reshape(seqs * span, width).astype(low))
    grad_out = cotangent.reshape(seqs * span, width)

    def own_rows(values):
        return lax.dynamic_slice_in_dim(values, skew, own, 0)

    rows = shards * seqs * span
    normed_all, _ = normalize(inputs_all.astype(f32))
    hidden_one = (normed_all * gain_one + shift_one).astype(low)
    bias_window = jnp.concatenate(
        [
            lax.dynamic_slice_in_dim(bias_query, start * size, window, 0),
            jnp.zeros((window,), low),
            lax.dynamic_slice_in_dim(bias_value, start * size, window, 0),
        ]
    ).astype(f32)
    projected = (contract(weight_in, hidden_one, 0, 1) + bias_window[:, None]).astype(low)

    def per_sequence(values):
        lead = values.shape[:-1]
        split = values.reshape(lead + (shards, seqs, span))
        return [split[..., :, s, :].reshape(lead + (shards * span,)) for s in range(seqs)]

    def join_sequences(parts):
        if seqs == 1:
            return parts[0]
        lead = parts[0].shape[:-1]
        joined = jnp.stack([p.reshape(lead + (shards, span)) for p in parts], axis=-2)
        return joined.reshape(lead + (rows,))

    projected_parts = per_sequence(projected) if seqs > 1 else [projected]
    forward_parts = [attend_forward(place, p, heads, span) for p in projected_parts]
    attended = own_rows(join_sequences([p[1] for p in forward_parts]))
    mixed_sum = scatter_relative(
        contract(attended, attention_output_weight, 0, 0)
    )
    layer_input = own_input.astype(f32)
    middle = layer_input + mixed_sum + bias_out

    normed_two, inverse_two = normalize(middle)
    hidden_two = gather_relative((normed_two * gain_two + shift_two).astype(low))
    before = contract(hidden_two, weight_up, 1, 0) + up_bias
    activated, slope = gelu_parts(before)
    activated = activated.astype(low)
    grad_before = (contract(branch, down_weight, 1, 1) * slope).astype(low)
    grad_hidden_two = scatter_relative(
        contract(grad_before, weight_up, 1, 1)
    )
    down_weight_grad = rep_sum(contract(activated, branch, 0, 0).astype(low))
    up_weight_grad = exchange(
        contract(hidden_two, grad_before, 0, 0).astype(low).reshape(shards, own, hidden)
    )
    up_weight_grad = rep_sum(up_weight_grad.reshape(width, hidden), turned=True)
    block_output = (
        middle
        + scatter_relative(
            contract(activated, down_weight, 1, 0)
        )
        + bias_down
    )
    grad_middle = grad_out + norm_back(grad_hidden_two, normed_two, inverse_two, gain_two)

    grad_mixed = gather_relative(grad_middle.astype(low))
    grad_attended = contract(weight_out_window, grad_mixed, 1, 1).astype(low)
    grad_parts = per_sequence(grad_attended) if seqs > 1 else [grad_attended]
    backward_parts = [
        attend_backward(place, p, g, f[0], f[2], heads, span)
        for p, g, f in zip(projected_parts, grad_parts, forward_parts)
    ]
    grad_query, grad_key, grad_value = (
        join_sequences([p[i] for p in backward_parts]) for i in range(3)
    )
    own_query, own_key, own_value = (own_rows(g) for g in (grad_query, grad_key, grad_value))
    own_projected = jnp.concatenate([own_query, own_key, own_value], axis=0)
    line = jnp.arange(window)
    mine = ((line >= skew) & (line < skew + own))[:, None]
    grad_projected = jnp.concatenate(
        [jnp.where(mine, g, jnp.zeros_like(g)) for g in (grad_query, grad_key, grad_value)], axis=0
    )
    input_weight_grad = exchange(
        contract(hidden_one, own_projected, 0, 1).astype(low).reshape(shards, own, 3 * own)
    )
    input_weight_grad = input_weight_grad.reshape(width, 3 * own)
    cut = (3 * own // 2) // 128 * 128
    input_weight_grad = jnp.concatenate(
        [
            rep_sum(input_weight_grad[:, :cut]),
            rep_sum(input_weight_grad[:, cut:], turned=True),
        ],
        axis=1,
    )
    output_weight_grad = rep_sum(
        contract(attended, grad_mixed, 1, 0).astype(low), halvings=1
    )
    grad_hidden_one = scatter_relative(
        contract(grad_projected, weight_in, 0, 1)
    )
    normed_one, inverse_one = normalize(layer_input)
    input_grad = grad_middle + norm_back(grad_hidden_one, normed_one, inverse_one, gain_one)

    def own_part(values):
        return lax.dynamic_slice_in_dim(values, index * own, own, 0)

    partial = jnp.stack(
        [
            jnp.sum(grad_hidden_one * normed_one, axis=0),
            jnp.sum(grad_hidden_one, axis=0),
            jnp.sum(grad_hidden_two * normed_two, axis=0),
            jnp.sum(grad_hidden_two, axis=0),
        ]
    )
    for bit in bits_far_first():
        partial = partial + swap(partial, bit)
    complete = jnp.concatenate(
        [own_part(partial[i]) for i in range(4)]
        + [
            jnp.sum(own_query.astype(f32), axis=1),
            jnp.sum(own_value.astype(f32), axis=1),
            own_part(jnp.sum(grad_mixed.astype(f32), axis=0)),
            own_part(jnp.sum(branch.astype(f32), axis=0)),
            jnp.sum(grad_before.astype(f32), axis=0),
        ]
    )
    for bit in rep_bits(False):
        complete = complete + swap_rep(complete, bit)
    (
        first_gain_grad,
        first_shift_grad,
        second_gain_grad,
        second_shift_grad,
        query_bias_grad,
        value_bias_grad,
        output_bias_grad,
        down_bias_grad,
    ) = (complete[i * own : (i + 1) * own] for i in range(8))
    up_bias_grad = complete[8 * own :]
    return (
        block_output.reshape(seqs, span, width),
        input_grad.reshape(seqs, span, width),
        first_gain_grad,
        first_shift_grad,
        jnp.concatenate(
            [
                input_weight_grad[s * own : (s + 1) * own, part * own : (part + 1) * own]
                for part in range(3)
                for s in range(shards)
            ],
            axis=1,
        ).astype(f32),
        query_bias_grad,
        value_bias_grad,
        output_weight_grad.astype(f32),
        output_bias_grad,
        second_gain_grad,
        second_shift_grad,
        jnp.concatenate(
            [up_weight_grad[s * own : (s + 1) * own] for s in range(shards)], axis=1
        ).astype(f32),
        up_bias_grad,
        down_weight_grad.astype(f32),
        down_bias_grad,
    )


def solution(mesh):
    matrix, vector, tokens = P("shard", None), P("shard"), P("rep", "shard", None)
    return jax.shard_map(
        local,
        mesh=mesh,
        in_specs=(
            tokens,
            vector,
            vector,
            matrix,
            vector,
            vector,
            matrix,
            vector,
            vector,
            vector,
            matrix,
            vector,
            matrix,
            vector,
            tokens,
        ),
        out_specs=(
            tokens,
            tokens,
            vector,
            vector,
            matrix,
            vector,
            vector,
            matrix,
            vector,
            vector,
            vector,
            matrix,
            vector,
            matrix,
            vector,
        ),
        check_vma=False,
    )
```

```python
import functools

import jax
import jax.numpy as jnp
from jax import lax
from jax.experimental import pallas as pl
from jax.experimental.pallas import tpu as pltpu
from jax.sharding import PartitionSpec as P

HEADS = 17

epsilon = 1e-05
score_scale = 0.125
low = jnp.bfloat16
f32 = jnp.float32


def normalize(values):
    centre = jnp.mean(values, axis=-1, keepdims=True)
    centred = values - centre
    inverse = lax.rsqrt(jnp.mean(centred * centred, axis=-1, keepdims=True) + epsilon)
    return (centred * inverse, inverse)


def norm_back(grad, normed, inverse, gain):
    scaled = grad * gain
    first = jnp.mean(scaled, axis=-1, keepdims=True)
    second = jnp.mean(scaled * normed, axis=-1, keepdims=True)
    return inverse * (scaled - first - normed * second)


def gelu_parts(values):
    cumulative = 0.5 * (1.0 + lax.erf(values * 0.7071067811865476))
    density = jnp.exp(-0.5 * values * values) * 0.3989422804014327
    return values * cumulative, cumulative + values * density


def contract(left, right, left_dim, right_dim):
    return lax.dot_general(
        left, right, (((left_dim,), (right_dim,)), ((), ())), preferred_element_type=f32
    )


def swap(values, bit):
    size = lax.axis_size("shard")
    return lax.ppermute(values, "shard", [(i, i ^ bit) for i in range(size)])


def bits_far_first():
    bit = lax.axis_size("shard") // 2
    bits = []
    while bit:
        bits.append(bit)
        bit //= 2
    return bits


def relative_order():
    order = [0]
    for bit in bits_far_first():
        order = order + [o ^ bit for o in order]
    return order


def gather_relative(block):
    for bit in bits_far_first():
        block = jnp.concatenate([block, swap(block, bit)], axis=0)
    return block


def gather_absolute(block):
    index = lax.axis_index("shard")
    stack = block[None]
    for bit in bits_far_first():
        other = swap(stack, bit)
        upper = (index & bit) != 0
        pair = jnp.stack(
            [jnp.where(upper, other, stack), jnp.where(upper, stack, other)], axis=1
        )
        stack = pair.reshape((2 * stack.shape[0],) + block.shape)
    return stack


def scatter_relative(parts):
    for bit in reversed(bits_far_first()):
        half = parts.shape[0] // 2
        other = swap(parts[half:].astype(low), bit)
        parts = parts[:half] + other.astype(f32)
    return parts


def swap_rep(values, bit):
    size = lax.axis_size("rep")
    return lax.ppermute(values, "rep", [(i, i ^ bit) for i in range(size)])


def rep_bits(turned):
    bits, bit = [], 1
    while bit < lax.axis_size("rep"):
        bits.append(bit)
        bit *= 2
    return bits[1:] + bits[:1] if turned else bits


def after(values, gate):
    return lax.optimization_barrier((values, gate))[0]


def half_window(rows):
    return min(rows, (rows + 15) // 16 * 8)


def halve(values, bit, gate=None):
    rows = values.shape[1]
    window = half_window(rows)
    mine = (lax.axis_index("rep") // bit) % 2
    far = rows - window
    send = lax.dynamic_slice_in_dim(values, (1 - mine) * far, window, 1)
    other = swap_rep(send, bit)
    if gate is not None:
        other = after(other, gate)
    keep = lax.dynamic_slice_in_dim(values, mine * far, window, 1)
    return (keep.astype(f32) + other.astype(f32)).astype(low)


def double(values, bit, rows, gate=None):
    window = values.shape[1]
    other = swap_rep(values, bit)
    if gate is not None:
        other = after(other, gate)
    upper = (lax.axis_index("rep") // bit) % 2 != 0
    first = jnp.where(upper, other, values)
    second = jnp.where(upper, values, other)
    return jnp.concatenate([first, second[:, 2 * window - rows :]], axis=1)


def rep_scatter(values, bits, gates=()):
    sizes = []
    for step, bit in enumerate(bits):
        sizes.append(values.shape[1])
        values = halve(values, bit, gates[step] if step < len(gates) else None)
    return lax.optimization_barrier(values), sizes


def rep_gather(values, bits, sizes):
    for bit, rows in zip(reversed(bits), reversed(sizes)):
        values = double(values, bit, rows)
    return values


def exchange(blocks):
    size = lax.axis_size("shard")
    index = lax.axis_index("shard")
    result = jnp.zeros_like(blocks)
    for offset in range(size):
        peer = index ^ offset
        piece = lax.dynamic_index_in_dim(blocks, peer, 0, keepdims=True)
        if offset:
            piece = swap(piece, offset)
        result = lax.dynamic_update_slice_in_dim(result, piece, peer, 0)
    return result


def send_halves(blocks):
    index = lax.axis_index("shard")
    size = lax.axis_size("shard")
    half = blocks.shape[1] // 2
    part = (lax.axis_index("rep") % 2) * half
    pieces = []
    for offset in range(size):
        piece = lax.dynamic_index_in_dim(blocks, index ^ offset, 0, keepdims=True)
        if offset >= 2:
            piece = lax.dynamic_slice_in_dim(piece, part, half, 1)
        if offset:
            piece = swap(piece, offset)
        pieces.append(piece)
    return pieces


def join_halves(pieces):
    index = lax.axis_index("shard")
    upper = lax.axis_index("rep") % 2 != 0
    full = pieces[0].shape[1]
    count = len(pieces)
    if count > 2:
        mine = jnp.concatenate(pieces[2:], axis=0)
        other = swap_rep(mine, 1)
        halves = jnp.concatenate(
            [jnp.where(upper, other, mine), jnp.where(upper, mine, other)], axis=1
        )
        pieces = pieces[:2] + [halves[i : i + 1] for i in range(count - 2)]
    result = jnp.zeros((count,) + pieces[0].shape[1:], pieces[0].dtype)
    for offset, piece in enumerate(pieces):
        result = lax.dynamic_update_slice_in_dim(result, piece, index ^ offset, 0)
    return result


def visible_part(scores, top, block, fill):
    rows = lax.broadcasted_iota(jnp.int32, (block, block), 0)
    cols = lax.broadcasted_iota(jnp.int32, (block, block), 1)
    last = jnp.where(rows <= cols, scores[top:], fill)
    if top == 0:
        return last
    return jnp.concatenate([scores[:top], last], axis=0)


def turn(values):
    return values.astype(f32).T


def forward_kernel(blocks, block, place, q_ref, k_ref, v_ref, o_ref, low_ref, log_ref, k_rows, v_cols):
    for i in range(blocks):
        here = pl.ds(pl.multiple_of(place[i] * block, block), block)
        there = pl.ds(i * block, block)
        k_rows[there, :] = turn(k_ref[:, here]).astype(low)
        v_cols[:, there] = v_ref[:, here]
    for i in range(blocks):
        here = pl.ds(pl.multiple_of(place[i] * block, block), block)
        top = i * block
        count = top + block
        q_cols = q_ref[:, here] * jnp.asarray(score_scale, low)
        scores = contract(k_rows[:count, :], q_cols, 1, 0)
        scores = visible_part(scores, top, block, -jnp.inf)
        peak = jnp.max(scores, axis=0, keepdims=True)
        weights = jnp.exp(scores - peak)
        total = jnp.sum(weights, axis=0, keepdims=True)
        mixed = contract(v_cols[:, :count], weights.astype(low), 1, 0) / total
        o_ref[:, here] = mixed
        low_ref[:, here] = mixed.astype(low)
        log_ref[0, :, here] = peak + jnp.log(total)


def backward_kernel(
    blocks,
    block,
    place,
    q_ref,
    k_ref,
    v_ref,
    g_ref,
    o_ref,
    log_ref,
    dq_ref,
    dk_ref,
    dv_ref,
    k_rows,
    v_rows,
    k_cols,
    dk_rows,
    dv_rows,
):
    for i in range(blocks):
        here = pl.ds(pl.multiple_of(place[i] * block, block), block)
        there = pl.ds(i * block, block)
        k_rows[there, :] = turn(k_ref[:, here]).astype(low)
        v_rows[there, :] = turn(v_ref[:, here]).astype(low)
        k_cols[:, there] = k_ref[:, here]
    for i in reversed(range(blocks)):
        here = pl.ds(pl.multiple_of(place[i] * block, block), block)
        top = i * block
        count = top + block
        q_cols = q_ref[:, here] * jnp.asarray(score_scale, low)
        g_cols = g_ref[:, here]
        q_rows = turn(q_cols).astype(low)
        g_rows = turn(g_cols).astype(low)
        correction = jnp.sum(g_cols.astype(f32) * o_ref[:, here], axis=0, keepdims=True)
        scores = contract(k_rows[:count, :], q_cols, 1, 0)
        probs = jnp.exp(scores - log_ref[0, :, here])
        probs = visible_part(probs, top, block, 0.0)
        grad_probs = contract(v_rows[:count, :], g_cols, 1, 0)
        grad_scores = (probs * (grad_probs - correction)).astype(low)
        dv_part = contract(probs.astype(low), g_rows, 1, 0)
        dk_part = contract(grad_scores, q_rows, 1, 0)
        if i == blocks - 1:
            dv_rows[:count, :] = dv_part
            dk_rows[:count, :] = dk_part
        else:
            dv_rows[:count, :] += dv_part
            dk_rows[:count, :] += dk_part
        dq = contract(k_cols[:, :count], grad_scores, 1, 0) * score_scale
        dq_ref[:, here] = dq.astype(low)
    for i in range(blocks):
        here = pl.ds(pl.multiple_of(place[i] * block, block), block)
        there = pl.ds(i * block, block)
        dk_ref[:, here] = dk_rows[there, :].T.astype(low)
        dv_ref[:, here] = dv_rows[there, :].T.astype(low)


def head_spec(size, length, first):
    return pl.BlockSpec((size, length), lambda h, place: (first + h, 0))


def attend_forward(place, projected, heads, block):
    size = projected.shape[0] // (3 * heads)
    length = projected.shape[1]
    blocks = length // block
    row = pl.BlockSpec((1, 1, length), lambda h, place: (h, 0, 0))
    return pl.pallas_call(
        functools.partial(forward_kernel, blocks, block),
        grid_spec=pltpu.PrefetchScalarGridSpec(
            num_scalar_prefetch=1,
            grid=(heads,),
            in_specs=[
                head_spec(size, length, 0),
                head_spec(size, length, heads),
                head_spec(size, length, 2 * heads),
            ],
            out_specs=[head_spec(size, length, 0), head_spec(size, length, 0), row],
            scratch_shapes=[
                pltpu.VMEM((length, size), low),
                pltpu.VMEM((size, length), low),
            ],
        ),
        out_shape=[
            jax.ShapeDtypeStruct((heads * size, length), f32),
            jax.ShapeDtypeStruct((heads * size, length), low),
            jax.ShapeDtypeStruct((heads, 1, length), f32),
        ],
        cost_estimate=pl.CostEstimate(
            flops=4 * heads * length * length * size,
            bytes_accessed=heads * length * size * 12,
            transcendentals=heads * length * length,
        ),
        compiler_params=pltpu.CompilerParams(vmem_limit_bytes=32 * 1024 * 1024),
        name="attend_forward",
    )(place, projected, projected, projected)


def attend_backward(place, projected, grad, mixed, log_total, heads, block):
    size = projected.shape[0] // (3 * heads)
    length = projected.shape[1]
    blocks = length // block
    row = pl.BlockSpec((1, 1, length), lambda h, place: (h, 0, 0))
    out = jax.ShapeDtypeStruct((heads * size, length), low)
    return pl.pallas_call(
        functools.partial(backward_kernel, blocks, block),
        grid_spec=pltpu.PrefetchScalarGridSpec(
            num_scalar_prefetch=1,
            grid=(heads,),
            in_specs=[
                head_spec(size, length, 0),
                head_spec(size, length, heads),
                head_spec(size, length, 2 * heads),
                head_spec(size, length, 0),
                head_spec(size, length, 0),
                row,
            ],
            out_specs=[head_spec(size, length, 0)] * 3,
            scratch_shapes=[
                pltpu.VMEM((length, size), low),
                pltpu.VMEM((length, size), low),
                pltpu.VMEM((size, length), low),
                pltpu.VMEM((length, size), f32),
                pltpu.VMEM((length, size), f32),
            ],
        ),
        out_shape=[out, out, out],
        cost_estimate=pl.CostEstimate(
            flops=10 * heads * length * length * size,
            bytes_accessed=heads * length * size * 20,
            transcendentals=heads * length * length,
        ),
        compiler_params=pltpu.CompilerParams(vmem_limit_bytes=32 * 1024 * 1024),
        name="attend_backward",
    )(place, projected, projected, projected, grad, mixed, log_total)


def local(
    block_input,
    first_gain,
    first_shift,
    query_key_value_weight,
    query_bias,
    value_bias,
    attention_output_weight,
    attention_output_bias,
    second_gain,
    second_shift,
    up_weight,
    up_bias,
    down_weight,
    down_bias,
    cotangent,
):
    shards = lax.axis_size("shard")
    index = lax.axis_index("shard")
    seqs, span, width = block_input.shape
    size = width // HEADS
    own = width // shards
    hidden = up_bias.shape[0]
    starts = [d * own // size for d in range(shards)]
    heads = max(-(-(d + 1) * own // size) - starts[d] for d in range(shards))
    window = heads * size
    pad = window - own
    start = index * own // size
    skew = index * own - start * size
    order = relative_order()
    inverse_order = jnp.asarray([order.index(o) for o in range(shards)], jnp.int32)
    place = inverse_order[jnp.arange(shards, dtype=jnp.int32) ^ index]

    own_input = block_input.reshape(seqs * span, width)
    inputs_all = gather_relative(own_input)
    vectors = gather_absolute(
        jnp.stack(
            [
                first_gain,
                first_shift,
                query_bias,
                value_bias,
                attention_output_bias,
                second_gain,
                second_shift,
                down_bias,
            ]
        )
    )
    vectors = vectors.transpose(1, 0, 2).reshape(8, width)
    gain_one, shift_one, bias_query, bias_value, bias_out, gain_two, shift_two, bias_down = (
        vectors[i] for i in range(8)
    )
    weight_in = exchange(
        jnp.stack(
            [
                jnp.concatenate(
                    [
                        query_key_value_weight[
                            :, part * width + s * size : part * width + s * size + window
                        ]
                        for part in range(3)
                    ],
                    axis=1,
                )
                for s in starts
            ]
        )
    ).reshape(width, 3 * window)
    up_blocks = jnp.stack([up_weight[:, s * hidden : (s + 1) * hidden] for s in range(shards)])
    up_pieces = send_halves(up_blocks)
    to_right = [(i, i + 1) for i in range(shards - 1)]
    to_left = [(i + 1, i) for i in range(shards - 1)]
    weight_out_window = lax.dynamic_slice_in_dim(
        jnp.concatenate(
            [
                lax.ppermute(attention_output_weight[own - pad :], "shard", to_right),
                attention_output_weight,
                lax.ppermute(attention_output_weight[:pad], "shard", to_left),
            ],
            axis=0,
        ),
        pad - skew,
        window,
        0,
    )
    branch = gather_relative(cotangent.reshape(seqs * span, width).astype(low))
    grad_out = cotangent.reshape(seqs * span, width)

    def own_rows(values):
        return lax.dynamic_slice_in_dim(values, skew, own, 0)

    rows = shards * seqs * span
    normed_all, _ = normalize(inputs_all.astype(f32))
    hidden_one = (normed_all * gain_one + shift_one).astype(low)
    bias_window = jnp.concatenate(
        [
            lax.dynamic_slice_in_dim(bias_query, start * size, window, 0),
            jnp.zeros((window,), low),
            lax.dynamic_slice_in_dim(bias_value, start * size, window, 0),
        ]
    ).astype(f32)
    projected = (contract(weight_in, hidden_one, 0, 1) + bias_window[:, None]).astype(low)

    def per_sequence(values):
        lead = values.shape[:-1]
        split = values.reshape(lead + (shards, seqs, span))
        return [split[..., :, s, :].reshape(lead + (shards * span,)) for s in range(seqs)]

    def join_sequences(parts):
        if seqs == 1:
            return parts[0]
        lead = parts[0].shape[:-1]
        joined = jnp.stack([p.reshape(lead + (shards, span)) for p in parts], axis=-2)
        return joined.reshape(lead + (rows,))

    projected_parts = per_sequence(projected) if seqs > 1 else [projected]
    forward_parts = [attend_forward(place, p, heads, span) for p in projected_parts]
    attended = join_sequences([p[1] for p in forward_parts])
    attended, up_pieces = lax.optimization_barrier((attended, up_pieces))
    attended = own_rows(attended)
    weight_up = join_halves(up_pieces).reshape(width, hidden)
    mixed_sum = scatter_relative(
        contract(attended, attention_output_weight, 0, 0)
    )
    layer_input = own_input.astype(f32)
    middle = layer_input + mixed_sum + bias_out

    normed_two, inverse_two = normalize(middle)
    hidden_two = gather_relative((normed_two * gain_two + shift_two).astype(low))
    before = contract(hidden_two, weight_up, 1, 0) + up_bias
    activated, slope = gelu_parts(before)
    activated = activated.astype(low)
    grad_before = (contract(branch, down_weight, 1, 1) * slope).astype(low)
    hidden_two_sum = contract(grad_before, weight_up, 1, 1)
    hidden_two_sum, late_before, late_active = lax.optimization_barrier(
        (hidden_two_sum, grad_before, activated)
    )
    grad_hidden_two = scatter_relative(hidden_two_sum)
    down_weight_grad = contract(late_active, branch, 0, 0).astype(low)[None]
    up_weight_grad = contract(hidden_two, late_before, 0, 0).astype(low)
    up_weight_grad = up_weight_grad.reshape(shards, own, hidden)
    down_sum = contract(late_active, down_weight, 1, 0)
    grad_middle = grad_out + norm_back(grad_hidden_two, normed_two, inverse_two, gain_two)

    grad_mixed = gather_relative(grad_middle.astype(low))
    grad_attended = contract(weight_out_window, grad_mixed, 1, 1).astype(low)
    grad_parts = per_sequence(grad_attended) if seqs > 1 else [grad_attended]
    block_output = middle + scatter_relative(after(down_sum, grad_mixed)) + bias_down
    backward_parts = [
        attend_backward(place, p, g, f[0], f[2], heads, span)
        for p, g, f in zip(projected_parts, grad_parts, forward_parts)
    ]
    grad_query, grad_key, grad_value = (
        join_sequences([p[i] for p in backward_parts]) for i in range(3)
    )
    own_query, own_key, own_value = (own_rows(g) for g in (grad_query, grad_key, grad_value))
    own_projected = jnp.concatenate([own_query, own_key, own_value], axis=0)
    line = jnp.arange(window)
    mine = ((line >= skew) & (line < skew + own))[:, None]
    grad_projected = jnp.concatenate(
        [jnp.where(mine, g, jnp.zeros_like(g)) for g in (grad_query, grad_key, grad_value)], axis=0
    )
    near, far = rep_bits(False), rep_bits(True)
    gates = (grad_middle, grad_mixed, grad_query)
    down_weight_grad, down_sizes = rep_scatter(down_weight_grad, near, gates)
    up_weight_grad, up_sizes = rep_scatter(up_weight_grad, far, gates)
    output_weight_grad = contract(attended, grad_mixed, 1, 0).astype(low)[None]
    output_weight_grad, output_sizes = rep_scatter(output_weight_grad, near[:1], (grad_query,))
    for bit in near[1:]:
        output_weight_grad = (
            output_weight_grad.astype(f32) + swap_rep(output_weight_grad, bit).astype(f32)
        ).astype(low)
    output_weight_grad = lax.optimization_barrier(output_weight_grad)
    input_weight_grad = contract(hidden_one, own_projected, 0, 1).astype(low)
    input_weight_grad = input_weight_grad.reshape(shards, own, 3 * own)
    cut = (3 * own // 2) // 128 * 128
    first_part, first_sizes = rep_scatter(input_weight_grad[:, :, :cut], near)
    second_part, second_sizes = rep_scatter(input_weight_grad[:, :, cut:], far)
    turned = exchange(jnp.concatenate([first_part, second_part], axis=2))
    up_weight_grad = rep_gather(exchange(up_weight_grad), far, up_sizes)
    down_weight_grad = rep_gather(down_weight_grad, near, down_sizes)[0]
    output_weight_grad = rep_gather(output_weight_grad, near[:1], output_sizes)[0]
    input_weight_grad = jnp.concatenate(
        [
            rep_gather(turned[:, :, :cut], near, first_sizes),
            rep_gather(turned[:, :, cut:], far, second_sizes),
        ],
        axis=2,
    )
    grad_hidden_one = scatter_relative(
        contract(grad_projected, weight_in, 0, 1)
    )
    normed_one, inverse_one = normalize(layer_input)
    input_grad = grad_middle + norm_back(grad_hidden_one, normed_one, inverse_one, gain_one)

    def own_part(values):
        return lax.dynamic_slice_in_dim(values, index * own, own, 0)

    partial = jnp.stack(
        [
            jnp.sum(grad_hidden_one * normed_one, axis=0),
            jnp.sum(grad_hidden_one, axis=0),
            jnp.sum(grad_hidden_two * normed_two, axis=0),
            jnp.sum(grad_hidden_two, axis=0),
        ]
    )
    for bit in bits_far_first():
        partial = partial + swap(partial, bit)
    complete = jnp.concatenate(
        [own_part(partial[i]) for i in range(4)]
        + [
            jnp.sum(own_query.astype(f32), axis=1),
            jnp.sum(own_value.astype(f32), axis=1),
            own_part(jnp.sum(grad_mixed.astype(f32), axis=0)),
            own_part(jnp.sum(branch.astype(f32), axis=0)),
            jnp.sum(grad_before.astype(f32), axis=0),
        ]
    )
    for bit in rep_bits(False):
        complete = complete + swap_rep(complete, bit)
    (
        first_gain_grad,
        first_shift_grad,
        second_gain_grad,
        second_shift_grad,
        query_bias_grad,
        value_bias_grad,
        output_bias_grad,
        down_bias_grad,
    ) = (complete[i * own : (i + 1) * own] for i in range(8))
    up_bias_grad = complete[8 * own :]
    return (
        block_output.reshape(seqs, span, width),
        input_grad.reshape(seqs, span, width),
        first_gain_grad,
        first_shift_grad,
        jnp.concatenate(
            [
                input_weight_grad[s, :, part * own : (part + 1) * own]
                for part in range(3)
                for s in range(shards)
            ],
            axis=1,
        ).astype(f32),
        query_bias_grad,
        value_bias_grad,
        output_weight_grad.astype(f32),
        output_bias_grad,
        second_gain_grad,
        second_shift_grad,
        jnp.concatenate(
            [up_weight_grad[s] for s in range(shards)], axis=1
        ).astype(f32),
        up_bias_grad,
        down_weight_grad.astype(f32),
        down_bias_grad,
    )


def solution(mesh):
    matrix, vector, tokens = P("shard", None), P("shard"), P("rep", "shard", None)
    return jax.shard_map(
        local,
        mesh=mesh,
        in_specs=(
            tokens,
            vector,
            vector,
            matrix,
            vector,
            vector,
            matrix,
            vector,
            vector,
            vector,
            matrix,
            vector,
            matrix,
            vector,
            tokens,
        ),
        out_specs=(
            tokens,
            tokens,
            vector,
            vector,
            matrix,
            vector,
            vector,
            matrix,
            vector,
            vector,
            vector,
            matrix,
            vector,
            matrix,
            vector,
        ),
        check_vma=False,
    )
```

```python
import functools

import jax
import jax.numpy as jnp
from jax import lax
from jax.experimental import pallas as pl
from jax.experimental.pallas import tpu as pltpu
from jax.sharding import PartitionSpec as P

HEADS = 17

epsilon = 1e-05
score_scale = 0.125
low = jnp.bfloat16
f32 = jnp.float32


def normalize(values):
    centre = jnp.mean(values, axis=-1, keepdims=True)
    centred = values - centre
    inverse = lax.rsqrt(jnp.mean(centred * centred, axis=-1, keepdims=True) + epsilon)
    return (centred * inverse, inverse)


def norm_back(grad, normed, inverse, gain):
    scaled = grad * gain
    first = jnp.mean(scaled, axis=-1, keepdims=True)
    second = jnp.mean(scaled * normed, axis=-1, keepdims=True)
    return inverse * (scaled - first - normed * second)


def gelu_parts(values):
    cumulative = 0.5 * (1.0 + lax.erf(values * 0.7071067811865476))
    density = jnp.exp(-0.5 * values * values) * 0.3989422804014327
    return values * cumulative, cumulative + values * density


def contract(left, right, left_dim, right_dim):
    return lax.dot_general(
        left, right, (((left_dim,), (right_dim,)), ((), ())), preferred_element_type=f32
    )


def swap(values, bit):
    size = lax.axis_size("shard")
    return lax.ppermute(values, "shard", [(i, i ^ bit) for i in range(size)])


def bits_far_first():
    bit = lax.axis_size("shard") // 2
    bits = []
    while bit:
        bits.append(bit)
        bit //= 2
    return bits


def relative_order():
    order = [0]
    for bit in bits_far_first():
        order = order + [o ^ bit for o in order]
    return order


def gather_relative(block):
    for bit in bits_far_first():
        block = jnp.concatenate([block, swap(block, bit)], axis=0)
    return block


def gather_absolute(block):
    index = lax.axis_index("shard")
    stack = block[None]
    for bit in bits_far_first():
        other = swap(stack, bit)
        upper = (index & bit) != 0
        pair = jnp.stack(
            [jnp.where(upper, other, stack), jnp.where(upper, stack, other)], axis=1
        )
        stack = pair.reshape((2 * stack.shape[0],) + block.shape)
    return stack


def scatter_relative(parts):
    for bit in reversed(bits_far_first()):
        half = parts.shape[0] // 2
        other = swap(parts[half:].astype(low), bit)
        parts = parts[:half] + other.astype(f32)
    return parts


def swap_rep(values, bit):
    size = lax.axis_size("rep")
    return lax.ppermute(values, "rep", [(i, i ^ bit) for i in range(size)])


def rep_bits(turned):
    bits, bit = [], 1
    while bit < lax.axis_size("rep"):
        bits.append(bit)
        bit *= 2
    return bits[1:2] + bits[:1] + bits[2:] if turned else bits


def after(values, gate):
    return lax.optimization_barrier((values, gate))[0]


def half_window(rows):
    return min(rows, (rows + 15) // 16 * 8)


def halve(values, bit):
    rows = values.shape[1]
    window = half_window(rows)
    mine = (lax.axis_index("rep") // bit) % 2
    far = rows - window
    send = lax.dynamic_slice_in_dim(values, (1 - mine) * far, window, 1)
    keep = lax.dynamic_slice_in_dim(values, mine * far, window, 1)
    return keep, swap_rep(send, bit)


def add(keep, other):
    return (keep.astype(f32) + other.astype(f32)).astype(low)


def join(values, other, bit, rows):
    window = values.shape[1]
    upper = (lax.axis_index("rep") // bit) % 2 != 0
    first = jnp.where(upper, other, values)
    second = jnp.where(upper, values, other)
    return jnp.concatenate([first, second[:, 2 * window - rows :]], axis=1)


class Chain:
    def __init__(self, steps):
        self.steps = steps
        self.result = None
        self.take(None)

    def take(self, got):
        try:
            self.waits = self.steps.send(got)
        except StopIteration as end:
            self.waits = None
            self.result = end.value


def advance(chains, gate=()):
    live = [c for c in chains if c.waits is not None]
    arrived, _ = lax.optimization_barrier((tuple(c.waits for c in live), gate))
    for chain, got in zip(live, arrived):
        chain.take(got)


def scatter_steps(lanes, orders):
    sizes = []
    for step in range(len(orders[0])):
        sizes.append(lanes[0].shape[1])
        halves = [halve(v, order[step]) for v, order in zip(lanes, orders)]
        others = yield tuple(h[1] for h in halves)
        lanes = [add(h[0], other) for h, other in zip(halves, others)]
    return list(lax.optimization_barrier(tuple(lanes))), sizes


def gather_steps(lanes, orders, sizes):
    for step in reversed(range(len(orders[0]))):
        others = yield tuple(swap_rep(v, order[step]) for v, order in zip(lanes, orders))
        lanes = [
            join(v, other, order[step], sizes[step])
            for v, other, order in zip(lanes, others, orders)
        ]
    return lanes


def exchange_steps(blocks):
    size = lax.axis_size("shard")
    index = lax.axis_index("shard")
    pieces = [lax.dynamic_index_in_dim(blocks, index ^ o, 0, keepdims=True) for o in range(size)]
    others = yield tuple(swap(pieces[o], o) for o in range(1, size))
    result = jnp.zeros_like(blocks)
    for o, piece in enumerate(pieces[:1] + list(others)):
        result = lax.dynamic_update_slice_in_dim(result, piece, index ^ o, 0)
    return [result[i] for i in range(size)]


def plain_sum(values, order):
    lanes, sizes = yield from scatter_steps([values], [order])
    lanes = yield from gather_steps(lanes, [order], sizes)
    return lanes[0]


def turned_sum(values, order):
    lanes, sizes = yield from scatter_steps([values], [order])
    blocks = yield from exchange_steps(lanes[0])
    lanes = yield from gather_steps([jnp.concatenate(blocks, axis=1)[None]], [order], sizes)
    return lanes[0][0]


def mixer_sum(first, second, orders, own):
    lanes, sizes = yield from scatter_steps([first, second], orders)
    blocks = yield from exchange_steps(
        jnp.concatenate([lanes[0], lanes[1][:, :, :own]], axis=2)
    )
    parts = [
        jnp.concatenate([b[:, i * own : (i + 1) * own] for b in blocks], axis=1) for i in range(3)
    ]
    output = jnp.concatenate([lanes[1][i, :, own:] for i in range(len(blocks))], axis=1)
    lanes = [
        jnp.concatenate(parts[:2], axis=1)[None],
        jnp.concatenate([parts[2], output], axis=1)[None],
    ]
    lanes = yield from gather_steps(lanes, orders, sizes)
    return lanes[0][0], lanes[1][0]


def shard_sum(parts):
    for bit in reversed(bits_far_first()):
        half = parts.shape[0] // 2
        (other,) = yield (swap(parts[half:].astype(low), bit),)
        parts = parts[:half] + other.astype(f32)
    return parts


def vector_sum(partial, complete, own_part):
    for bit in bits_far_first():
        (other,) = yield (swap(partial, bit),)
        partial = partial + other
    total = jnp.concatenate([own_part(p) for p in partial] + complete)
    for bit in rep_bits(False):
        (other,) = yield (swap_rep(total, bit),)
        total = total + other
    return total


def exchange(blocks):
    size = lax.axis_size("shard")
    index = lax.axis_index("shard")
    result = jnp.zeros_like(blocks)
    for offset in range(size):
        peer = index ^ offset
        piece = lax.dynamic_index_in_dim(blocks, peer, 0, keepdims=True)
        if offset:
            piece = swap(piece, offset)
        result = lax.dynamic_update_slice_in_dim(result, piece, peer, 0)
    return result


def send_halves(blocks):
    index = lax.axis_index("shard")
    size = lax.axis_size("shard")
    half = blocks.shape[1] // 2
    part = (lax.axis_index("rep") % 2) * half
    pieces = []
    for offset in range(size):
        piece = lax.dynamic_index_in_dim(blocks, index ^ offset, 0, keepdims=True)
        if offset >= 2:
            piece = lax.dynamic_slice_in_dim(piece, part, half, 1)
        if offset:
            piece = swap(piece, offset)
        pieces.append(piece)
    return pieces


def join_halves(pieces):
    index = lax.axis_index("shard")
    upper = lax.axis_index("rep") % 2 != 0
    full = pieces[0].shape[1]
    count = len(pieces)
    if count > 2:
        mine = jnp.concatenate(pieces[2:], axis=0)
        other = swap_rep(mine, 1)
        halves = jnp.concatenate(
            [jnp.where(upper, other, mine), jnp.where(upper, mine, other)], axis=1
        )
        pieces = pieces[:2] + [halves[i : i + 1] for i in range(count - 2)]
    result = jnp.zeros((count,) + pieces[0].shape[1:], pieces[0].dtype)
    for offset, piece in enumerate(pieces):
        result = lax.dynamic_update_slice_in_dim(result, piece, index ^ offset, 0)
    return result


def visible_part(scores, top, block, fill):
    rows = lax.broadcasted_iota(jnp.int32, (block, block), 0)
    cols = lax.broadcasted_iota(jnp.int32, (block, block), 1)
    last = jnp.where(rows <= cols, scores[top:], fill)
    if top == 0:
        return last
    return jnp.concatenate([scores[:top], last], axis=0)


def turn(values):
    return values.astype(f32).T


def forward_kernel(blocks, block, place, q_ref, k_ref, v_ref, o_ref, low_ref, log_ref, k_rows, v_cols):
    for i in range(blocks):
        here = pl.ds(pl.multiple_of(place[i] * block, block), block)
        there = pl.ds(i * block, block)
        k_rows[there, :] = turn(k_ref[:, here]).astype(low)
        v_cols[:, there] = v_ref[:, here]
    for i in range(blocks):
        here = pl.ds(pl.multiple_of(place[i] * block, block), block)
        top = i * block
        count = top + block
        q_cols = q_ref[:, here] * jnp.asarray(score_scale, low)
        scores = contract(k_rows[:count, :], q_cols, 1, 0)
        scores = visible_part(scores, top, block, -jnp.inf)
        peak = jnp.max(scores, axis=0, keepdims=True)
        weights = jnp.exp(scores - peak)
        total = jnp.sum(weights, axis=0, keepdims=True)
        mixed = contract(v_cols[:, :count], weights.astype(low), 1, 0) / total
        o_ref[:, here] = mixed
        low_ref[:, here] = mixed.astype(low)
        log_ref[0, :, here] = peak + jnp.log(total)


def backward_kernel(
    blocks,
    block,
    place,
    q_ref,
    k_ref,
    v_ref,
    g_ref,
    o_ref,
    log_ref,
    dq_ref,
    dk_ref,
    dv_ref,
    k_rows,
    v_rows,
    k_cols,
    dk_rows,
    dv_rows,
):
    for i in range(blocks):
        here = pl.ds(pl.multiple_of(place[i] * block, block), block)
        there = pl.ds(i * block, block)
        k_rows[there, :] = turn(k_ref[:, here]).astype(low)
        v_rows[there, :] = turn(v_ref[:, here]).astype(low)
        k_cols[:, there] = k_ref[:, here]
    for i in reversed(range(blocks)):
        here = pl.ds(pl.multiple_of(place[i] * block, block), block)
        top = i * block
        count = top + block
        q_cols = q_ref[:, here] * jnp.asarray(score_scale, low)
        g_cols = g_ref[:, here]
        q_rows = turn(q_cols).astype(low)
        g_rows = turn(g_cols).astype(low)
        correction = jnp.sum(g_cols.astype(f32) * o_ref[:, here], axis=0, keepdims=True)
        scores = contract(k_rows[:count, :], q_cols, 1, 0)
        probs = jnp.exp(scores - log_ref[0, :, here])
        probs = visible_part(probs, top, block, 0.0)
        grad_probs = contract(v_rows[:count, :], g_cols, 1, 0)
        grad_scores = (probs * (grad_probs - correction)).astype(low)
        dv_part = contract(probs.astype(low), g_rows, 1, 0)
        dk_part = contract(grad_scores, q_rows, 1, 0)
        if i == blocks - 1:
            dv_rows[:count, :] = dv_part
            dk_rows[:count, :] = dk_part
        else:
            dv_rows[:count, :] += dv_part
            dk_rows[:count, :] += dk_part
        dq = contract(k_cols[:, :count], grad_scores, 1, 0) * score_scale
        dq_ref[:, here] = dq.astype(low)
    for i in range(blocks):
        here = pl.ds(pl.multiple_of(place[i] * block, block), block)
        there = pl.ds(i * block, block)
        dk_ref[:, here] = dk_rows[there, :].T.astype(low)
        dv_ref[:, here] = dv_rows[there, :].T.astype(low)


def head_spec(size, length, first):
    return pl.BlockSpec((size, length), lambda h, place: (first + h, 0))


def attend_forward(place, projected, heads, block):
    size = projected.shape[0] // (3 * heads)
    length = projected.shape[1]
    blocks = length // block
    row = pl.BlockSpec((1, 1, length), lambda h, place: (h, 0, 0))
    return pl.pallas_call(
        functools.partial(forward_kernel, blocks, block),
        grid_spec=pltpu.PrefetchScalarGridSpec(
            num_scalar_prefetch=1,
            grid=(heads,),
            in_specs=[
                head_spec(size, length, 0),
                head_spec(size, length, heads),
                head_spec(size, length, 2 * heads),
            ],
            out_specs=[head_spec(size, length, 0), head_spec(size, length, 0), row],
            scratch_shapes=[
                pltpu.VMEM((length, size), low),
                pltpu.VMEM((size, length), low),
            ],
        ),
        out_shape=[
            jax.ShapeDtypeStruct((heads * size, length), f32),
            jax.ShapeDtypeStruct((heads * size, length), low),
            jax.ShapeDtypeStruct((heads, 1, length), f32),
        ],
        cost_estimate=pl.CostEstimate(
            flops=4 * heads * length * length * size,
            bytes_accessed=heads * length * size * 12,
            transcendentals=heads * length * length,
        ),
        compiler_params=pltpu.CompilerParams(vmem_limit_bytes=32 * 1024 * 1024),
        name="attend_forward",
    )(place, projected, projected, projected)


def attend_backward(place, projected, grad, mixed, log_total, heads, block):
    size = projected.shape[0] // (3 * heads)
    length = projected.shape[1]
    blocks = length // block
    row = pl.BlockSpec((1, 1, length), lambda h, place: (h, 0, 0))
    out = jax.ShapeDtypeStruct((heads * size, length), low)
    return pl.pallas_call(
        functools.partial(backward_kernel, blocks, block),
        grid_spec=pltpu.PrefetchScalarGridSpec(
            num_scalar_prefetch=1,
            grid=(heads,),
            in_specs=[
                head_spec(size, length, 0),
                head_spec(size, length, heads),
                head_spec(size, length, 2 * heads),
                head_spec(size, length, 0),
                head_spec(size, length, 0),
                row,
            ],
            out_specs=[head_spec(size, length, 0)] * 3,
            scratch_shapes=[
                pltpu.VMEM((length, size), low),
                pltpu.VMEM((length, size), low),
                pltpu.VMEM((size, length), low),
                pltpu.VMEM((length, size), f32),
                pltpu.VMEM((length, size), f32),
            ],
        ),
        out_shape=[out, out, out],
        cost_estimate=pl.CostEstimate(
            flops=10 * heads * length * length * size,
            bytes_accessed=heads * length * size * 20,
            transcendentals=heads * length * length,
        ),
        compiler_params=pltpu.CompilerParams(vmem_limit_bytes=32 * 1024 * 1024),
        name="attend_backward",
    )(place, projected, projected, projected, grad, mixed, log_total)


def local(
    block_input,
    first_gain,
    first_shift,
    query_key_value_weight,
    query_bias,
    value_bias,
    attention_output_weight,
    attention_output_bias,
    second_gain,
    second_shift,
    up_weight,
    up_bias,
    down_weight,
    down_bias,
    cotangent,
):
    shards = lax.axis_size("shard")
    index = lax.axis_index("shard")
    seqs, span, width = block_input.shape
    size = width // HEADS
    own = width // shards
    hidden = up_bias.shape[0]
    starts = [d * own // size for d in range(shards)]
    heads = max(-(-(d + 1) * own // size) - starts[d] for d in range(shards))
    window = heads * size
    pad = window - own
    start = index * own // size
    skew = index * own - start * size
    order = relative_order()
    inverse_order = jnp.asarray([order.index(o) for o in range(shards)], jnp.int32)
    place = inverse_order[jnp.arange(shards, dtype=jnp.int32) ^ index]

    own_input = block_input.reshape(seqs * span, width)
    inputs_all = gather_relative(own_input)
    vectors = gather_absolute(
        jnp.stack(
            [
                first_gain,
                first_shift,
                query_bias,
                value_bias,
                attention_output_bias,
                second_gain,
                second_shift,
                down_bias,
            ]
        )
    )
    vectors = vectors.transpose(1, 0, 2).reshape(8, width)
    gain_one, shift_one, bias_query, bias_value, bias_out, gain_two, shift_two, bias_down = (
        vectors[i] for i in range(8)
    )
    weight_in = exchange(
        jnp.stack(
            [
                jnp.concatenate(
                    [
                        query_key_value_weight[
                            :, part * width + s * size : part * width + s * size + window
                        ]
                        for part in range(3)
                    ],
                    axis=1,
                )
                for s in starts
            ]
        )
    ).reshape(width, 3 * window)
    up_blocks = jnp.stack([up_weight[:, s * hidden : (s + 1) * hidden] for s in range(shards)])
    up_pieces = send_halves(after(up_blocks, weight_in))
    to_right = [(i, i + 1) for i in range(shards - 1)]
    to_left = [(i + 1, i) for i in range(shards - 1)]
    weight_out_window = lax.dynamic_slice_in_dim(
        jnp.concatenate(
            [
                lax.ppermute(attention_output_weight[own - pad :], "shard", to_right),
                attention_output_weight,
                lax.ppermute(attention_output_weight[:pad], "shard", to_left),
            ],
            axis=0,
        ),
        pad - skew,
        window,
        0,
    )
    branch = gather_relative(after(cotangent.reshape(seqs * span, width).astype(low), up_pieces))
    grad_out = cotangent.reshape(seqs * span, width)

    def own_rows(values):
        return lax.dynamic_slice_in_dim(values, skew, own, 0)

    rows = shards * seqs * span
    normed_all, _ = normalize(inputs_all.astype(f32))
    hidden_one = (normed_all * gain_one + shift_one).astype(low)
    bias_window = jnp.concatenate(
        [
            lax.dynamic_slice_in_dim(bias_query, start * size, window, 0),
            jnp.zeros((window,), low),
            lax.dynamic_slice_in_dim(bias_value, start * size, window, 0),
        ]
    ).astype(f32)
    projected = (contract(weight_in, hidden_one, 0, 1) + bias_window[:, None]).astype(low)

    def per_sequence(values):
        lead = values.shape[:-1]
        split = values.reshape(lead + (shards, seqs, span))
        return [split[..., :, s, :].reshape(lead + (shards * span,)) for s in range(seqs)]

    def join_sequences(parts):
        if seqs == 1:
            return parts[0]
        lead = parts[0].shape[:-1]
        joined = jnp.stack([p.reshape(lead + (shards, span)) for p in parts], axis=-2)
        return joined.reshape(lead + (rows,))

    projected_parts = per_sequence(projected) if seqs > 1 else [projected]
    forward_parts = [attend_forward(place, p, heads, span) for p in projected_parts]
    attended = join_sequences([p[1] for p in forward_parts])
    attended, up_pieces = lax.optimization_barrier((attended, up_pieces))
    attended = own_rows(attended)
    weight_up = join_halves(up_pieces).reshape(width, hidden)
    mixed_sum = scatter_relative(
        contract(attended, attention_output_weight, 0, 0)
    )
    layer_input = own_input.astype(f32)
    middle = layer_input + mixed_sum + bias_out

    normed_two, inverse_two = normalize(middle)
    hidden_two = gather_relative((normed_two * gain_two + shift_two).astype(low))
    before = contract(hidden_two, weight_up, 1, 0) + up_bias
    activated, slope = gelu_parts(before)
    activated = activated.astype(low)
    grad_before = (contract(branch, down_weight, 1, 1) * slope).astype(low)
    hidden_two_sum = contract(grad_before, weight_up, 1, 1)
    hidden_two_sum, late_before, late_active = lax.optimization_barrier(
        (hidden_two_sum, grad_before, activated)
    )
    grad_hidden_two = scatter_relative(hidden_two_sum)
    down_weight_grad = contract(late_active, branch, 0, 0).astype(low)[None]
    up_weight_grad = contract(hidden_two, late_before, 0, 0).astype(low)
    up_weight_grad = up_weight_grad.reshape(shards, own, hidden)
    down_sum = contract(late_active, down_weight, 1, 0)
    grad_middle = grad_out + norm_back(grad_hidden_two, normed_two, inverse_two, gain_two)
    near, far = rep_bits(False), rep_bits(True)
    down_chain = Chain(plain_sum(down_weight_grad, near))
    up_chain = Chain(turned_sum(up_weight_grad, far))
    advance([down_chain, up_chain], grad_middle)

    grad_mixed = gather_relative(grad_middle.astype(low))
    grad_attended = contract(weight_out_window, grad_mixed, 1, 1).astype(low)
    grad_parts = per_sequence(grad_attended) if seqs > 1 else [grad_attended]
    backward_parts = [
        attend_backward(place, p, g, f[0], f[2], heads, span)
        for p, g, f in zip(projected_parts, grad_parts, forward_parts)
    ]
    grad_query, grad_key, grad_value = (
        join_sequences([p[i] for p in backward_parts]) for i in range(3)
    )
    own_query, own_key, own_value = (own_rows(g) for g in (grad_query, grad_key, grad_value))
    own_projected = jnp.concatenate([own_query, own_key, own_value], axis=0)
    line = jnp.arange(window)
    mine = ((line >= skew) & (line < skew + own))[:, None]
    grad_projected = jnp.concatenate(
        [jnp.where(mine, g, jnp.zeros_like(g)) for g in (grad_query, grad_key, grad_value)], axis=0
    )
    output_weight_grad = contract(attended, grad_mixed, 1, 0).astype(low)
    block_chain = Chain(shard_sum(after(down_sum, grad_mixed)))
    advance([down_chain, up_chain, block_chain], grad_query)

    def by_owner(gradient):
        return gradient.reshape(shards, own, gradient.shape[1])

    first_part = by_owner(contract(hidden_one, own_projected[: 2 * own], 0, 1).astype(low))
    second_part = by_owner(contract(hidden_one, own_value, 0, 1).astype(low))
    output_blocks = jnp.stack(
        [output_weight_grad[:, s * own : (s + 1) * own] for s in range(shards)]
    )
    second_part = jnp.concatenate([second_part, output_blocks], axis=2)
    mixer_chain = Chain(mixer_sum(first_part, second_part, [near, far], own))
    hidden_chain = Chain(shard_sum(contract(grad_projected, weight_in, 0, 1)))
    chains = [down_chain, up_chain, block_chain, mixer_chain, hidden_chain]
    while hidden_chain.waits is not None:
        advance(chains)
    block_output = middle + block_chain.result + bias_down
    grad_hidden_one = hidden_chain.result
    normed_one, inverse_one = normalize(layer_input)
    input_grad = grad_middle + norm_back(grad_hidden_one, normed_one, inverse_one, gain_one)

    def own_part(values):
        return lax.dynamic_slice_in_dim(values, index * own, own, 0)

    partial = jnp.stack(
        [
            jnp.sum(grad_hidden_one * normed_one, axis=0),
            jnp.sum(grad_hidden_one, axis=0),
            jnp.sum(grad_hidden_two * normed_two, axis=0),
            jnp.sum(grad_hidden_two, axis=0),
        ]
    )
    vector_chain = Chain(
        vector_sum(
            partial,
            [
                jnp.sum(own_query.astype(f32), axis=1),
                jnp.sum(own_value.astype(f32), axis=1),
                own_part(jnp.sum(grad_mixed.astype(f32), axis=0)),
                own_part(jnp.sum(branch.astype(f32), axis=0)),
                jnp.sum(grad_before.astype(f32), axis=0),
            ],
            own_part,
        )
    )
    chains.append(vector_chain)
    while any(c.waits is not None for c in chains):
        advance(chains)
    complete = vector_chain.result
    down_weight_grad = down_chain.result[0]
    up_weight_grad = up_chain.result
    first_part, second_part = mixer_chain.result
    input_weight_grad = jnp.concatenate([first_part, second_part[:, :width]], axis=1)
    output_weight_grad = second_part[:, width:]
    (
        first_gain_grad,
        first_shift_grad,
        second_gain_grad,
        second_shift_grad,
        query_bias_grad,
        value_bias_grad,
        output_bias_grad,
        down_bias_grad,
    ) = (complete[i * own : (i + 1) * own] for i in range(8))
    up_bias_grad = complete[8 * own :]
    return (
        block_output.reshape(seqs, span, width),
        input_grad.reshape(seqs, span, width),
        first_gain_grad,
        first_shift_grad,
        input_weight_grad.astype(f32),
        query_bias_grad,
        value_bias_grad,
        output_weight_grad.astype(f32),
        output_bias_grad,
        second_gain_grad,
        second_shift_grad,
        up_weight_grad.astype(f32),
        up_bias_grad,
        down_weight_grad.astype(f32),
        down_bias_grad,
    )


def solution(mesh):
    matrix, vector, tokens = P("shard", None), P("shard"), P("rep", "shard", None)
    return jax.shard_map(
        local,
        mesh=mesh,
        in_specs=(
            tokens,
            vector,
            vector,
            matrix,
            vector,
            vector,
            matrix,
            vector,
            vector,
            vector,
            matrix,
            vector,
            matrix,
            vector,
            tokens,
        ),
        out_specs=(
            tokens,
            tokens,
            vector,
            vector,
            matrix,
            vector,
            vector,
            matrix,
            vector,
            vector,
            vector,
            matrix,
            vector,
            matrix,
            vector,
        ),
        check_vma=False,
    )
```

```python
import functools

import jax
import jax.numpy as jnp
from jax import lax
from jax.experimental import pallas as pl
from jax.experimental.pallas import tpu as pltpu
from jax.sharding import PartitionSpec as P

HEADS = 17

epsilon = 1e-05
score_scale = 0.125
low = jnp.bfloat16
f32 = jnp.float32


def normalize(values):
    centre = jnp.mean(values, axis=-1, keepdims=True)
    centred = values - centre
    inverse = lax.rsqrt(jnp.mean(centred * centred, axis=-1, keepdims=True) + epsilon)
    return (centred * inverse, inverse)


def norm_back(grad, normed, inverse, gain):
    scaled = grad * gain
    first = jnp.mean(scaled, axis=-1, keepdims=True)
    second = jnp.mean(scaled * normed, axis=-1, keepdims=True)
    return inverse * (scaled - first - normed * second)


def gelu_parts(values):
    cumulative = 0.5 * (1.0 + lax.erf(values * 0.7071067811865476))
    density = jnp.exp(-0.5 * values * values) * 0.3989422804014327
    return values * cumulative, cumulative + values * density


def contract(left, right, left_dim, right_dim):
    return lax.dot_general(
        left, right, (((left_dim,), (right_dim,)), ((), ())), preferred_element_type=f32
    )


def swap(values, bit):
    size = lax.axis_size("shard")
    return lax.ppermute(values, "shard", [(i, i ^ bit) for i in range(size)])


def bits_far_first():
    bit = lax.axis_size("shard") // 2
    bits = []
    while bit:
        bits.append(bit)
        bit //= 2
    return bits


def relative_order():
    order = [0]
    for bit in bits_far_first():
        order = order + [o ^ bit for o in order]
    return order


def gather_relative(block):
    for bit in bits_far_first():
        block = jnp.concatenate([block, swap(block, bit)], axis=0)
    return block


def gather_absolute(block):
    index = lax.axis_index("shard")
    stack = block[None]
    for bit in bits_far_first():
        other = swap(stack, bit)
        upper = (index & bit) != 0
        pair = jnp.stack(
            [jnp.where(upper, other, stack), jnp.where(upper, stack, other)], axis=1
        )
        stack = pair.reshape((2 * stack.shape[0],) + block.shape)
    return stack


def scatter_relative(parts):
    for bit in reversed(bits_far_first()):
        half = parts.shape[0] // 2
        other = swap(parts[half:].astype(low), bit)
        parts = parts[:half] + other.astype(f32)
    return parts


def swap_rep(values, bit):
    size = lax.axis_size("rep")
    return lax.ppermute(values, "rep", [(i, i ^ bit) for i in range(size)])


def rep_bits(turned):
    bits, bit = [], 1
    while bit < lax.axis_size("rep"):
        bits.append(bit)
        bit *= 2
    return bits[1:2] + bits[:1] + bits[2:] if turned else bits


def after(values, gate):
    return lax.optimization_barrier((values, gate))


def half_window(rows):
    return min(rows, (rows + 15) // 16 * 8)


def half_of(values, index):
    rows = values.shape[1]
    window = half_window(rows)
    return lax.dynamic_slice_in_dim(values, index * (rows - window), window, 1)


def sent_half(values, bit):
    return swap_rep(half_of(values, 1 - (lax.axis_index("rep") // bit) % 2), bit)


def kept_half(values, bit):
    return half_of(values, (lax.axis_index("rep") // bit) % 2)


def add(keep, other):
    return (keep.astype(f32) + other.astype(f32)).astype(low)


def join(values, other, bit, rows):
    window = values.shape[1]
    upper = (lax.axis_index("rep") // bit) % 2 != 0
    first = jnp.where(upper, other, values)
    second = jnp.where(upper, values, other)
    return jnp.concatenate([first, second[:, 2 * window - rows :]], axis=1)


class Chain:
    def __init__(self, steps):
        self.steps = steps
        self.take(None)

    def take(self, got):
        try:
            self.waits, self.holds = self.steps.send(got)
        except StopIteration as end:
            self.waits, self.holds = None, end.value

    def advance(self, previous, gate=()):
        if self.waits is not None:
            if previous is self:
                waits, gate = after(self.waits, gate)
            else:
                waits, (previous.holds, gate) = after(self.waits, (previous.holds, gate))
            self.take((waits, self.holds))
        return gate


def scatter_steps(lanes, orders):
    sizes = []
    for step in range(len(orders[0])):
        sizes.append(lanes[0].shape[1])
        others, held = yield (
            tuple(sent_half(v, order[step]) for v, order in zip(lanes, orders)),
            tuple(lanes),
        )
        lanes = [
            add(kept_half(v, order[step]), other) for v, other, order in zip(held, others, orders)
        ]
    return list(lax.optimization_barrier(tuple(lanes))), sizes


def gather_steps(lanes, orders, sizes):
    for step in reversed(range(len(orders[0]))):
        others, lanes = yield (
            tuple(swap_rep(v, order[step]) for v, order in zip(lanes, orders)),
            tuple(lanes),
        )
        lanes = [
            join(v, other, order[step], sizes[step])
            for v, other, order in zip(lanes, others, orders)
        ]
    return lanes


def exchange_steps(blocks):
    size = lax.axis_size("shard")
    index = lax.axis_index("shard")
    pieces = [lax.dynamic_index_in_dim(blocks, index ^ o, 0, keepdims=True) for o in range(size)]
    others, first = yield tuple(swap(pieces[o], o) for o in range(1, size)), pieces[0]
    result = jnp.zeros_like(blocks)
    for o, piece in enumerate((first,) + tuple(others)):
        result = lax.dynamic_update_slice_in_dim(result, piece, index ^ o, 0)
    return [result[i] for i in range(size)]


def plain_sum(values, order):
    lanes, sizes = yield from scatter_steps([values], [order])
    lanes = yield from gather_steps(lanes, [order], sizes)
    return lanes[0]


def turned_sum(values, order):
    lanes, sizes = yield from scatter_steps([values], [order])
    blocks = yield from exchange_steps(lanes[0])
    lanes = yield from gather_steps([jnp.concatenate(blocks, axis=1)[None]], [order], sizes)
    return lanes[0][0]


def mixer_sum(first, second, orders, own):
    lanes, sizes = yield from scatter_steps([first, second], orders)
    blocks = yield from exchange_steps(
        jnp.concatenate([lanes[0], lanes[1][:, :, :own]], axis=2)
    )
    parts = [
        jnp.concatenate([b[:, i * own : (i + 1) * own] for b in blocks], axis=1) for i in range(3)
    ]
    output = jnp.concatenate([lanes[1][i, :, own:] for i in range(len(blocks))], axis=1)
    lanes = [
        jnp.concatenate(parts[:2], axis=1)[None],
        jnp.concatenate([parts[2], output], axis=1)[None],
    ]
    lanes = yield from gather_steps(lanes, orders, sizes)
    return lanes[0][0], lanes[1][0]


def shard_sum(parts):
    for bit in reversed(bits_far_first()):
        half = parts.shape[0] // 2
        (other,), kept = yield (swap(parts[half:].astype(low), bit),), parts[:half]
        parts = kept + other.astype(f32)
    return parts


def vector_sum(partial, complete, own_part):
    for bit in bits_far_first():
        (other,), partial = yield (swap(partial, bit),), partial
        partial = partial + other
    total = jnp.concatenate([own_part(p) for p in partial] + complete)
    for bit in rep_bits(False):
        (other,), total = yield (swap_rep(total, bit),), total
        total = total + other
    return total


def exchange(blocks):
    size = lax.axis_size("shard")
    index = lax.axis_index("shard")
    result = jnp.zeros_like(blocks)
    for offset in range(size):
        peer = index ^ offset
        piece = lax.dynamic_index_in_dim(blocks, peer, 0, keepdims=True)
        if offset:
            piece = swap(piece, offset)
        result = lax.dynamic_update_slice_in_dim(result, piece, peer, 0)
    return result


def send_halves(blocks):
    index = lax.axis_index("shard")
    size = lax.axis_size("shard")
    half = blocks.shape[1] // 2
    part = (lax.axis_index("rep") % 2) * half
    pieces = []
    for offset in range(size):
        piece = lax.dynamic_index_in_dim(blocks, index ^ offset, 0, keepdims=True)
        if offset >= 2:
            piece = lax.dynamic_slice_in_dim(piece, part, half, 1)
        if offset:
            piece = swap(piece, offset)
        pieces.append(piece)
    return pieces


def join_halves(pieces):
    index = lax.axis_index("shard")
    upper = lax.axis_index("rep") % 2 != 0
    full = pieces[0].shape[1]
    count = len(pieces)
    if count > 2:
        mine = jnp.concatenate(pieces[2:], axis=0)
        other = swap_rep(mine, 1)
        halves = jnp.concatenate(
            [jnp.where(upper, other, mine), jnp.where(upper, mine, other)], axis=1
        )
        pieces = pieces[:2] + [halves[i : i + 1] for i in range(count - 2)]
    result = jnp.zeros((count,) + pieces[0].shape[1:], pieces[0].dtype)
    for offset, piece in enumerate(pieces):
        result = lax.dynamic_update_slice_in_dim(result, piece, index ^ offset, 0)
    return result


def visible_part(scores, top, block, fill):
    rows = lax.broadcasted_iota(jnp.int32, (block, block), 0)
    cols = lax.broadcasted_iota(jnp.int32, (block, block), 1)
    last = jnp.where(rows <= cols, scores[top:], fill)
    if top == 0:
        return last
    return jnp.concatenate([scores[:top], last], axis=0)


def turn(values):
    return values.astype(f32).T


def forward_kernel(blocks, block, place, q_ref, k_ref, v_ref, o_ref, low_ref, log_ref, k_rows, v_cols):
    for i in range(blocks):
        here = pl.ds(pl.multiple_of(place[i] * block, block), block)
        there = pl.ds(i * block, block)
        k_rows[there, :] = turn(k_ref[:, here]).astype(low)
        v_cols[:, there] = v_ref[:, here]
    for i in range(blocks):
        here = pl.ds(pl.multiple_of(place[i] * block, block), block)
        top = i * block
        count = top + block
        q_cols = q_ref[:, here] * jnp.asarray(score_scale, low)
        scores = contract(k_rows[:count, :], q_cols, 1, 0)
        scores = visible_part(scores, top, block, -jnp.inf)
        peak = jnp.max(scores, axis=0, keepdims=True)
        weights = jnp.exp(scores - peak)
        total = jnp.sum(weights, axis=0, keepdims=True)
        mixed = contract(v_cols[:, :count], weights.astype(low), 1, 0) / total
        o_ref[:, here] = mixed
        low_ref[:, here] = mixed.astype(low)
        log_ref[0, :, here] = peak + jnp.log(total)


def backward_kernel(
    blocks,
    block,
    place,
    q_ref,
    k_ref,
    v_ref,
    g_ref,
    o_ref,
    log_ref,
    dq_ref,
    dk_ref,
    dv_ref,
    k_rows,
    v_rows,
    k_cols,
    dk_rows,
    dv_rows,
):
    for i in range(blocks):
        here = pl.ds(pl.multiple_of(place[i] * block, block), block)
        there = pl.ds(i * block, block)
        k_rows[there, :] = turn(k_ref[:, here]).astype(low)
        v_rows[there, :] = turn(v_ref[:, here]).astype(low)
        k_cols[:, there] = k_ref[:, here]
    for i in reversed(range(blocks)):
        here = pl.ds(pl.multiple_of(place[i] * block, block), block)
        top = i * block
        count = top + block
        q_cols = q_ref[:, here] * jnp.asarray(score_scale, low)
        g_cols = g_ref[:, here]
        q_rows = turn(q_cols).astype(low)
        g_rows = turn(g_cols).astype(low)
        correction = jnp.sum(g_cols.astype(f32) * o_ref[:, here], axis=0, keepdims=True)
        scores = contract(k_rows[:count, :], q_cols, 1, 0)
        probs = jnp.exp(scores - log_ref[0, :, here])
        probs = visible_part(probs, top, block, 0.0)
        grad_probs = contract(v_rows[:count, :], g_cols, 1, 0)
        grad_scores = (probs * (grad_probs - correction)).astype(low)
        dv_part = contract(probs.astype(low), g_rows, 1, 0)
        dk_part = contract(grad_scores, q_rows, 1, 0)
        if i == blocks - 1:
            dv_rows[:count, :] = dv_part
            dk_rows[:count, :] = dk_part
        else:
            dv_rows[:count, :] += dv_part
            dk_rows[:count, :] += dk_part
        dq = contract(k_cols[:, :count], grad_scores, 1, 0) * score_scale
        dq_ref[:, here] = dq.astype(low)
    for i in range(blocks):
        here = pl.ds(pl.multiple_of(place[i] * block, block), block)
        there = pl.ds(i * block, block)
        dk_ref[:, here] = dk_rows[there, :].T.astype(low)
        dv_ref[:, here] = dv_rows[there, :].T.astype(low)


def head_spec(size, length, first):
    return pl.BlockSpec((size, length), lambda h, place: (first + h, 0))


def attend_forward(place, projected, heads, block):
    size = projected.shape[0] // (3 * heads)
    length = projected.shape[1]
    blocks = length // block
    row = pl.BlockSpec((1, 1, length), lambda h, place: (h, 0, 0))
    return pl.pallas_call(
        functools.partial(forward_kernel, blocks, block),
        grid_spec=pltpu.PrefetchScalarGridSpec(
            num_scalar_prefetch=1,
            grid=(heads,),
            in_specs=[
                head_spec(size, length, 0),
                head_spec(size, length, heads),
                head_spec(size, length, 2 * heads),
            ],
            out_specs=[head_spec(size, length, 0), head_spec(size, length, 0), row],
            scratch_shapes=[
                pltpu.VMEM((length, size), low),
                pltpu.VMEM((size, length), low),
            ],
        ),
        out_shape=[
            jax.ShapeDtypeStruct((heads * size, length), f32),
            jax.ShapeDtypeStruct((heads * size, length), low),
            jax.ShapeDtypeStruct((heads, 1, length), f32),
        ],
        cost_estimate=pl.CostEstimate(
            flops=4 * heads * length * length * size,
            bytes_accessed=heads * length * size * 12,
            transcendentals=heads * length * length,
        ),
        compiler_params=pltpu.CompilerParams(vmem_limit_bytes=32 * 1024 * 1024),
        name="attend_forward",
    )(place, projected, projected, projected)


def attend_backward(place, projected, grad, mixed, log_total, heads, block):
    size = projected.shape[0] // (3 * heads)
    length = projected.shape[1]
    blocks = length // block
    row = pl.BlockSpec((1, 1, length), lambda h, place: (h, 0, 0))
    out = jax.ShapeDtypeStruct((heads * size, length), low)
    return pl.pallas_call(
        functools.partial(backward_kernel, blocks, block),
        grid_spec=pltpu.PrefetchScalarGridSpec(
            num_scalar_prefetch=1,
            grid=(heads,),
            in_specs=[
                head_spec(size, length, 0),
                head_spec(size, length, heads),
                head_spec(size, length, 2 * heads),
                head_spec(size, length, 0),
                head_spec(size, length, 0),
                row,
            ],
            out_specs=[head_spec(size, length, 0)] * 3,
            scratch_shapes=[
                pltpu.VMEM((length, size), low),
                pltpu.VMEM((length, size), low),
                pltpu.VMEM((size, length), low),
                pltpu.VMEM((length, size), f32),
                pltpu.VMEM((length, size), f32),
            ],
        ),
        out_shape=[out, out, out],
        cost_estimate=pl.CostEstimate(
            flops=10 * heads * length * length * size,
            bytes_accessed=heads * length * size * 20,
            transcendentals=heads * length * length,
        ),
        compiler_params=pltpu.CompilerParams(vmem_limit_bytes=32 * 1024 * 1024),
        name="attend_backward",
    )(place, projected, projected, projected, grad, mixed, log_total)


def local(
    block_input,
    first_gain,
    first_shift,
    query_key_value_weight,
    query_bias,
    value_bias,
    attention_output_weight,
    attention_output_bias,
    second_gain,
    second_shift,
    up_weight,
    up_bias,
    down_weight,
    down_bias,
    cotangent,
):
    shards = lax.axis_size("shard")
    index = lax.axis_index("shard")
    seqs, span, width = block_input.shape
    size = width // HEADS
    own = width // shards
    hidden = up_bias.shape[0]
    starts = [d * own // size for d in range(shards)]
    heads = max(-(-(d + 1) * own // size) - starts[d] for d in range(shards))
    window = heads * size
    pad = window - own
    start = index * own // size
    skew = index * own - start * size
    order = relative_order()
    inverse_order = jnp.asarray([order.index(o) for o in range(shards)], jnp.int32)
    place = inverse_order[jnp.arange(shards, dtype=jnp.int32) ^ index]

    own_input = block_input.reshape(seqs * span, width)
    inputs_all = gather_relative(own_input)
    vectors = gather_absolute(
        jnp.stack(
            [
                first_gain,
                first_shift,
                query_bias,
                value_bias,
                attention_output_bias,
                second_gain,
                second_shift,
                down_bias,
            ]
        )
    )
    vectors = vectors.transpose(1, 0, 2).reshape(8, width)
    gain_one, shift_one, bias_query, bias_value, bias_out, gain_two, shift_two, bias_down = (
        vectors[i] for i in range(8)
    )
    weight_in = exchange(
        jnp.stack(
            [
                jnp.concatenate(
                    [
                        query_key_value_weight[
                            :, part * width + s * size : part * width + s * size + window
                        ]
                        for part in range(3)
                    ],
                    axis=1,
                )
                for s in starts
            ]
        )
    ).reshape(width, 3 * window)
    up_blocks = jnp.stack([up_weight[:, s * hidden : (s + 1) * hidden] for s in range(shards)])
    up_blocks, weight_in = after(up_blocks, weight_in)
    up_pieces = send_halves(up_blocks)
    to_right = [(i, i + 1) for i in range(shards - 1)]
    to_left = [(i + 1, i) for i in range(shards - 1)]
    edges = (
        lax.ppermute(attention_output_weight[own - pad :], "shard", to_right),
        lax.ppermute(attention_output_weight[:pad], "shard", to_left),
    )
    own_branch, up_pieces = after(cotangent.reshape(seqs * span, width).astype(low), up_pieces)
    branch = gather_relative(own_branch)
    grad_out = cotangent.reshape(seqs * span, width)

    def own_rows(values):
        return lax.dynamic_slice_in_dim(values, skew, own, 0)

    rows = shards * seqs * span
    normed_all, _ = normalize(inputs_all.astype(f32))
    hidden_one = (normed_all * gain_one + shift_one).astype(low)
    bias_window = jnp.concatenate(
        [
            lax.dynamic_slice_in_dim(bias_query, start * size, window, 0),
            jnp.zeros((window,), low),
            lax.dynamic_slice_in_dim(bias_value, start * size, window, 0),
        ]
    ).astype(f32)
    projected = (contract(weight_in, hidden_one, 0, 1) + bias_window[:, None]).astype(low)

    def per_sequence(values):
        lead = values.shape[:-1]
        split = values.reshape(lead + (shards, seqs, span))
        return [split[..., :, s, :].reshape(lead + (shards * span,)) for s in range(seqs)]

    def join_sequences(parts):
        if seqs == 1:
            return parts[0]
        lead = parts[0].shape[:-1]
        joined = jnp.stack([p.reshape(lead + (shards, span)) for p in parts], axis=-2)
        return joined.reshape(lead + (rows,))

    projected_parts = per_sequence(projected) if seqs > 1 else [projected]
    forward_parts = [attend_forward(place, p, heads, span) for p in projected_parts]
    attended = join_sequences([p[1] for p in forward_parts])
    attended, up_pieces, edges = lax.optimization_barrier((attended, up_pieces, edges))
    weight_out_window = lax.dynamic_slice_in_dim(
        jnp.concatenate([edges[0], attention_output_weight, edges[1]], axis=0),
        pad - skew,
        window,
        0,
    )
    attended = own_rows(attended)
    weight_up = join_halves(up_pieces).reshape(width, hidden)
    mixed_sum = scatter_relative(
        contract(attended, attention_output_weight, 0, 0)
    )
    layer_input = own_input.astype(f32)
    middle = layer_input + mixed_sum + bias_out

    normed_two, inverse_two = normalize(middle)
    hidden_two = gather_relative((normed_two * gain_two + shift_two).astype(low))
    before = contract(hidden_two, weight_up, 1, 0) + up_bias
    activated, slope = gelu_parts(before)
    activated = activated.astype(low)
    down_weight_grad = contract(activated, branch, 0, 0).astype(low)[None]
    near, far = rep_bits(False), rep_bits(True)
    down_chain = Chain(plain_sum(down_weight_grad, near))
    late_branch, down_chain.holds = after(branch, down_chain.holds)
    grad_before = (contract(late_branch, down_weight, 1, 1) * slope).astype(low)
    hidden_two_sum = contract(grad_before, weight_up, 1, 1)
    hidden_two_sum, late_before, late_active = lax.optimization_barrier(
        (hidden_two_sum, grad_before, activated)
    )
    grad_hidden_two = scatter_relative(hidden_two_sum)
    up_weight_grad = contract(hidden_two, late_before, 0, 0).astype(low)
    up_weight_grad = up_weight_grad.reshape(shards, own, hidden)
    down_sum = contract(late_active, down_weight, 1, 0)
    grad_middle = grad_out + norm_back(grad_hidden_two, normed_two, inverse_two, gain_two)
    up_chain = Chain(turned_sum(up_weight_grad, near))
    down_chain.advance(up_chain)
    late_middle = down_chain.advance(down_chain, grad_middle)

    grad_mixed = gather_relative(grad_middle.astype(low))
    late_mixed = up_chain.advance(down_chain, grad_mixed)
    down_chain.advance(up_chain)
    grad_attended = contract(weight_out_window, grad_mixed, 1, 1).astype(low)
    grad_attended, (down_chain.holds, up_chain.holds) = after(
        grad_attended, (down_chain.holds, up_chain.holds)
    )
    grad_parts = per_sequence(grad_attended) if seqs > 1 else [grad_attended]
    backward_parts = [
        attend_backward(place, p, g, f[0], f[2], heads, span)
        for p, g, f in zip(projected_parts, grad_parts, forward_parts)
    ]
    grad_query, grad_key, grad_value = (
        join_sequences([p[i] for p in backward_parts]) for i in range(3)
    )
    own_query, own_key, own_value = (own_rows(g) for g in (grad_query, grad_key, grad_value))
    own_projected = jnp.concatenate([own_query, own_key, own_value], axis=0)
    line = jnp.arange(window)
    mine = ((line >= skew) & (line < skew + own))[:, None]
    grad_projected = jnp.concatenate(
        [jnp.where(mine, g, jnp.zeros_like(g)) for g in (grad_query, grad_key, grad_value)], axis=0
    )
    output_weight_grad = contract(attended, grad_mixed, 1, 0).astype(low)
    down_sum, late_mixed = after(down_sum, late_mixed)
    block_chain = Chain(shard_sum(down_sum))
    late_query = up_chain.advance(down_chain, own_query)
    down_chain.advance(up_chain)

    def by_owner(gradient):
        return gradient.reshape(shards, own, gradient.shape[1])

    first_part = by_owner(contract(hidden_one, own_projected[: 2 * own], 0, 1).astype(low))
    second_part = by_owner(contract(hidden_one, own_value, 0, 1).astype(low))
    output_blocks = jnp.stack(
        [output_weight_grad[:, s * own : (s + 1) * own] for s in range(shards)]
    )
    second_part = jnp.concatenate([second_part, output_blocks], axis=2)
    mixer_chain = Chain(mixer_sum(first_part, second_part, [near, far], own))
    hidden_chain = Chain(shard_sum(contract(grad_projected, weight_in, 0, 1)))
    chain = down_chain
    for step in (
        [block_chain, hidden_chain, up_chain, down_chain, up_chain, mixer_chain, hidden_chain]
        + [block_chain, hidden_chain] * shards
    ):
        step.advance(chain)
        chain = step
    block_output = middle + block_chain.holds + bias_down
    grad_hidden_one = hidden_chain.holds
    normed_one, inverse_one = normalize(layer_input)
    input_grad = late_middle + norm_back(grad_hidden_one, normed_one, inverse_one, gain_one)

    def own_part(values):
        return lax.dynamic_slice_in_dim(values, index * own, own, 0)

    partial = jnp.stack(
        [
            jnp.sum(grad_hidden_one * normed_one, axis=0),
            jnp.sum(grad_hidden_one, axis=0),
            jnp.sum(grad_hidden_two * normed_two, axis=0),
            jnp.sum(grad_hidden_two, axis=0),
        ]
    )
    vector_chain = Chain(
        vector_sum(
            partial,
            [
                jnp.sum(late_query.astype(f32), axis=1),
                jnp.sum(own_value.astype(f32), axis=1),
                own_part(jnp.sum(late_mixed.astype(f32), axis=0)),
                own_part(jnp.sum(branch.astype(f32), axis=0)),
                jnp.sum(grad_before.astype(f32), axis=0),
            ],
            own_part,
        )
    )
    down, up, mixer, vector = chains = [down_chain, up_chain, mixer_chain, vector_chain]
    chain = up
    for step in (
        [vector, vector, up, mixer, vector, vector, vector, mixer]
        + [down, up, mixer, mixer, up, mixer]
        + chains * 8
    ):
        if step.waits is not None:
            step.advance(chain)
            chain = step
    complete = vector_chain.holds
    down_weight_grad = down_chain.holds[0]
    up_weight_grad = up_chain.holds
    first_part, second_part = mixer_chain.holds
    input_weight_grad = jnp.concatenate([first_part, second_part[:, :width]], axis=1)
    output_weight_grad = second_part[:, width:]
    (
        first_gain_grad,
        first_shift_grad,
        second_gain_grad,
        second_shift_grad,
        query_bias_grad,
        value_bias_grad,
        output_bias_grad,
        down_bias_grad,
    ) = (complete[i * own : (i + 1) * own] for i in range(8))
    up_bias_grad = complete[8 * own :]
    return (
        block_output.reshape(seqs, span, width),
        input_grad.reshape(seqs, span, width),
        first_gain_grad,
        first_shift_grad,
        input_weight_grad.astype(f32),
        query_bias_grad,
        value_bias_grad,
        output_weight_grad.astype(f32),
        output_bias_grad,
        second_gain_grad,
        second_shift_grad,
        up_weight_grad.astype(f32),
        up_bias_grad,
        down_weight_grad.astype(f32),
        down_bias_grad,
    )


def solution(mesh):
    matrix, vector, tokens = P("shard", None), P("shard"), P("rep", "shard", None)
    return jax.shard_map(
        local,
        mesh=mesh,
        in_specs=(
            tokens,
            vector,
            vector,
            matrix,
            vector,
            vector,
            matrix,
            vector,
            vector,
            vector,
            matrix,
            vector,
            matrix,
            vector,
            tokens,
        ),
        out_specs=(
            tokens,
            tokens,
            vector,
            vector,
            matrix,
            vector,
            vector,
            matrix,
            vector,
            vector,
            vector,
            matrix,
            vector,
            matrix,
            vector,
        ),
        check_vma=False,
    )
```

```python
import functools

import jax
import jax.numpy as jnp
from jax import lax
from jax.experimental import pallas as pl
from jax.experimental.pallas import tpu as pltpu
from jax.sharding import PartitionSpec as P

HEADS = 17

epsilon = 1e-05
score_scale = 0.125
low = jnp.bfloat16
f32 = jnp.float32


def normalize(values):
    centre = jnp.mean(values, axis=-1, keepdims=True)
    centred = values - centre
    inverse = lax.rsqrt(jnp.mean(centred * centred, axis=-1, keepdims=True) + epsilon)
    return (centred * inverse, inverse)


def norm_back(grad, normed, inverse, gain):
    scaled = grad * gain
    first = jnp.mean(scaled, axis=-1, keepdims=True)
    second = jnp.mean(scaled * normed, axis=-1, keepdims=True)
    return inverse * (scaled - first - normed * second)


def gelu_parts(values):
    cumulative = 0.5 * (1.0 + lax.erf(values * 0.7071067811865476))
    density = jnp.exp(-0.5 * values * values) * 0.3989422804014327
    return values * cumulative, cumulative + values * density


def contract(left, right, left_dim, right_dim):
    return lax.dot_general(
        left, right, (((left_dim,), (right_dim,)), ((), ())), preferred_element_type=f32
    )


def swap(values, bit):
    size = lax.axis_size("shard")
    return lax.ppermute(values, "shard", [(i, i ^ bit) for i in range(size)])


def bits_far_first():
    bit = lax.axis_size("shard") // 2
    bits = []
    while bit:
        bits.append(bit)
        bit //= 2
    return bits


def relative_order():
    order = [0]
    for bit in bits_far_first():
        order = order + [o ^ bit for o in order]
    return order


def gather_relative(block, steps=slice(None)):
    for bit in bits_far_first()[steps]:
        block = jnp.concatenate([block, swap(block, bit)], axis=0)
    return block


def gather_absolute(block):
    index = lax.axis_index("shard")
    stack = block[None]
    for bit in bits_far_first():
        other = swap(stack, bit)
        upper = (index & bit) != 0
        pair = jnp.stack(
            [jnp.where(upper, other, stack), jnp.where(upper, stack, other)], axis=1
        )
        stack = pair.reshape((2 * stack.shape[0],) + block.shape)
    return stack


def scatter_relative(parts):
    for bit in reversed(bits_far_first()):
        half = parts.shape[0] // 2
        other = swap(parts[half:].astype(low), bit)
        parts = parts[:half] + other.astype(f32)
    return parts


def swap_rep(values, bit):
    size = lax.axis_size("rep")
    return lax.ppermute(values, "rep", [(i, i ^ bit) for i in range(size)])


def rep_bits(turned):
    bits, bit = [], 1
    while bit < lax.axis_size("rep"):
        bits.append(bit)
        bit *= 2
    return bits[1:2] + bits[:1] + bits[2:] if turned else bits


def after(values, gate):
    return lax.optimization_barrier((values, gate))


def half_window(rows):
    return min(rows, (rows + 15) // 16 * 8)


def half_of(values, index):
    rows = values.shape[1]
    window = half_window(rows)
    return lax.dynamic_slice_in_dim(values, index * (rows - window), window, 1)


def sent_half(values, bit):
    return swap_rep(half_of(values, 1 - (lax.axis_index("rep") // bit) % 2), bit)


def kept_half(values, bit):
    return half_of(values, (lax.axis_index("rep") // bit) % 2)


def add(keep, other):
    return (keep.astype(f32) + other.astype(f32)).astype(low)


def join(values, other, bit, rows):
    window = values.shape[1]
    upper = (lax.axis_index("rep") // bit) % 2 != 0
    first = jnp.where(upper, other, values)
    second = jnp.where(upper, values, other)
    return jnp.concatenate([first, second[:, 2 * window - rows :]], axis=1)


class Chain:
    def __init__(self, steps):
        self.steps = steps
        self.take(None)

    def take(self, got):
        try:
            self.waits, self.holds = self.steps.send(got)
        except StopIteration as end:
            self.waits, self.holds = None, end.value

    def advance(self, previous, gate=()):
        if self.waits is not None:
            if previous is self:
                waits, gate = after(self.waits, gate)
            else:
                waits, (previous.holds, gate) = after(self.waits, (previous.holds, gate))
            self.take((waits, self.holds))
        return gate


def scatter_steps(lanes, orders):
    sizes = []
    for step in range(len(orders[0])):
        sizes.append(lanes[0].shape[1])
        others, held = yield (
            tuple(sent_half(v, order[step]) for v, order in zip(lanes, orders)),
            tuple(lanes),
        )
        lanes = [
            add(kept_half(v, order[step]), other) for v, other, order in zip(held, others, orders)
        ]
    return list(lax.optimization_barrier(tuple(lanes))), sizes


def gather_steps(lanes, orders, sizes):
    for step in reversed(range(len(orders[0]))):
        others, lanes = yield (
            tuple(swap_rep(v, order[step]) for v, order in zip(lanes, orders)),
            tuple(lanes),
        )
        lanes = [
            join(v, other, order[step], sizes[step])
            for v, other, order in zip(lanes, others, orders)
        ]
    return lanes


def exchange_steps(blocks):
    size = lax.axis_size("shard")
    index = lax.axis_index("shard")
    pieces = [lax.dynamic_index_in_dim(blocks, index ^ o, 0, keepdims=True) for o in range(size)]
    others, first = yield tuple(swap(pieces[o], o) for o in range(1, size)), pieces[0]
    result = jnp.zeros_like(blocks)
    for o, piece in enumerate((first,) + tuple(others)):
        result = lax.dynamic_update_slice_in_dim(result, piece, index ^ o, 0)
    return [result[i] for i in range(size)]


def plain_sum(values, order):
    lanes, sizes = yield from scatter_steps([values], [order])
    lanes = yield from gather_steps(lanes, [order], sizes)
    return lanes[0]


def turned_sum(values, order):
    lanes, sizes = yield from scatter_steps([values], [order])
    blocks = yield from exchange_steps(lanes[0])
    lanes = yield from gather_steps([jnp.concatenate(blocks, axis=1)[None]], [order], sizes)
    return lanes[0][0]


def mixer_sum(first, second, orders, own):
    lanes, sizes = yield from scatter_steps([first, second], orders)
    blocks = yield from exchange_steps(
        jnp.concatenate([lanes[0], lanes[1][:, :, :own]], axis=2)
    )
    parts = [
        jnp.concatenate([b[:, i * own : (i + 1) * own] for b in blocks], axis=1) for i in range(3)
    ]
    output = jnp.concatenate([lanes[1][i, :, own:] for i in range(len(blocks))], axis=1)
    lanes = [
        jnp.concatenate(parts[:2], axis=1)[None],
        jnp.concatenate([parts[2], output], axis=1)[None],
    ]
    lanes = yield from gather_steps(lanes, orders, sizes)
    return lanes[0][0], lanes[1][0]


def shard_sum(parts):
    for bit in reversed(bits_far_first()):
        half = parts.shape[0] // 2
        (other,), kept = yield (swap(parts[half:].astype(low), bit),), parts[:half]
        parts = kept + other.astype(f32)
    return parts


def vector_sum(partial, complete, own_part):
    for bit in bits_far_first():
        (other,), partial = yield (swap(partial, bit),), partial
        partial = partial + other
    total = jnp.concatenate([own_part(p) for p in partial] + complete)
    for bit in rep_bits(False):
        (other,), total = yield (swap_rep(total, bit),), total
        total = total + other
    return total


def exchange(blocks):
    size = lax.axis_size("shard")
    index = lax.axis_index("shard")
    result = jnp.zeros_like(blocks)
    for offset in range(size):
        peer = index ^ offset
        piece = lax.dynamic_index_in_dim(blocks, peer, 0, keepdims=True)
        if offset:
            piece = swap(piece, offset)
        result = lax.dynamic_update_slice_in_dim(result, piece, peer, 0)
    return result


def is_neighbour_offset(offset):
    return offset & (offset + 1) == 0


def send_halves(blocks, first, last):
    index = lax.axis_index("shard")
    size = lax.axis_size("shard")
    half = blocks.shape[1] // 2
    part = (lax.axis_index("rep") % 2) * half
    pieces = []
    for offset in range(size):
        piece = lax.dynamic_index_in_dim(blocks, index ^ offset, 0, keepdims=True)
        if offset >= 2:
            piece = lax.dynamic_slice_in_dim(piece, part, half, 1)
        if offset:
            if is_neighbour_offset(offset):
                edge = jnp.where((index ^ offset) == index + 1, last, first)
                edge = edge.reshape(1, -1, piece.shape[2])
                piece = jnp.concatenate([piece, edge], axis=1)
            piece = swap(piece, offset)
        pieces.append(piece)
    return pieces


def take_edges(pieces, shape):
    index = lax.axis_index("shard")
    before = behind = None
    rest = pieces[:1]
    count = shape[0] * shape[1] // pieces[0].shape[2]
    for offset in range(1, len(pieces)):
        piece = pieces[offset]
        if is_neighbour_offset(offset):
            edge = piece[0, piece.shape[1] - count :].reshape(shape)
            piece = piece[:, : piece.shape[1] - count]
            if before is None:
                before = behind = edge
            before = jnp.where((index ^ offset) == index - 1, edge, before)
            behind = jnp.where((index ^ offset) == index + 1, edge, behind)
        rest.append(piece)
    return before, behind, rest


def join_halves(pieces):
    index = lax.axis_index("shard")
    upper = lax.axis_index("rep") % 2 != 0
    full = pieces[0].shape[1]
    count = len(pieces)
    if count > 2:
        mine = jnp.concatenate(pieces[2:], axis=0)
        other = swap_rep(mine, 1)
        halves = jnp.concatenate(
            [jnp.where(upper, other, mine), jnp.where(upper, mine, other)], axis=1
        )
        pieces = pieces[:2] + [halves[i : i + 1] for i in range(count - 2)]
    result = jnp.zeros((count,) + pieces[0].shape[1:], pieces[0].dtype)
    for offset, piece in enumerate(pieces):
        result = lax.dynamic_update_slice_in_dim(result, piece, index ^ offset, 0)
    return result


def visible_part(scores, top, block, fill):
    rows = lax.broadcasted_iota(jnp.int32, (block, block), 0)
    cols = lax.broadcasted_iota(jnp.int32, (block, block), 1)
    last = jnp.where(rows <= cols, scores[top:], fill)
    if top == 0:
        return last
    return jnp.concatenate([scores[:top], last], axis=0)


def turn(values):
    return values.astype(f32).T


def forward_kernel(blocks, block, place, q_ref, k_ref, v_ref, o_ref, low_ref, log_ref, k_rows, v_cols):
    for i in range(blocks):
        here = pl.ds(pl.multiple_of(place[i] * block, block), block)
        there = pl.ds(i * block, block)
        k_rows[there, :] = turn(k_ref[:, here]).astype(low)
        v_cols[:, there] = v_ref[:, here]
    for i in range(blocks):
        here = pl.ds(pl.multiple_of(place[i] * block, block), block)
        top = i * block
        count = top + block
        q_cols = q_ref[:, here] * jnp.asarray(score_scale, low)
        scores = contract(k_rows[:count, :], q_cols, 1, 0)
        scores = visible_part(scores, top, block, -jnp.inf)
        peak = jnp.max(scores, axis=0, keepdims=True)
        weights = jnp.exp(scores - peak)
        total = jnp.sum(weights, axis=0, keepdims=True)
        mixed = contract(v_cols[:, :count], weights.astype(low), 1, 0) / total
        o_ref[:, here] = mixed
        low_ref[:, here] = mixed.astype(low)
        log_ref[0, :, here] = peak + jnp.log(total)


def backward_kernel(
    blocks,
    block,
    place,
    q_ref,
    k_ref,
    v_ref,
    g_ref,
    o_ref,
    log_ref,
    dq_ref,
    dk_ref,
    dv_ref,
    k_rows,
    v_rows,
    k_cols,
    dk_rows,
    dv_rows,
):
    for i in range(blocks):
        here = pl.ds(pl.multiple_of(place[i] * block, block), block)
        there = pl.ds(i * block, block)
        k_rows[there, :] = turn(k_ref[:, here]).astype(low)
        v_rows[there, :] = turn(v_ref[:, here]).astype(low)
        k_cols[:, there] = k_ref[:, here]
    for i in reversed(range(blocks)):
        here = pl.ds(pl.multiple_of(place[i] * block, block), block)
        top = i * block
        count = top + block
        q_cols = q_ref[:, here] * jnp.asarray(score_scale, low)
        g_cols = g_ref[:, here]
        q_rows = turn(q_cols).astype(low)
        g_rows = turn(g_cols).astype(low)
        correction = jnp.sum(g_cols.astype(f32) * o_ref[:, here], axis=0, keepdims=True)
        scores = contract(k_rows[:count, :], q_cols, 1, 0)
        probs = jnp.exp(scores - log_ref[0, :, here])
        probs = visible_part(probs, top, block, 0.0)
        grad_probs = contract(v_rows[:count, :], g_cols, 1, 0)
        grad_scores = (probs * (grad_probs - correction)).astype(low)
        dv_part = contract(probs.astype(low), g_rows, 1, 0)
        dk_part = contract(grad_scores, q_rows, 1, 0)
        if i == blocks - 1:
            dv_rows[:count, :] = dv_part
            dk_rows[:count, :] = dk_part
        else:
            dv_rows[:count, :] += dv_part
            dk_rows[:count, :] += dk_part
        dq = contract(k_cols[:, :count], grad_scores, 1, 0) * score_scale
        dq_ref[:, here] = dq.astype(low)
    for i in range(blocks):
        here = pl.ds(pl.multiple_of(place[i] * block, block), block)
        there = pl.ds(i * block, block)
        dk_ref[:, here] = dk_rows[there, :].T.astype(low)
        dv_ref[:, here] = dv_rows[there, :].T.astype(low)


def head_spec(size, length, first):
    return pl.BlockSpec((size, length), lambda h, place: (first + h, 0))


def attend_forward(place, projected, heads, block):
    size = projected.shape[0] // (3 * heads)
    length = projected.shape[1]
    blocks = length // block
    row = pl.BlockSpec((1, 1, length), lambda h, place: (h, 0, 0))
    return pl.pallas_call(
        functools.partial(forward_kernel, blocks, block),
        grid_spec=pltpu.PrefetchScalarGridSpec(
            num_scalar_prefetch=1,
            grid=(heads,),
            in_specs=[
                head_spec(size, length, 0),
                head_spec(size, length, heads),
                head_spec(size, length, 2 * heads),
            ],
            out_specs=[head_spec(size, length, 0), head_spec(size, length, 0), row],
            scratch_shapes=[
                pltpu.VMEM((length, size), low),
                pltpu.VMEM((size, length), low),
            ],
        ),
        out_shape=[
            jax.ShapeDtypeStruct((heads * size, length), f32),
            jax.ShapeDtypeStruct((heads * size, length), low),
            jax.ShapeDtypeStruct((heads, 1, length), f32),
        ],
        cost_estimate=pl.CostEstimate(
            flops=4 * heads * length * length * size,
            bytes_accessed=heads * length * size * 12,
            transcendentals=heads * length * length,
        ),
        compiler_params=pltpu.CompilerParams(vmem_limit_bytes=32 * 1024 * 1024),
        name="attend_forward",
    )(place, projected, projected, projected)


def attend_backward(place, projected, grad, mixed, log_total, heads, block):
    size = projected.shape[0] // (3 * heads)
    length = projected.shape[1]
    blocks = length // block
    row = pl.BlockSpec((1, 1, length), lambda h, place: (h, 0, 0))
    out = jax.ShapeDtypeStruct((heads * size, length), low)
    return pl.pallas_call(
        functools.partial(backward_kernel, blocks, block),
        grid_spec=pltpu.PrefetchScalarGridSpec(
            num_scalar_prefetch=1,
            grid=(heads,),
            in_specs=[
                head_spec(size, length, 0),
                head_spec(size, length, heads),
                head_spec(size, length, 2 * heads),
                head_spec(size, length, 0),
                head_spec(size, length, 0),
                row,
            ],
            out_specs=[head_spec(size, length, 0)] * 3,
            scratch_shapes=[
                pltpu.VMEM((length, size), low),
                pltpu.VMEM((length, size), low),
                pltpu.VMEM((size, length), low),
                pltpu.VMEM((length, size), f32),
                pltpu.VMEM((length, size), f32),
            ],
        ),
        out_shape=[out, out, out],
        cost_estimate=pl.CostEstimate(
            flops=10 * heads * length * length * size,
            bytes_accessed=heads * length * size * 20,
            transcendentals=heads * length * length,
        ),
        compiler_params=pltpu.CompilerParams(vmem_limit_bytes=32 * 1024 * 1024),
        name="attend_backward",
    )(place, projected, projected, projected, grad, mixed, log_total)


def local(
    block_input,
    first_gain,
    first_shift,
    query_key_value_weight,
    query_bias,
    value_bias,
    attention_output_weight,
    attention_output_bias,
    second_gain,
    second_shift,
    up_weight,
    up_bias,
    down_weight,
    down_bias,
    cotangent,
):
    shards = lax.axis_size("shard")
    index = lax.axis_index("shard")
    seqs, span, width = block_input.shape
    size = width // HEADS
    own = width // shards
    hidden = up_bias.shape[0]
    starts = [d * own // size for d in range(shards)]
    heads = max(-(-(d + 1) * own // size) - starts[d] for d in range(shards))
    window = heads * size
    pad = window - own
    start = index * own // size
    skew = index * own - start * size
    order = relative_order()
    inverse_order = jnp.asarray([order.index(o) for o in range(shards)], jnp.int32)
    place = inverse_order[jnp.arange(shards, dtype=jnp.int32) ^ index]

    own_input = block_input.reshape(seqs * span, width)
    inputs_all = gather_relative(own_input)
    vectors = gather_absolute(
        jnp.stack(
            [
                first_gain,
                first_shift,
                query_bias,
                value_bias,
                attention_output_bias,
                second_gain,
                second_shift,
                down_bias,
            ]
        )
    )
    vectors = vectors.transpose(1, 0, 2).reshape(8, width)
    gain_one, shift_one, bias_query, bias_value, bias_out, gain_two, shift_two, bias_down = (
        vectors[i] for i in range(8)
    )
    weight_in = exchange(
        jnp.stack(
            [
                jnp.concatenate(
                    [
                        query_key_value_weight[
                            :, part * width + s * size : part * width + s * size + window
                        ]
                        for part in range(3)
                    ],
                    axis=1,
                )
                for s in starts
            ]
        )
    ).reshape(width, 3 * window)
    up_blocks = jnp.stack([up_weight[:, s * hidden : (s + 1) * hidden] for s in range(shards)])
    own_branch = cotangent.reshape(seqs * span, width).astype(low)
    (up_blocks, own_branch), weight_in = after((up_blocks, own_branch), weight_in)
    up_pieces = send_halves(
        up_blocks, attention_output_weight[:pad], attention_output_weight[own - pad :]
    )
    far_branch = swap(own_branch, bits_far_first()[0])
    grad_out = cotangent.reshape(seqs * span, width)

    def own_rows(values):
        return lax.dynamic_slice_in_dim(values, skew, own, 0)

    rows = shards * seqs * span
    normed_all, _ = normalize(inputs_all.astype(f32))
    hidden_one = (normed_all * gain_one + shift_one).astype(low)
    bias_window = jnp.concatenate(
        [
            lax.dynamic_slice_in_dim(bias_query, start * size, window, 0),
            jnp.zeros((window,), low),
            lax.dynamic_slice_in_dim(bias_value, start * size, window, 0),
        ]
    ).astype(f32)
    projected = (contract(weight_in, hidden_one, 0, 1) + bias_window[:, None]).astype(low)

    def per_sequence(values):
        lead = values.shape[:-1]
        split = values.reshape(lead + (shards, seqs, span))
        return [split[..., :, s, :].reshape(lead + (shards * span,)) for s in range(seqs)]

    def join_sequences(parts):
        if seqs == 1:
            return parts[0]
        lead = parts[0].shape[:-1]
        joined = jnp.stack([p.reshape(lead + (shards, span)) for p in parts], axis=-2)
        return joined.reshape(lead + (rows,))

    projected_parts = per_sequence(projected) if seqs > 1 else [projected]
    forward_parts = [attend_forward(place, p, heads, span) for p in projected_parts]
    attended = join_sequences([p[1] for p in forward_parts])
    attended, (up_pieces, far_branch) = after(attended, (up_pieces, far_branch))
    branch = gather_relative(jnp.concatenate([own_branch, far_branch], axis=0), slice(1, None))
    before_rows, behind_rows, up_pieces = take_edges(up_pieces, (pad, width))
    weight_out_window = lax.dynamic_slice_in_dim(
        jnp.concatenate([before_rows, attention_output_weight, behind_rows], axis=0),
        pad - skew,
        window,
        0,
    )
    attended = own_rows(attended)
    weight_up = join_halves(up_pieces).reshape(width, hidden)
    mixed_sum = scatter_relative(
        contract(attended, attention_output_weight, 0, 0)
    )
    layer_input = own_input.astype(f32)
    middle = layer_input + mixed_sum + bias_out

    normed_two, inverse_two = normalize(middle)
    hidden_two = gather_relative((normed_two * gain_two + shift_two).astype(low))
    before = contract(hidden_two, weight_up, 1, 0) + up_bias
    activated, slope = gelu_parts(before)
    activated = activated.astype(low)
    grad_before = (contract(branch, down_weight, 1, 1) * slope).astype(low)
    hidden_two_sum = contract(grad_before, weight_up, 1, 1)
    hidden_two_sum, late_before, late_active = lax.optimization_barrier(
        (hidden_two_sum, grad_before, activated)
    )
    hidden_chain = Chain(shard_sum(hidden_two_sum))
    late_before = hidden_chain.advance(hidden_chain, late_before)
    while hidden_chain.waits is not None:
        hidden_chain.advance(hidden_chain)
    grad_hidden_two = hidden_chain.holds
    near, far = rep_bits(False), rep_bits(True)
    down_weight_grad = contract(late_active, branch, 0, 0).astype(low)[None]
    down_chain = Chain(plain_sum(down_weight_grad, near))
    up_weight_grad = contract(hidden_two, late_before, 0, 0).astype(low)
    up_weight_grad = up_weight_grad.reshape(shards, own, hidden)
    down_sum = contract(late_active, down_weight, 1, 0)
    grad_middle = grad_out + norm_back(grad_hidden_two, normed_two, inverse_two, gain_two)
    up_chain = Chain(turned_sum(up_weight_grad, far))
    late_middle = down_chain.advance(up_chain, grad_middle)

    grad_mixed = gather_relative(grad_middle.astype(low))
    up_chain.advance(down_chain)
    block_chain = Chain(shard_sum(down_sum))
    late_mixed = block_chain.advance(up_chain, grad_mixed)
    grad_attended = contract(weight_out_window, grad_mixed, 1, 1).astype(low)
    grad_attended, (down_chain.holds, up_chain.holds, block_chain.holds) = after(
        grad_attended, (down_chain.holds, up_chain.holds, block_chain.holds)
    )
    grad_parts = per_sequence(grad_attended) if seqs > 1 else [grad_attended]
    backward_parts = [
        attend_backward(place, p, g, f[0], f[2], heads, span)
        for p, g, f in zip(projected_parts, grad_parts, forward_parts)
    ]
    grad_query, grad_key, grad_value = (
        join_sequences([p[i] for p in backward_parts]) for i in range(3)
    )
    own_query, own_key, own_value = (own_rows(g) for g in (grad_query, grad_key, grad_value))
    own_projected = jnp.concatenate([own_query, own_key, own_value], axis=0)
    line = jnp.arange(window)
    mine = ((line >= skew) & (line < skew + own))[:, None]
    grad_projected = jnp.concatenate(
        [jnp.where(mine, g, jnp.zeros_like(g)) for g in (grad_query, grad_key, grad_value)], axis=0
    )
    output_weight_grad = contract(attended, grad_mixed, 1, 0).astype(low)
    late_query = block_chain.advance(up_chain, own_query)
    down_chain.advance(block_chain)
    up_chain.advance(down_chain)

    def by_owner(gradient):
        return gradient.reshape(shards, own, gradient.shape[1])

    first_part = by_owner(contract(hidden_one, own_projected[: 2 * own], 0, 1).astype(low))
    second_part = by_owner(contract(hidden_one, own_value, 0, 1).astype(low))
    output_blocks = jnp.stack(
        [output_weight_grad[:, s * own : (s + 1) * own] for s in range(shards)]
    )
    second_part = jnp.concatenate([second_part, output_blocks], axis=2)
    mixer_chain = Chain(mixer_sum(first_part, second_part, [near, far], own))
    hidden_chain = Chain(shard_sum(contract(grad_projected, weight_in, 0, 1)))
    chain = up_chain
    for step in (
        [hidden_chain, down_chain, mixer_chain, up_chain, hidden_chain]
        + [block_chain, hidden_chain] * shards
    ):
        step.advance(chain)
        chain = step
    block_output = middle + block_chain.holds + bias_down
    grad_hidden_one = hidden_chain.holds
    normed_one, inverse_one = normalize(layer_input)
    input_grad = late_middle + norm_back(grad_hidden_one, normed_one, inverse_one, gain_one)

    def own_part(values):
        return lax.dynamic_slice_in_dim(values, index * own, own, 0)

    partial = jnp.stack(
        [
            jnp.sum(grad_hidden_one * normed_one, axis=0),
            jnp.sum(grad_hidden_one, axis=0),
            jnp.sum(grad_hidden_two * normed_two, axis=0),
            jnp.sum(grad_hidden_two, axis=0),
        ]
    )
    vector_chain = Chain(
        vector_sum(
            partial,
            [
                jnp.sum(late_query.astype(f32), axis=1),
                jnp.sum(own_value.astype(f32), axis=1),
                own_part(jnp.sum(late_mixed.astype(f32), axis=0)),
                own_part(jnp.sum(branch.astype(f32), axis=0)),
                jnp.sum(grad_before.astype(f32), axis=0),
            ],
            own_part,
        )
    )
    down, up, mixer, vector = chains = [down_chain, up_chain, mixer_chain, vector_chain]
    chain = hidden_chain
    for step in (
        [up, vector, vector, vector, mixer, down, vector, vector, up]
        + [mixer, down, mixer, up, mixer, mixer, down, up, mixer]
        + chains * 8
    ):
        if step.waits is not None:
            step.advance(chain)
            chain = step
    complete = vector_chain.holds
    down_weight_grad = down_chain.holds[0]
    up_weight_grad = up_chain.holds
    first_part, second_part = mixer_chain.holds
    input_weight_grad = jnp.concatenate([first_part, second_part[:, :width]], axis=1)
    output_weight_grad = second_part[:, width:]
    (
        first_gain_grad,
        first_shift_grad,
        second_gain_grad,
        second_shift_grad,
        query_bias_grad,
        value_bias_grad,
        output_bias_grad,
        down_bias_grad,
    ) = (complete[i * own : (i + 1) * own] for i in range(8))
    up_bias_grad = complete[8 * own :]
    return (
        block_output.reshape(seqs, span, width),
        input_grad.reshape(seqs, span, width),
        first_gain_grad,
        first_shift_grad,
        input_weight_grad.astype(f32),
        query_bias_grad,
        value_bias_grad,
        output_weight_grad.astype(f32),
        output_bias_grad,
        second_gain_grad,
        second_shift_grad,
        up_weight_grad.astype(f32),
        up_bias_grad,
        down_weight_grad.astype(f32),
        down_bias_grad,
    )


def solution(mesh):
    matrix, vector, tokens = P("shard", None), P("shard"), P("rep", "shard", None)
    return jax.shard_map(
        local,
        mesh=mesh,
        in_specs=(
            tokens,
            vector,
            vector,
            matrix,
            vector,
            vector,
            matrix,
            vector,
            vector,
            vector,
            matrix,
            vector,
            matrix,
            vector,
            tokens,
        ),
        out_specs=(
            tokens,
            tokens,
            vector,
            vector,
            matrix,
            vector,
            vector,
            matrix,
            vector,
            vector,
            vector,
            matrix,
            vector,
            matrix,
            vector,
        ),
        check_vma=False,
    )
```

```python
import functools

import jax
import jax.numpy as jnp
from jax import lax
from jax.experimental import pallas as pl
from jax.experimental.pallas import tpu as pltpu
from jax.sharding import PartitionSpec as P

HEADS = 17

epsilon = 1e-05
score_scale = 0.125
low = jnp.bfloat16
f32 = jnp.float32


def normalize(values):
    centre = jnp.mean(values, axis=-1, keepdims=True)
    centred = values - centre
    inverse = lax.rsqrt(jnp.mean(centred * centred, axis=-1, keepdims=True) + epsilon)
    return (centred * inverse, inverse)


def norm_back(grad, normed, inverse, gain):
    scaled = grad * gain
    first = jnp.mean(scaled, axis=-1, keepdims=True)
    second = jnp.mean(scaled * normed, axis=-1, keepdims=True)
    return inverse * (scaled - first - normed * second)


def gelu_parts(values):
    cumulative = 0.5 * (1.0 + lax.erf(values * 0.7071067811865476))
    density = jnp.exp(-0.5 * values * values) * 0.3989422804014327
    return values * cumulative, cumulative + values * density


def contract(left, right, left_dim, right_dim):
    return lax.dot_general(
        left, right, (((left_dim,), (right_dim,)), ((), ())), preferred_element_type=f32
    )


def swap(values, bit):
    size = lax.axis_size("shard")
    return lax.ppermute(values, "shard", [(i, i ^ bit) for i in range(size)])


def bits_far_first():
    bit = lax.axis_size("shard") // 2
    bits = []
    while bit:
        bits.append(bit)
        bit //= 2
    return bits


def relative_order():
    order = [0]
    for bit in bits_far_first():
        order = order + [o ^ bit for o in order]
    return order


def gather_relative(block, steps=slice(None)):
    for bit in bits_far_first()[steps]:
        block = jnp.concatenate([block, swap(block, bit)], axis=0)
    return block


def gather_absolute(block):
    index = lax.axis_index("shard")
    stack = block[None]
    for bit in bits_far_first():
        other = swap(stack, bit)
        upper = (index & bit) != 0
        pair = jnp.stack(
            [jnp.where(upper, other, stack), jnp.where(upper, stack, other)], axis=1
        )
        stack = pair.reshape((2 * stack.shape[0],) + block.shape)
    return stack


def scatter_relative(parts):
    for bit in reversed(bits_far_first()):
        half = parts.shape[0] // 2
        other = swap(parts[half:].astype(low), bit)
        parts = parts[:half] + other.astype(f32)
    return parts


def swap_rep(values, bit):
    size = lax.axis_size("rep")
    return lax.ppermute(values, "rep", [(i, i ^ bit) for i in range(size)])


def rep_bits(turned):
    bits, bit = [], 1
    while bit < lax.axis_size("rep"):
        bits.append(bit)
        bit *= 2
    return bits[1:2] + bits[:1] + bits[2:] if turned else bits


def after(values, gate):
    return lax.optimization_barrier((values, gate))


def half_window(rows):
    return min(rows, (rows + 15) // 16 * 8)


def half_of(values, index):
    rows = values.shape[1]
    window = half_window(rows)
    return lax.dynamic_slice_in_dim(values, index * (rows - window), window, 1)


def sent_half(values, bit):
    return swap_rep(half_of(values, 1 - (lax.axis_index("rep") // bit) % 2), bit)


def kept_half(values, bit):
    return half_of(values, (lax.axis_index("rep") // bit) % 2)


def add(keep, other):
    return (keep.astype(f32) + other.astype(f32)).astype(low)


def join(values, other, bit, rows):
    window = values.shape[1]
    upper = (lax.axis_index("rep") // bit) % 2 != 0
    first = jnp.where(upper, other, values)
    second = jnp.where(upper, values, other)
    return jnp.concatenate([first, second[:, 2 * window - rows :]], axis=1)


class Chain:
    def __init__(self, steps):
        self.steps = steps
        self.take(None)

    def take(self, got):
        try:
            self.waits, self.holds = self.steps.send(got)
        except StopIteration as end:
            self.waits, self.holds = None, end.value

    def advance(self, previous, gate=()):
        if self.waits is not None:
            if previous is self:
                waits, gate = after(self.waits, gate)
            else:
                waits, (previous.holds, gate) = after(self.waits, (previous.holds, gate))
            self.take((waits, self.holds))
        return gate


def scatter_steps(lanes, orders):
    sizes = []
    for step in range(len(orders[0])):
        sizes.append(lanes[0].shape[1])
        others, held = yield (
            tuple(sent_half(v, order[step]) for v, order in zip(lanes, orders)),
            tuple(lanes),
        )
        lanes = [
            add(kept_half(v, order[step]), other) for v, other, order in zip(held, others, orders)
        ]
    return list(lax.optimization_barrier(tuple(lanes))), sizes


def gather_steps(lanes, orders, sizes):
    for step in reversed(range(len(orders[0]))):
        others, lanes = yield (
            tuple(swap_rep(v, order[step]) for v, order in zip(lanes, orders)),
            tuple(lanes),
        )
        lanes = [
            join(v, other, order[step], sizes[step])
            for v, other, order in zip(lanes, others, orders)
        ]
    return lanes


def exchange_steps(blocks):
    size = lax.axis_size("shard")
    index = lax.axis_index("shard")
    pieces = [lax.dynamic_index_in_dim(blocks, index ^ o, 0, keepdims=True) for o in range(size)]
    others, first = yield tuple(swap(pieces[o], o) for o in range(1, size)), pieces[0]
    result = jnp.zeros_like(blocks)
    for o, piece in enumerate((first,) + tuple(others)):
        result = lax.dynamic_update_slice_in_dim(result, piece, index ^ o, 0)
    return result


def plain_sum(values, order):
    lanes, sizes = yield from scatter_steps([values], [order])
    lanes = yield from gather_steps(lanes, [order], sizes)
    return lanes[0]


def turned_sum(values, order):
    lanes, sizes = yield from scatter_steps([values], [order])
    blocks = yield from exchange_steps(lanes[0])
    columns = jnp.concatenate([blocks[i] for i in range(blocks.shape[0])], axis=1)
    lanes = yield from gather_steps([columns[None]], [order], sizes)
    return lanes[0][0]


def mixer_sum(first, second, orders, own):
    lanes, sizes = yield from scatter_steps([first, second], orders)
    blocks = yield from exchange_steps(
        jnp.concatenate([lanes[0], lanes[1][:, :, :own]], axis=2)
    )
    count = blocks.shape[0]
    parts = [
        jnp.concatenate([blocks[s, :, i * own : (i + 1) * own] for s in range(count)], axis=1)
        for i in range(3)
    ]
    output = jnp.concatenate([lanes[1][i, :, own:] for i in range(count)], axis=1)
    lanes = [
        jnp.concatenate(parts[:2], axis=1)[None],
        jnp.concatenate([parts[2], output], axis=1)[None],
    ]
    lanes = yield from gather_steps(lanes, orders, sizes)
    return lanes[0][0], lanes[1][0]


def shard_sum(parts):
    for bit in reversed(bits_far_first()):
        half = parts.shape[0] // 2
        (other,), kept = yield (swap(parts[half:].astype(low), bit),), parts[:half]
        parts = kept + other.astype(f32)
    return parts


def vector_sum(partial, complete, own_part):
    for bit in bits_far_first():
        (other,), partial = yield (swap(partial, bit),), partial
        partial = partial + other
    total = jnp.concatenate([own_part(p) for p in partial] + complete)
    for bit in rep_bits(False):
        (other,), total = yield (swap_rep(total, bit),), total
        total = total + other
    return total


def is_neighbour_offset(offset):
    return offset & (offset + 1) == 0


def send_halves(blocks, first, last):
    index = lax.axis_index("shard")
    size = lax.axis_size("shard")
    half = blocks.shape[1] // 2
    part = (lax.axis_index("rep") % 2) * half
    pieces = []
    for offset in range(size):
        piece = lax.dynamic_index_in_dim(blocks, index ^ offset, 0, keepdims=True)
        if offset >= 2:
            piece = lax.dynamic_slice_in_dim(piece, part, half, 1)
        if offset:
            if is_neighbour_offset(offset):
                edge = jnp.where((index ^ offset) == index + 1, last, first)
                edge = edge.reshape(1, -1, piece.shape[2])
                piece = jnp.concatenate([piece, edge], axis=1)
            piece = swap(piece, offset)
        pieces.append(piece)
    return pieces


def take_edges(pieces, shape):
    index = lax.axis_index("shard")
    before = behind = None
    rest = pieces[:1]
    count = shape[0] * shape[1] // pieces[0].shape[2]
    for offset in range(1, len(pieces)):
        piece = pieces[offset]
        if is_neighbour_offset(offset):
            edge = piece[0, piece.shape[1] - count :].reshape(shape)
            piece = piece[:, : piece.shape[1] - count]
            if before is None:
                before = behind = edge
            before = jnp.where((index ^ offset) == index - 1, edge, before)
            behind = jnp.where((index ^ offset) == index + 1, edge, behind)
        rest.append(piece)
    return before, behind, rest


def join_halves(pieces):
    index = lax.axis_index("shard")
    upper = lax.axis_index("rep") % 2 != 0
    full = pieces[0].shape[1]
    count = len(pieces)
    if count > 2:
        mine = jnp.concatenate(pieces[2:], axis=0)
        other = swap_rep(mine, 1)
        halves = jnp.concatenate(
            [jnp.where(upper, other, mine), jnp.where(upper, mine, other)], axis=1
        )
        pieces = pieces[:2] + [halves[i : i + 1] for i in range(count - 2)]
    result = jnp.zeros((count,) + pieces[0].shape[1:], pieces[0].dtype)
    for offset, piece in enumerate(pieces):
        result = lax.dynamic_update_slice_in_dim(result, piece, index ^ offset, 0)
    return result


def visible_part(scores, top, block, fill):
    rows = lax.broadcasted_iota(jnp.int32, (block, block), 0)
    cols = lax.broadcasted_iota(jnp.int32, (block, block), 1)
    last = jnp.where(rows <= cols, scores[top:], fill)
    if top == 0:
        return last
    return jnp.concatenate([scores[:top], last], axis=0)


def turn(values):
    return values.astype(f32).T


def forward_kernel(blocks, block, place, q_ref, k_ref, v_ref, o_ref, low_ref, log_ref, k_rows, v_cols):
    for i in range(blocks):
        here = pl.ds(pl.multiple_of(place[i] * block, block), block)
        there = pl.ds(i * block, block)
        k_rows[there, :] = turn(k_ref[:, here]).astype(low)
        v_cols[:, there] = v_ref[:, here]
    for i in range(blocks):
        here = pl.ds(pl.multiple_of(place[i] * block, block), block)
        top = i * block
        count = top + block
        q_cols = q_ref[:, here] * jnp.asarray(score_scale, low)
        scores = contract(k_rows[:count, :], q_cols, 1, 0)
        scores = visible_part(scores, top, block, -jnp.inf)
        peak = jnp.max(scores, axis=0, keepdims=True)
        weights = jnp.exp(scores - peak)
        total = jnp.sum(weights, axis=0, keepdims=True)
        mixed = contract(v_cols[:, :count], weights.astype(low), 1, 0) / total
        o_ref[:, here] = mixed
        low_ref[:, here] = mixed.astype(low)
        log_ref[0, :, here] = peak + jnp.log(total)


def backward_kernel(
    blocks,
    block,
    place,
    q_ref,
    k_ref,
    v_ref,
    g_ref,
    o_ref,
    log_ref,
    dq_ref,
    dk_ref,
    dv_ref,
    k_rows,
    v_rows,
    k_cols,
    dk_rows,
    dv_rows,
):
    for i in range(blocks):
        here = pl.ds(pl.multiple_of(place[i] * block, block), block)
        there = pl.ds(i * block, block)
        k_rows[there, :] = turn(k_ref[:, here]).astype(low)
        v_rows[there, :] = turn(v_ref[:, here]).astype(low)
        k_cols[:, there] = k_ref[:, here]
    for i in reversed(range(blocks)):
        here = pl.ds(pl.multiple_of(place[i] * block, block), block)
        top = i * block
        count = top + block
        q_cols = q_ref[:, here] * jnp.asarray(score_scale, low)
        g_cols = g_ref[:, here]
        q_rows = turn(q_cols).astype(low)
        g_rows = turn(g_cols).astype(low)
        correction = jnp.sum(g_cols.astype(f32) * o_ref[:, here], axis=0, keepdims=True)
        scores = contract(k_rows[:count, :], q_cols, 1, 0)
        probs = jnp.exp(scores - log_ref[0, :, here])
        probs = visible_part(probs, top, block, 0.0)
        grad_probs = contract(v_rows[:count, :], g_cols, 1, 0)
        grad_scores = (probs * (grad_probs - correction)).astype(low)
        dv_part = contract(probs.astype(low), g_rows, 1, 0)
        dk_part = contract(grad_scores, q_rows, 1, 0)
        if i == blocks - 1:
            dv_rows[:count, :] = dv_part
            dk_rows[:count, :] = dk_part
        else:
            dv_rows[:count, :] += dv_part
            dk_rows[:count, :] += dk_part
        dq = contract(k_cols[:, :count], grad_scores, 1, 0) * score_scale
        dq_ref[:, here] = dq.astype(low)
    for i in range(blocks):
        here = pl.ds(pl.multiple_of(place[i] * block, block), block)
        there = pl.ds(i * block, block)
        dk_ref[:, here] = dk_rows[there, :].T.astype(low)
        dv_ref[:, here] = dv_rows[there, :].T.astype(low)


def head_spec(size, length, first):
    return pl.BlockSpec((size, length), lambda h, place: (first + h, 0))


def attend_forward(place, projected, heads, block):
    size = projected.shape[0] // (3 * heads)
    length = projected.shape[1]
    blocks = length // block
    row = pl.BlockSpec((1, 1, length), lambda h, place: (h, 0, 0))
    return pl.pallas_call(
        functools.partial(forward_kernel, blocks, block),
        grid_spec=pltpu.PrefetchScalarGridSpec(
            num_scalar_prefetch=1,
            grid=(heads,),
            in_specs=[
                head_spec(size, length, 0),
                head_spec(size, length, heads),
                head_spec(size, length, 2 * heads),
            ],
            out_specs=[head_spec(size, length, 0), head_spec(size, length, 0), row],
            scratch_shapes=[
                pltpu.VMEM((length, size), low),
                pltpu.VMEM((size, length), low),
            ],
        ),
        out_shape=[
            jax.ShapeDtypeStruct((heads * size, length), f32),
            jax.ShapeDtypeStruct((heads * size, length), low),
            jax.ShapeDtypeStruct((heads, 1, length), f32),
        ],
        cost_estimate=pl.CostEstimate(
            flops=4 * heads * length * length * size,
            bytes_accessed=heads * length * size * 12,
            transcendentals=heads * length * length,
        ),
        compiler_params=pltpu.CompilerParams(vmem_limit_bytes=32 * 1024 * 1024),
        name="attend_forward",
    )(place, projected, projected, projected)


def attend_backward(place, projected, grad, mixed, log_total, heads, block):
    size = projected.shape[0] // (3 * heads)
    length = projected.shape[1]
    blocks = length // block
    row = pl.BlockSpec((1, 1, length), lambda h, place: (h, 0, 0))
    out = jax.ShapeDtypeStruct((heads * size, length), low)
    return pl.pallas_call(
        functools.partial(backward_kernel, blocks, block),
        grid_spec=pltpu.PrefetchScalarGridSpec(
            num_scalar_prefetch=1,
            grid=(heads,),
            in_specs=[
                head_spec(size, length, 0),
                head_spec(size, length, heads),
                head_spec(size, length, 2 * heads),
                head_spec(size, length, 0),
                head_spec(size, length, 0),
                row,
            ],
            out_specs=[head_spec(size, length, 0)] * 3,
            scratch_shapes=[
                pltpu.VMEM((length, size), low),
                pltpu.VMEM((length, size), low),
                pltpu.VMEM((size, length), low),
                pltpu.VMEM((length, size), f32),
                pltpu.VMEM((length, size), f32),
            ],
        ),
        out_shape=[out, out, out],
        cost_estimate=pl.CostEstimate(
            flops=10 * heads * length * length * size,
            bytes_accessed=heads * length * size * 20,
            transcendentals=heads * length * length,
        ),
        compiler_params=pltpu.CompilerParams(vmem_limit_bytes=32 * 1024 * 1024),
        name="attend_backward",
    )(place, projected, projected, projected, grad, mixed, log_total)


def local(
    block_input,
    first_gain,
    first_shift,
    query_key_value_weight,
    query_bias,
    value_bias,
    attention_output_weight,
    attention_output_bias,
    second_gain,
    second_shift,
    up_weight,
    up_bias,
    down_weight,
    down_bias,
    cotangent,
):
    shards = lax.axis_size("shard")
    index = lax.axis_index("shard")
    seqs, span, width = block_input.shape
    size = width // HEADS
    own = width // shards
    hidden = up_bias.shape[0]
    starts = [d * own // size for d in range(shards)]
    heads = max(-(-(d + 1) * own // size) - starts[d] for d in range(shards))
    window = heads * size
    pad = window - own
    start = index * own // size
    skew = index * own - start * size
    order = relative_order()
    inverse_order = jnp.asarray([order.index(o) for o in range(shards)], jnp.int32)
    place = inverse_order[jnp.arange(shards, dtype=jnp.int32) ^ index]

    own_input = block_input.reshape(seqs * span, width)
    inputs_all = gather_relative(own_input)
    vectors = gather_absolute(
        jnp.stack(
            [
                first_gain,
                first_shift,
                query_bias,
                value_bias,
                attention_output_bias,
                second_gain,
                second_shift,
                down_bias,
            ]
        )
    )
    vectors = vectors.transpose(1, 0, 2).reshape(8, width)
    gain_one, shift_one, bias_query, bias_value, bias_out, gain_two, shift_two, bias_down = (
        vectors[i] for i in range(8)
    )
    weight_in_chain = Chain(
        exchange_steps(
            jnp.stack(
            [
                jnp.concatenate(
                    [
                        query_key_value_weight[
                            :, part * width + s * size : part * width + s * size + window
                        ]
                        for part in range(3)
                    ],
                    axis=1,
                )
                for s in starts
            ]
        )
    ))
    rows = shards * seqs * span
    normed_all, _ = normalize(inputs_all.astype(f32))
    hidden_one = (normed_all * gain_one + shift_one).astype(low)
    hidden_one = weight_in_chain.advance(weight_in_chain, hidden_one)
    weight_in = weight_in_chain.holds.reshape(width, 3 * window)
    up_blocks = jnp.stack([up_weight[:, s * hidden : (s + 1) * hidden] for s in range(shards)])
    own_branch = cotangent.reshape(seqs * span, width).astype(low)
    (up_blocks, own_branch), weight_in = after((up_blocks, own_branch), weight_in)
    up_pieces = send_halves(
        up_blocks, attention_output_weight[:pad], attention_output_weight[own - pad :]
    )
    far_branch = swap(own_branch, bits_far_first()[0])
    grad_out = cotangent.reshape(seqs * span, width)

    def own_rows(values):
        return lax.dynamic_slice_in_dim(values, skew, own, 0)

    bias_window = jnp.concatenate(
        [
            lax.dynamic_slice_in_dim(bias_query, start * size, window, 0),
            jnp.zeros((window,), low),
            lax.dynamic_slice_in_dim(bias_value, start * size, window, 0),
        ]
    ).astype(f32)
    projected = (contract(weight_in, hidden_one, 0, 1) + bias_window[:, None]).astype(low)

    def per_sequence(values):
        lead = values.shape[:-1]
        split = values.reshape(lead + (shards, seqs, span))
        return [split[..., :, s, :].reshape(lead + (shards * span,)) for s in range(seqs)]

    def join_sequences(parts):
        if seqs == 1:
            return parts[0]
        lead = parts[0].shape[:-1]
        joined = jnp.stack([p.reshape(lead + (shards, span)) for p in parts], axis=-2)
        return joined.reshape(lead + (rows,))

    projected_parts = per_sequence(projected) if seqs > 1 else [projected]
    forward_parts = [attend_forward(place, p, heads, span) for p in projected_parts]
    attended = join_sequences([p[1] for p in forward_parts])
    attended, (up_pieces, far_branch) = after(attended, (up_pieces, far_branch))
    branch = gather_relative(jnp.concatenate([own_branch, far_branch], axis=0), slice(1, None))
    before_rows, behind_rows, up_pieces = take_edges(up_pieces, (pad, width))
    weight_out_window = lax.dynamic_slice_in_dim(
        jnp.concatenate([before_rows, attention_output_weight, behind_rows], axis=0),
        pad - skew,
        window,
        0,
    )
    attended = own_rows(attended)
    weight_up = join_halves(up_pieces).reshape(width, hidden)
    mixed_sum = scatter_relative(
        contract(attended, attention_output_weight, 0, 0)
    )
    layer_input = own_input.astype(f32)
    middle = layer_input + mixed_sum + bias_out

    normed_two, inverse_two = normalize(middle)
    hidden_two = gather_relative((normed_two * gain_two + shift_two).astype(low))
    before = contract(hidden_two, weight_up, 1, 0) + up_bias
    activated, slope = gelu_parts(before)
    activated = activated.astype(low)
    grad_before = (contract(branch, down_weight, 1, 1) * slope).astype(low)
    hidden_two_sum = contract(grad_before, weight_up, 1, 1)
    hidden_two_sum, late_before, late_active = lax.optimization_barrier(
        (hidden_two_sum, grad_before, activated)
    )
    hidden_chain = Chain(shard_sum(hidden_two_sum))
    late_before = hidden_chain.advance(hidden_chain, late_before)
    while hidden_chain.waits is not None:
        hidden_chain.advance(hidden_chain)
    grad_hidden_two = hidden_chain.holds
    near, far = rep_bits(False), rep_bits(True)
    down_weight_grad = contract(late_active, branch, 0, 0).astype(low)[None]
    down_chain = Chain(plain_sum(down_weight_grad, near))
    up_weight_grad = contract(hidden_two, late_before, 0, 0).astype(low)
    up_weight_grad = up_weight_grad.reshape(shards, own, hidden)
    down_sum = contract(late_active, down_weight, 1, 0)
    grad_middle = grad_out + norm_back(grad_hidden_two, normed_two, inverse_two, gain_two)
    up_chain = Chain(turned_sum(up_weight_grad, far))
    late_middle = down_chain.advance(up_chain, grad_middle)

    grad_mixed = gather_relative(grad_middle.astype(low))
    up_chain.advance(down_chain)
    block_chain = Chain(shard_sum(down_sum))
    late_mixed = block_chain.advance(up_chain, grad_mixed)
    grad_attended = contract(weight_out_window, grad_mixed, 1, 1).astype(low)
    grad_attended, (down_chain.holds, up_chain.holds, block_chain.holds) = after(
        grad_attended, (down_chain.holds, up_chain.holds, block_chain.holds)
    )
    grad_parts = per_sequence(grad_attended) if seqs > 1 else [grad_attended]
    backward_parts = [
        attend_backward(place, p, g, f[0], f[2], heads, span)
        for p, g, f in zip(projected_parts, grad_parts, forward_parts)
    ]
    grad_query, grad_key, grad_value = (
        join_sequences([p[i] for p in backward_parts]) for i in range(3)
    )
    own_query, own_key, own_value = (own_rows(g) for g in (grad_query, grad_key, grad_value))
    output_weight_grad = contract(attended, grad_mixed, 1, 0).astype(low)
    late_query = block_chain.advance(up_chain, own_query)
    down_chain.advance(block_chain)
    up_chain.advance(down_chain)

    (grad_query, grad_key, grad_value), (down_chain.holds, up_chain.holds) = after(
        (grad_query, grad_key, grad_value), (down_chain.holds, up_chain.holds)
    )
    own_query, own_key, own_value = (own_rows(g) for g in (grad_query, grad_key, grad_value))
    own_projected = jnp.concatenate([own_query, own_key, own_value], axis=0)

    def by_owner(gradient):
        return gradient.reshape(shards, own, gradient.shape[1])

    first_part = by_owner(contract(hidden_one, own_projected[: 2 * own], 0, 1).astype(low))
    second_part = by_owner(contract(hidden_one, own_value, 0, 1).astype(low))
    output_blocks = jnp.stack(
        [output_weight_grad[:, s * own : (s + 1) * own] for s in range(shards)]
    )
    second_part = jnp.concatenate([second_part, output_blocks], axis=2)
    mixer_chain = Chain(mixer_sum(first_part, second_part, [near, far], own))
    line = jnp.arange(window)
    mine = ((line >= skew) & (line < skew + own))[:, None]
    grad_projected = jnp.concatenate(
        [jnp.where(mine, g, jnp.zeros_like(g)) for g in (grad_query, grad_key, grad_value)], axis=0
    )
    hidden_chain = Chain(shard_sum(contract(grad_projected, weight_in, 0, 1)))
    chain = up_chain
    for step in (
        [hidden_chain, down_chain, mixer_chain, up_chain, hidden_chain]
        + [block_chain, hidden_chain] * shards
    ):
        step.advance(chain)
        chain = step
    block_output = middle + block_chain.holds + bias_down
    grad_hidden_one = hidden_chain.holds
    normed_one, inverse_one = normalize(layer_input)
    input_grad = late_middle + norm_back(grad_hidden_one, normed_one, inverse_one, gain_one)

    def own_part(values):
        return lax.dynamic_slice_in_dim(values, index * own, own, 0)

    partial = jnp.stack(
        [
            jnp.sum(grad_hidden_one * normed_one, axis=0),
            jnp.sum(grad_hidden_one, axis=0),
            jnp.sum(grad_hidden_two * normed_two, axis=0),
            jnp.sum(grad_hidden_two, axis=0),
        ]
    )
    vector_chain = Chain(
        vector_sum(
            partial,
            [
                jnp.sum(late_query.astype(f32), axis=1),
                jnp.sum(own_value.astype(f32), axis=1),
                own_part(jnp.sum(late_mixed.astype(f32), axis=0)),
                own_part(jnp.sum(branch.astype(f32), axis=0)),
                jnp.sum(grad_before.astype(f32), axis=0),
            ],
            own_part,
        )
    )
    down, up, mixer, vector = chains = [down_chain, up_chain, mixer_chain, vector_chain]
    chain = hidden_chain
    for step in (
        [up, vector, vector, vector, mixer, down, vector, vector, up]
        + [mixer, down, mixer, up, mixer, mixer, down, up, mixer]
        + chains * 8
    ):
        if step.waits is not None:
            step.advance(chain)
            chain = step
    complete = vector_chain.holds
    down_weight_grad = down_chain.holds[0]
    up_weight_grad = up_chain.holds
    first_part, second_part = mixer_chain.holds
    input_weight_grad = jnp.concatenate([first_part, second_part[:, :width]], axis=1)
    output_weight_grad = second_part[:, width:]
    (
        first_gain_grad,
        first_shift_grad,
        second_gain_grad,
        second_shift_grad,
        query_bias_grad,
        value_bias_grad,
        output_bias_grad,
        down_bias_grad,
    ) = (complete[i * own : (i + 1) * own] for i in range(8))
    up_bias_grad = complete[8 * own :]
    return (
        block_output.reshape(seqs, span, width),
        input_grad.reshape(seqs, span, width),
        first_gain_grad,
        first_shift_grad,
        input_weight_grad.astype(f32),
        query_bias_grad,
        value_bias_grad,
        output_weight_grad.astype(f32),
        output_bias_grad,
        second_gain_grad,
        second_shift_grad,
        up_weight_grad.astype(f32),
        up_bias_grad,
        down_weight_grad.astype(f32),
        down_bias_grad,
    )


def solution(mesh):
    matrix, vector, tokens = P("shard", None), P("shard"), P("rep", "shard", None)
    return jax.shard_map(
        local,
        mesh=mesh,
        in_specs=(
            tokens,
            vector,
            vector,
            matrix,
            vector,
            vector,
            matrix,
            vector,
            vector,
            vector,
            matrix,
            vector,
            matrix,
            vector,
            tokens,
        ),
        out_specs=(
            tokens,
            tokens,
            vector,
            vector,
            matrix,
            vector,
            vector,
            matrix,
            vector,
            vector,
            vector,
            matrix,
            vector,
            matrix,
            vector,
        ),
        check_vma=False,
    )
```

```python
import functools

import jax
import jax.numpy as jnp
from jax import lax
from jax.experimental import pallas as pl
from jax.experimental.pallas import tpu as pltpu
from jax.sharding import PartitionSpec as P

HEADS = 17

epsilon = 1e-05
score_scale = 0.125
low = jnp.bfloat16
f32 = jnp.float32


def normalize(values):
    centre = jnp.mean(values, axis=-1, keepdims=True)
    centred = values - centre
    inverse = lax.rsqrt(jnp.mean(centred * centred, axis=-1, keepdims=True) + epsilon)
    return (centred * inverse, inverse)


def norm_back(grad, normed, inverse, gain):
    scaled = grad * gain
    first = jnp.mean(scaled, axis=-1, keepdims=True)
    second = jnp.mean(scaled * normed, axis=-1, keepdims=True)
    return inverse * (scaled - first - normed * second)


def gelu_parts(values):
    cumulative = 0.5 * (1.0 + lax.erf(values * 0.7071067811865476))
    density = jnp.exp(-0.5 * values * values) * 0.3989422804014327
    return values * cumulative, cumulative + values * density


def contract(left, right, left_dim, right_dim):
    return lax.dot_general(
        left, right, (((left_dim,), (right_dim,)), ((), ())), preferred_element_type=f32
    )


def swap(values, bit):
    size = lax.axis_size("shard")
    return lax.ppermute(values, "shard", [(i, i ^ bit) for i in range(size)])


def bits_far_first():
    bit = lax.axis_size("shard") // 2
    bits = []
    while bit:
        bits.append(bit)
        bit //= 2
    return bits


def relative_order():
    order = [0]
    for bit in bits_far_first():
        order = order + [o ^ bit for o in order]
    return order


def gather_relative(block, steps=slice(None)):
    for bit in bits_far_first()[steps]:
        block = jnp.concatenate([block, swap(block, bit)], axis=0)
    return block


def gather_absolute(block):
    index = lax.axis_index("shard")
    stack = block[None]
    for bit in bits_far_first():
        other = swap(stack, bit)
        upper = (index & bit) != 0
        pair = jnp.stack(
            [jnp.where(upper, other, stack), jnp.where(upper, stack, other)], axis=1
        )
        stack = pair.reshape((2 * stack.shape[0],) + block.shape)
    return stack


def scatter_relative(parts):
    for bit in reversed(bits_far_first()):
        half = parts.shape[0] // 2
        other = swap(parts[half:].astype(low), bit)
        parts = parts[:half] + other.astype(f32)
    return parts


def swap_rep(values, bit):
    size = lax.axis_size("rep")
    return lax.ppermute(values, "rep", [(i, i ^ bit) for i in range(size)])


def rep_bits(turned):
    bits, bit = [], 1
    while bit < lax.axis_size("rep"):
        bits.append(bit)
        bit *= 2
    return bits[1:2] + bits[:1] + bits[2:] if turned else bits


def after(values, gate):
    return lax.optimization_barrier((values, gate))


def half_window(rows):
    return min(rows, (rows + 15) // 16 * 8)


def half_of(values, index):
    rows = values.shape[1]
    window = half_window(rows)
    return lax.dynamic_slice_in_dim(values, index * (rows - window), window, 1)


def sent_half(values, bit):
    return swap_rep(half_of(values, 1 - (lax.axis_index("rep") // bit) % 2), bit)


def kept_half(values, bit):
    return half_of(values, (lax.axis_index("rep") // bit) % 2)


def add(keep, other):
    return (keep.astype(f32) + other.astype(f32)).astype(low)


def join(values, other, bit, rows):
    window = values.shape[1]
    upper = (lax.axis_index("rep") // bit) % 2 != 0
    first = jnp.where(upper, other, values)
    second = jnp.where(upper, values, other)
    return jnp.concatenate([first, second[:, 2 * window - rows :]], axis=1)


class Chain:
    def __init__(self, steps):
        self.steps = steps
        self.take(None)

    def take(self, got):
        try:
            self.waits, self.holds = self.steps.send(got)
        except StopIteration as end:
            self.waits, self.holds = None, end.value

    def advance(self, previous, gate=()):
        if self.waits is not None:
            if previous is self:
                waits, gate = after(self.waits, gate)
            else:
                waits, (previous.holds, gate) = after(self.waits, (previous.holds, gate))
            self.take((waits, self.holds))
        return gate


def scatter_steps(lanes, orders):
    sizes = []
    for step in range(len(orders[0])):
        sizes.append(lanes[0].shape[1])
        others, held = yield (
            tuple(sent_half(v, order[step]) for v, order in zip(lanes, orders)),
            tuple(lanes),
        )
        lanes = [
            add(kept_half(v, order[step]), other) for v, other, order in zip(held, others, orders)
        ]
    return list(lax.optimization_barrier(tuple(lanes))), sizes


def gather_steps(lanes, orders, sizes):
    for step in reversed(range(len(orders[0]))):
        others, lanes = yield (
            tuple(swap_rep(v, order[step]) for v, order in zip(lanes, orders)),
            tuple(lanes),
        )
        lanes = [
            join(v, other, order[step], sizes[step])
            for v, other, order in zip(lanes, others, orders)
        ]
    return lanes


def exchange_steps(blocks):
    size = lax.axis_size("shard")
    index = lax.axis_index("shard")
    pieces = [lax.dynamic_index_in_dim(blocks, index ^ o, 0, keepdims=True) for o in range(size)]
    others, first = yield tuple(swap(pieces[o], o) for o in range(1, size)), pieces[0]
    result = jnp.zeros_like(blocks)
    for o, piece in enumerate((first,) + tuple(others)):
        result = lax.dynamic_update_slice_in_dim(result, piece, index ^ o, 0)
    return result


def plain_sum(values, order):
    lanes, sizes = yield from scatter_steps([values], [order])
    lanes = yield from gather_steps(lanes, [order], sizes)
    return lanes[0]


def turned_sum(values, order):
    lanes, sizes = yield from scatter_steps([values], [order])
    blocks = yield from exchange_steps(lanes[0])
    columns = jnp.concatenate([blocks[i] for i in range(blocks.shape[0])], axis=1)
    lanes = yield from gather_steps([columns[None]], [order], sizes)
    return lanes[0][0]


def mixer_sum(first, second, orders, own):
    lanes, sizes = yield from scatter_steps([first, second], orders)
    blocks = yield from exchange_steps(
        jnp.concatenate([lanes[0], lanes[1][:, :, :own]], axis=2)
    )
    count = blocks.shape[0]
    parts = [
        jnp.concatenate([blocks[s, :, i * own : (i + 1) * own] for s in range(count)], axis=1)
        for i in range(3)
    ]
    output = jnp.concatenate([lanes[1][i, :, own:] for i in range(count)], axis=1)
    lanes = [
        jnp.concatenate(parts[:2], axis=1)[None],
        jnp.concatenate([parts[2], output], axis=1)[None],
    ]
    lanes = yield from gather_steps(lanes, orders, sizes)
    return lanes[0][0], lanes[1][0]


def shard_sum(parts):
    for bit in reversed(bits_far_first()):
        half = parts.shape[0] // 2
        (other,), kept = yield (swap(parts[half:].astype(low), bit),), parts[:half]
        parts = kept + other.astype(f32)
    return parts


def vector_sum(partial, complete, own_part):
    for bit in bits_far_first():
        (other,), partial = yield (swap(partial, bit),), partial
        partial = partial + other
    total = jnp.concatenate([own_part(p) for p in partial] + complete)
    for bit in rep_bits(False):
        (other,), total = yield (swap_rep(total, bit),), total
        total = total + other
    return total


def is_neighbour_offset(offset):
    return offset & (offset + 1) == 0


def send_halves(blocks, first, last):
    index = lax.axis_index("shard")
    size = lax.axis_size("shard")
    half = blocks.shape[1] // 2
    part = (lax.axis_index("rep") % 2) * half
    pieces = []
    for offset in range(size):
        piece = lax.dynamic_index_in_dim(blocks, index ^ offset, 0, keepdims=True)
        if offset >= 2:
            piece = lax.dynamic_slice_in_dim(piece, part, half, 1)
        if offset:
            if is_neighbour_offset(offset):
                edge = jnp.where((index ^ offset) == index + 1, last, first)
                edge = edge.reshape(1, -1, piece.shape[2])
                piece = jnp.concatenate([piece, edge], axis=1)
            piece = swap(piece, offset)
        pieces.append(piece)
    return pieces


def take_edges(pieces, shape):
    index = lax.axis_index("shard")
    before = behind = None
    rest = pieces[:1]
    count = shape[0] * shape[1] // pieces[0].shape[2]
    for offset in range(1, len(pieces)):
        piece = pieces[offset]
        if is_neighbour_offset(offset):
            edge = piece[0, piece.shape[1] - count :].reshape(shape)
            piece = piece[:, : piece.shape[1] - count]
            if before is None:
                before = behind = edge
            before = jnp.where((index ^ offset) == index - 1, edge, before)
            behind = jnp.where((index ^ offset) == index + 1, edge, behind)
        rest.append(piece)
    return before, behind, rest


def join_halves(pieces):
    index = lax.axis_index("shard")
    upper = lax.axis_index("rep") % 2 != 0
    full = pieces[0].shape[1]
    count = len(pieces)
    if count > 2:
        mine = jnp.concatenate(pieces[2:], axis=0)
        other = swap_rep(mine, 1)
        halves = jnp.concatenate(
            [jnp.where(upper, other, mine), jnp.where(upper, mine, other)], axis=1
        )
        pieces = pieces[:2] + [halves[i : i + 1] for i in range(count - 2)]
    result = jnp.zeros((count,) + pieces[0].shape[1:], pieces[0].dtype)
    for offset, piece in enumerate(pieces):
        result = lax.dynamic_update_slice_in_dim(result, piece, index ^ offset, 0)
    return result


def visible_part(scores, top, block, fill):
    rows = lax.broadcasted_iota(jnp.int32, (block, block), 0)
    cols = lax.broadcasted_iota(jnp.int32, (block, block), 1)
    last = jnp.where(rows <= cols, scores[top:], fill)
    if top == 0:
        return last
    return jnp.concatenate([scores[:top], last], axis=0)


def turn(values):
    return values.astype(f32).T


def forward_kernel(blocks, block, place, q_ref, k_ref, v_ref, o_ref, low_ref, log_ref, k_rows, v_cols):
    for i in range(blocks):
        here = pl.ds(pl.multiple_of(place[i] * block, block), block)
        there = pl.ds(i * block, block)
        k_rows[there, :] = turn(k_ref[:, here]).astype(low)
        v_cols[:, there] = v_ref[:, here]
    for i in range(blocks):
        here = pl.ds(pl.multiple_of(place[i] * block, block), block)
        top = i * block
        count = top + block
        q_cols = q_ref[:, here] * jnp.asarray(score_scale, low)
        scores = contract(k_rows[:count, :], q_cols, 1, 0)
        scores = visible_part(scores, top, block, -jnp.inf)
        peak = jnp.max(scores, axis=0, keepdims=True)
        weights = jnp.exp(scores - peak)
        total = jnp.sum(weights, axis=0, keepdims=True)
        mixed = contract(v_cols[:, :count], weights.astype(low), 1, 0) / total
        o_ref[:, here] = mixed
        low_ref[:, here] = mixed.astype(low)
        log_ref[0, :, here] = peak + jnp.log(total)


def backward_kernel(
    blocks,
    block,
    place,
    q_ref,
    k_ref,
    v_ref,
    g_ref,
    o_ref,
    log_ref,
    dq_ref,
    dk_ref,
    dv_ref,
    k_rows,
    v_rows,
    k_cols,
    dk_rows,
    dv_rows,
):
    for i in range(blocks):
        here = pl.ds(pl.multiple_of(place[i] * block, block), block)
        there = pl.ds(i * block, block)
        k_rows[there, :] = turn(k_ref[:, here]).astype(low)
        v_rows[there, :] = turn(v_ref[:, here]).astype(low)
        k_cols[:, there] = k_ref[:, here]
    for i in reversed(range(blocks)):
        here = pl.ds(pl.multiple_of(place[i] * block, block), block)
        top = i * block
        count = top + block
        q_cols = q_ref[:, here] * jnp.asarray(score_scale, low)
        g_cols = g_ref[:, here]
        q_rows = turn(q_cols).astype(low)
        g_rows = turn(g_cols).astype(low)
        correction = jnp.sum(g_cols.astype(f32) * o_ref[:, here], axis=0, keepdims=True)
        scores = contract(k_rows[:count, :], q_cols, 1, 0)
        probs = jnp.exp(scores - log_ref[0, :, here])
        probs = visible_part(probs, top, block, 0.0)
        grad_probs = contract(v_rows[:count, :], g_cols, 1, 0)
        grad_scores = (probs * (grad_probs - correction)).astype(low)
        dv_part = contract(probs.astype(low), g_rows, 1, 0)
        dk_part = contract(grad_scores, q_rows, 1, 0)
        if i == blocks - 1:
            dv_rows[:count, :] = dv_part
            dk_rows[:count, :] = dk_part
        else:
            dv_rows[:count, :] += dv_part
            dk_rows[:count, :] += dk_part
        dq = contract(k_cols[:, :count], grad_scores, 1, 0) * score_scale
        dq_ref[:, here] = dq.astype(low)
    for i in range(blocks):
        here = pl.ds(pl.multiple_of(place[i] * block, block), block)
        there = pl.ds(i * block, block)
        dk_ref[:, here] = dk_rows[there, :].T.astype(low)
        dv_ref[:, here] = dv_rows[there, :].T.astype(low)


def head_spec(size, length, first):
    return pl.BlockSpec((size, length), lambda h, place: (first + h, 0))


def attend_forward(place, projected, heads, block):
    size = projected.shape[0] // (3 * heads)
    length = projected.shape[1]
    blocks = length // block
    row = pl.BlockSpec((1, 1, length), lambda h, place: (h, 0, 0))
    return pl.pallas_call(
        functools.partial(forward_kernel, blocks, block),
        grid_spec=pltpu.PrefetchScalarGridSpec(
            num_scalar_prefetch=1,
            grid=(heads,),
            in_specs=[
                head_spec(size, length, 0),
                head_spec(size, length, heads),
                head_spec(size, length, 2 * heads),
            ],
            out_specs=[head_spec(size, length, 0), head_spec(size, length, 0), row],
            scratch_shapes=[
                pltpu.VMEM((length, size), low),
                pltpu.VMEM((size, length), low),
            ],
        ),
        out_shape=[
            jax.ShapeDtypeStruct((heads * size, length), f32),
            jax.ShapeDtypeStruct((heads * size, length), low),
            jax.ShapeDtypeStruct((heads, 1, length), f32),
        ],
        cost_estimate=pl.CostEstimate(
            flops=4 * heads * length * length * size,
            bytes_accessed=heads * length * size * 12,
            transcendentals=heads * length * length,
        ),
        compiler_params=pltpu.CompilerParams(vmem_limit_bytes=32 * 1024 * 1024),
        name="attend_forward",
    )(place, projected, projected, projected)


def attend_backward(place, projected, grad, mixed, log_total, heads, block):
    size = projected.shape[0] // (3 * heads)
    length = projected.shape[1]
    blocks = length // block
    row = pl.BlockSpec((1, 1, length), lambda h, place: (h, 0, 0))
    out = jax.ShapeDtypeStruct((heads * size, length), low)
    return pl.pallas_call(
        functools.partial(backward_kernel, blocks, block),
        grid_spec=pltpu.PrefetchScalarGridSpec(
            num_scalar_prefetch=1,
            grid=(heads,),
            in_specs=[
                head_spec(size, length, 0),
                head_spec(size, length, heads),
                head_spec(size, length, 2 * heads),
                head_spec(size, length, 0),
                head_spec(size, length, 0),
                row,
            ],
            out_specs=[head_spec(size, length, 0)] * 3,
            scratch_shapes=[
                pltpu.VMEM((length, size), low),
                pltpu.VMEM((length, size), low),
                pltpu.VMEM((size, length), low),
                pltpu.VMEM((length, size), f32),
                pltpu.VMEM((length, size), f32),
            ],
        ),
        out_shape=[out, out, out],
        cost_estimate=pl.CostEstimate(
            flops=10 * heads * length * length * size,
            bytes_accessed=heads * length * size * 20,
            transcendentals=heads * length * length,
        ),
        compiler_params=pltpu.CompilerParams(vmem_limit_bytes=32 * 1024 * 1024),
        name="attend_backward",
    )(place, projected, projected, projected, grad, mixed, log_total)


def local(
    block_input,
    first_gain,
    first_shift,
    query_key_value_weight,
    query_bias,
    value_bias,
    attention_output_weight,
    attention_output_bias,
    second_gain,
    second_shift,
    up_weight,
    up_bias,
    down_weight,
    down_bias,
    cotangent,
):
    shards = lax.axis_size("shard")
    index = lax.axis_index("shard")
    seqs, span, width = block_input.shape
    size = width // HEADS
    own = width // shards
    hidden = up_bias.shape[0]
    starts = [d * own // size for d in range(shards)]
    heads = max(-(-(d + 1) * own // size) - starts[d] for d in range(shards))
    window = heads * size
    pad = window - own
    start = index * own // size
    skew = index * own - start * size
    order = relative_order()
    inverse_order = jnp.asarray([order.index(o) for o in range(shards)], jnp.int32)
    place = inverse_order[jnp.arange(shards, dtype=jnp.int32) ^ index]

    own_input = block_input.reshape(seqs * span, width)
    inputs_all = gather_relative(own_input)
    vectors = gather_absolute(
        jnp.stack(
            [
                first_gain,
                first_shift,
                query_bias,
                value_bias,
                attention_output_bias,
                second_gain,
                second_shift,
                down_bias,
            ]
        )
    )
    vectors = vectors.transpose(1, 0, 2).reshape(8, width)
    gain_one, shift_one, bias_query, bias_value, bias_out, gain_two, shift_two, bias_down = (
        vectors[i] for i in range(8)
    )
    weight_in_chain = Chain(
        exchange_steps(
            jnp.stack(
            [
                jnp.concatenate(
                    [
                        query_key_value_weight[
                            :, part * width + s * size : part * width + s * size + window
                        ]
                        for part in range(3)
                    ],
                    axis=1,
                )
                for s in starts
            ]
        )
    ))
    rows = shards * seqs * span
    normed_all, _ = normalize(inputs_all.astype(f32))
    hidden_one = (normed_all * gain_one + shift_one).astype(low)
    up_blocks = jnp.stack([up_weight[:, s * hidden : (s + 1) * hidden] for s in range(shards)])
    own_branch = cotangent.reshape(seqs * span, width).astype(low)
    hidden_one, up_blocks, own_branch = weight_in_chain.advance(
        weight_in_chain, (hidden_one, up_blocks, own_branch)
    )
    weight_in = weight_in_chain.holds.reshape(width, 3 * window)
    up_pieces = send_halves(
        up_blocks, attention_output_weight[:pad], attention_output_weight[own - pad :]
    )
    far_branch = swap(own_branch, bits_far_first()[0])
    grad_out = cotangent.reshape(seqs * span, width)

    def own_rows(values):
        return lax.dynamic_slice_in_dim(values, skew, own, 0)

    bias_window = jnp.concatenate(
        [
            lax.dynamic_slice_in_dim(bias_query, start * size, window, 0),
            jnp.zeros((window,), low),
            lax.dynamic_slice_in_dim(bias_value, start * size, window, 0),
        ]
    ).astype(f32)
    projected = (contract(weight_in, hidden_one, 0, 1) + bias_window[:, None]).astype(low)

    def per_sequence(values):
        lead = values.shape[:-1]
        split = values.reshape(lead + (shards, seqs, span))
        return [split[..., :, s, :].reshape(lead + (shards * span,)) for s in range(seqs)]

    def join_sequences(parts):
        if seqs == 1:
            return parts[0]
        lead = parts[0].shape[:-1]
        joined = jnp.stack([p.reshape(lead + (shards, span)) for p in parts], axis=-2)
        return joined.reshape(lead + (rows,))

    projected_parts = per_sequence(projected) if seqs > 1 else [projected]
    forward_parts = [attend_forward(place, p, heads, span) for p in projected_parts]
    attended = join_sequences([p[1] for p in forward_parts])
    attended, (up_pieces, far_branch) = after(attended, (up_pieces, far_branch))
    branch = gather_relative(jnp.concatenate([own_branch, far_branch], axis=0), slice(1, None))
    before_rows, behind_rows, up_pieces = take_edges(up_pieces, (pad, width))
    weight_out_window = lax.dynamic_slice_in_dim(
        jnp.concatenate([before_rows, attention_output_weight, behind_rows], axis=0),
        pad - skew,
        window,
        0,
    )
    attended = own_rows(attended)
    weight_up = join_halves(up_pieces).reshape(width, hidden)
    mixed_sum = scatter_relative(
        contract(attended, attention_output_weight, 0, 0)
    )
    layer_input = own_input.astype(f32)
    middle = layer_input + mixed_sum + bias_out

    normed_two, inverse_two = normalize(middle)
    hidden_two = gather_relative((normed_two * gain_two + shift_two).astype(low))
    before = contract(hidden_two, weight_up, 1, 0) + up_bias
    activated, slope = gelu_parts(before)
    activated = activated.astype(low)
    grad_before = (contract(branch, down_weight, 1, 1) * slope).astype(low)
    hidden_two_sum = contract(grad_before, weight_up, 1, 1)
    hidden_two_sum, late_before, late_active = lax.optimization_barrier(
        (hidden_two_sum, grad_before, activated)
    )
    hidden_chain = Chain(shard_sum(hidden_two_sum))
    late_before = hidden_chain.advance(hidden_chain, late_before)
    while hidden_chain.waits is not None:
        hidden_chain.advance(hidden_chain)
    grad_hidden_two = hidden_chain.holds
    near, far = rep_bits(False), rep_bits(True)
    down_weight_grad = contract(late_active, branch, 0, 0).astype(low)[None]
    down_chain = Chain(plain_sum(down_weight_grad, near))
    up_weight_grad = contract(hidden_two, late_before, 0, 0).astype(low)
    up_weight_grad = up_weight_grad.reshape(shards, own, hidden)
    down_sum = contract(late_active, down_weight, 1, 0)
    grad_middle = grad_out + norm_back(grad_hidden_two, normed_two, inverse_two, gain_two)
    up_chain = Chain(turned_sum(up_weight_grad, far))
    late_middle = down_chain.advance(up_chain, grad_middle)

    grad_mixed = gather_relative(grad_middle.astype(low))
    up_chain.advance(down_chain)
    block_chain = Chain(shard_sum(down_sum))
    late_mixed = block_chain.advance(up_chain, grad_mixed)
    grad_attended = contract(weight_out_window, grad_mixed, 1, 1).astype(low)
    grad_attended, (down_chain.holds, up_chain.holds, block_chain.holds) = after(
        grad_attended, (down_chain.holds, up_chain.holds, block_chain.holds)
    )
    grad_parts = per_sequence(grad_attended) if seqs > 1 else [grad_attended]
    backward_parts = [
        attend_backward(place, p, g, f[0], f[2], heads, span)
        for p, g, f in zip(projected_parts, grad_parts, forward_parts)
    ]
    grad_query, grad_key, grad_value = (
        join_sequences([p[i] for p in backward_parts]) for i in range(3)
    )
    own_query, own_key, own_value = (own_rows(g) for g in (grad_query, grad_key, grad_value))
    output_weight_grad = contract(attended, grad_mixed, 1, 0).astype(low)
    late_query = block_chain.advance(up_chain, own_query)
    down_chain.advance(block_chain)
    up_chain.advance(down_chain)

    (grad_query, grad_key, grad_value), (down_chain.holds, up_chain.holds) = after(
        (grad_query, grad_key, grad_value), (down_chain.holds, up_chain.holds)
    )
    own_query, own_key, own_value = (own_rows(g) for g in (grad_query, grad_key, grad_value))
    own_projected = jnp.concatenate([own_query, own_key, own_value], axis=0)

    def by_owner(gradient):
        return gradient.reshape(shards, own, gradient.shape[1])

    first_part = by_owner(contract(hidden_one, own_projected[: 2 * own], 0, 1).astype(low))
    second_part = by_owner(contract(hidden_one, own_value, 0, 1).astype(low))
    output_blocks = jnp.stack(
        [output_weight_grad[:, s * own : (s + 1) * own] for s in range(shards)]
    )
    second_part = jnp.concatenate([second_part, output_blocks], axis=2)
    mixer_chain = Chain(mixer_sum(first_part, second_part, [near, far], own))
    line = jnp.arange(window)
    mine = ((line >= skew) & (line < skew + own))[:, None]
    grad_projected = jnp.concatenate(
        [jnp.where(mine, g, jnp.zeros_like(g)) for g in (grad_query, grad_key, grad_value)], axis=0
    )
    hidden_chain = Chain(shard_sum(contract(grad_projected, weight_in, 0, 1)))
    chain = up_chain
    for step in (
        [hidden_chain, down_chain, mixer_chain, up_chain, hidden_chain]
        + [block_chain, hidden_chain] * shards
    ):
        step.advance(chain)
        chain = step
    block_output = middle + block_chain.holds + bias_down
    grad_hidden_one = hidden_chain.holds
    normed_one, inverse_one = normalize(layer_input)
    input_grad = late_middle + norm_back(grad_hidden_one, normed_one, inverse_one, gain_one)

    def own_part(values):
        return lax.dynamic_slice_in_dim(values, index * own, own, 0)

    partial = jnp.stack(
        [
            jnp.sum(grad_hidden_one * normed_one, axis=0),
            jnp.sum(grad_hidden_one, axis=0),
            jnp.sum(grad_hidden_two * normed_two, axis=0),
            jnp.sum(grad_hidden_two, axis=0),
        ]
    )
    vector_chain = Chain(
        vector_sum(
            partial,
            [
                jnp.sum(late_query.astype(f32), axis=1),
                jnp.sum(own_value.astype(f32), axis=1),
                own_part(jnp.sum(late_mixed.astype(f32), axis=0)),
                own_part(jnp.sum(branch.astype(f32), axis=0)),
                jnp.sum(grad_before.astype(f32), axis=0),
            ],
            own_part,
        )
    )
    down, up, mixer, vector = chains = [down_chain, up_chain, mixer_chain, vector_chain]
    chain = hidden_chain
    for step in (
        [up, vector, vector, vector, mixer, down, vector, vector, up]
        + [mixer, down, mixer, up, mixer, mixer, down, up]
        + [down, up, vector] * 8
    ):
        if step.waits is not None:
            step.advance(chain)
            chain = step
    grads = (down.holds[0].astype(f32), up.holds.astype(f32))
    while mixer.waits is not None:
        grads = mixer.advance(mixer, grads)
    down_weight_grad, up_weight_grad = grads
    complete = vector_chain.holds
    first_part, second_part = mixer_chain.holds
    input_weight_grad = jnp.concatenate([first_part, second_part[:, :width]], axis=1)
    output_weight_grad = second_part[:, width:]
    (
        first_gain_grad,
        first_shift_grad,
        second_gain_grad,
        second_shift_grad,
        query_bias_grad,
        value_bias_grad,
        output_bias_grad,
        down_bias_grad,
    ) = (complete[i * own : (i + 1) * own] for i in range(8))
    up_bias_grad = complete[8 * own :]
    return (
        block_output.reshape(seqs, span, width),
        input_grad.reshape(seqs, span, width),
        first_gain_grad,
        first_shift_grad,
        input_weight_grad.astype(f32),
        query_bias_grad,
        value_bias_grad,
        output_weight_grad.astype(f32),
        output_bias_grad,
        second_gain_grad,
        second_shift_grad,
        up_weight_grad,
        up_bias_grad,
        down_weight_grad,
        down_bias_grad,
    )


def solution(mesh):
    matrix, vector, tokens = P("shard", None), P("shard"), P("rep", "shard", None)
    return jax.shard_map(
        local,
        mesh=mesh,
        in_specs=(
            tokens,
            vector,
            vector,
            matrix,
            vector,
            vector,
            matrix,
            vector,
            vector,
            vector,
            matrix,
            vector,
            matrix,
            vector,
            tokens,
        ),
        out_specs=(
            tokens,
            tokens,
            vector,
            vector,
            matrix,
            vector,
            vector,
            matrix,
            vector,
            vector,
            vector,
            matrix,
            vector,
            matrix,
            vector,
        ),
        check_vma=False,
    )
```

```python
import functools

import jax
import jax.numpy as jnp
from jax import lax
from jax.experimental import pallas as pl
from jax.experimental.pallas import tpu as pltpu
from jax.sharding import PartitionSpec as P

HEADS = 17

epsilon = 1e-05
score_scale = 0.125
low = jnp.bfloat16
f32 = jnp.float32


def normalize(values):
    centre = jnp.mean(values, axis=-1, keepdims=True)
    centred = values - centre
    inverse = lax.rsqrt(jnp.mean(centred * centred, axis=-1, keepdims=True) + epsilon)
    return (centred * inverse, inverse)


def norm_back(grad, normed, inverse, gain):
    scaled = grad * gain
    first = jnp.mean(scaled, axis=-1, keepdims=True)
    second = jnp.mean(scaled * normed, axis=-1, keepdims=True)
    return inverse * (scaled - first - normed * second)


def gelu_parts(values):
    cumulative = 0.5 * (1.0 + lax.erf(values * 0.7071067811865476))
    density = jnp.exp(-0.5 * values * values) * 0.3989422804014327
    return values * cumulative, cumulative + values * density


def contract(left, right, left_dim, right_dim):
    return lax.dot_general(
        left, right, (((left_dim,), (right_dim,)), ((), ())), preferred_element_type=f32
    )


def swap(values, bit):
    size = lax.axis_size("shard")
    return lax.ppermute(values, "shard", [(i, i ^ bit) for i in range(size)])


def bits_far_first():
    bit = lax.axis_size("shard") // 2
    bits = []
    while bit:
        bits.append(bit)
        bit //= 2
    return bits


def relative_order():
    order = [0]
    for bit in bits_far_first():
        order = order + [o ^ bit for o in order]
    return order


def gather_relative(block, steps=slice(None)):
    for bit in bits_far_first()[steps]:
        block = jnp.concatenate([block, swap(block, bit)], axis=0)
    return block


def gather_absolute(block):
    index = lax.axis_index("shard")
    stack = block[None]
    for bit in bits_far_first():
        other = swap(stack, bit)
        upper = (index & bit) != 0
        pair = jnp.stack(
            [jnp.where(upper, other, stack), jnp.where(upper, stack, other)], axis=1
        )
        stack = pair.reshape((2 * stack.shape[0],) + block.shape)
    return stack


def scatter_relative(parts):
    for bit in reversed(bits_far_first()):
        half = parts.shape[0] // 2
        other = swap(parts[half:].astype(low), bit)
        parts = parts[:half] + other.astype(f32)
    return parts


def swap_rep(values, bit):
    size = lax.axis_size("rep")
    return lax.ppermute(values, "rep", [(i, i ^ bit) for i in range(size)])


def rep_bits(turned):
    bits, bit = [], 1
    while bit < lax.axis_size("rep"):
        bits.append(bit)
        bit *= 2
    return bits[1:2] + bits[:1] + bits[2:] if turned else bits


def after(values, gate):
    return lax.optimization_barrier((values, gate))


def half_window(rows):
    return min(rows, (rows + 15) // 16 * 8)


def half_of(values, index):
    rows = values.shape[1]
    window = half_window(rows)
    return lax.dynamic_slice_in_dim(values, index * (rows - window), window, 1)


def sent_half(values, bit):
    return swap_rep(half_of(values, 1 - (lax.axis_index("rep") // bit) % 2), bit)


def kept_half(values, bit):
    return half_of(values, (lax.axis_index("rep") // bit) % 2)


def add(keep, other):
    return (keep.astype(f32) + other.astype(f32)).astype(low)


def join(values, other, bit, rows):
    window = values.shape[1]
    upper = (lax.axis_index("rep") // bit) % 2 != 0
    first = jnp.where(upper, other, values)
    second = jnp.where(upper, values, other)
    return jnp.concatenate([first, second[:, 2 * window - rows :]], axis=1)


class Chain:
    def __init__(self, steps):
        self.steps = steps
        self.take(None)

    def take(self, got):
        try:
            self.waits, self.holds = self.steps.send(got)
        except StopIteration as end:
            self.waits, self.holds = None, end.value

    def advance(self, previous, gate=()):
        if self.waits is not None:
            if previous is self:
                waits, gate = after(self.waits, gate)
            else:
                waits, (previous.holds, gate) = after(self.waits, (previous.holds, gate))
            self.take((waits, self.holds))
        return gate


def scatter_steps(lanes, orders):
    sizes = []
    for step in range(len(orders[0])):
        sizes.append(lanes[0].shape[1])
        others, held = yield (
            tuple(sent_half(v, order[step]) for v, order in zip(lanes, orders)),
            tuple(lanes),
        )
        lanes = [
            add(kept_half(v, order[step]), other) for v, other, order in zip(held, others, orders)
        ]
    return list(lax.optimization_barrier(tuple(lanes))), sizes


def gather_steps(lanes, orders, sizes):
    for step in reversed(range(len(orders[0]))):
        others, lanes = yield (
            tuple(swap_rep(v, order[step]) for v, order in zip(lanes, orders)),
            tuple(lanes),
        )
        lanes = [
            join(v, other, order[step], sizes[step])
            for v, other, order in zip(lanes, others, orders)
        ]
    return lanes


def exchange_steps(blocks):
    size = lax.axis_size("shard")
    index = lax.axis_index("shard")
    pieces = [lax.dynamic_index_in_dim(blocks, index ^ o, 0, keepdims=True) for o in range(size)]
    others, first = yield tuple(swap(pieces[o], o) for o in range(1, size)), pieces[0]
    result = jnp.zeros_like(blocks)
    for o, piece in enumerate((first,) + tuple(others)):
        result = lax.dynamic_update_slice_in_dim(result, piece, index ^ o, 0)
    return result


def plain_sum(values, order):
    lanes, sizes = yield from scatter_steps([values], [order])
    lanes = yield from gather_steps(lanes, [order], sizes)
    return lanes[0]


def turned_sum(values, order):
    lanes, sizes = yield from scatter_steps([values], [order])
    blocks = yield from exchange_steps(lanes[0])
    columns = jnp.concatenate([blocks[i] for i in range(blocks.shape[0])], axis=1)
    lanes = yield from gather_steps([columns[None]], [order], sizes)
    return lanes[0][0]


def mixer_sum(first, second, orders, own):
    lanes, sizes = yield from scatter_steps([first, second], orders)
    blocks = yield from exchange_steps(
        jnp.concatenate([lanes[0], lanes[1][:, :, :own]], axis=2)
    )
    count = blocks.shape[0]
    parts = [
        jnp.concatenate([blocks[s, :, i * own : (i + 1) * own] for s in range(count)], axis=1)
        for i in range(3)
    ]
    output = jnp.concatenate([lanes[1][i, :, own:] for i in range(count)], axis=1)
    lanes = [
        jnp.concatenate(parts[:2], axis=1)[None],
        jnp.concatenate([parts[2], output], axis=1)[None],
    ]
    lanes = yield from gather_steps(lanes, orders, sizes)
    return lanes[0][0], lanes[1][0]


def shard_sum(parts):
    for bit in reversed(bits_far_first()):
        half = parts.shape[0] // 2
        (other,), kept = yield (swap(parts[half:].astype(low), bit),), parts[:half]
        parts = kept + other.astype(f32)
    return parts


def vector_sum(partial, complete, own_part):
    for bit in bits_far_first():
        (other,), partial = yield (swap(partial, bit),), partial
        partial = partial + other
    total = jnp.concatenate([own_part(p) for p in partial] + complete)
    for bit in rep_bits(False):
        (other,), total = yield (swap_rep(total, bit),), total
        total = total + other
    return total


def is_neighbour_offset(offset):
    return offset & (offset + 1) == 0


def send_halves(blocks, first, last):
    index = lax.axis_index("shard")
    size = lax.axis_size("shard")
    half = blocks.shape[1] // 2
    part = (lax.axis_index("rep") % 2) * half
    pieces = []
    for offset in range(size):
        piece = lax.dynamic_index_in_dim(blocks, index ^ offset, 0, keepdims=True)
        if offset >= 2:
            piece = lax.dynamic_slice_in_dim(piece, part, half, 1)
        if offset:
            if is_neighbour_offset(offset):
                edge = jnp.where((index ^ offset) == index + 1, last, first)
                edge = edge.reshape(1, -1, piece.shape[2])
                piece = jnp.concatenate([piece, edge], axis=1)
            piece = swap(piece, offset)
        pieces.append(piece)
    return pieces


def take_edges(pieces, shape):
    index = lax.axis_index("shard")
    before = behind = None
    rest = pieces[:1]
    count = shape[0] * shape[1] // pieces[0].shape[2]
    for offset in range(1, len(pieces)):
        piece = pieces[offset]
        if is_neighbour_offset(offset):
            edge = piece[0, piece.shape[1] - count :].reshape(shape)
            piece = piece[:, : piece.shape[1] - count]
            if before is None:
                before = behind = edge
            before = jnp.where((index ^ offset) == index - 1, edge, before)
            behind = jnp.where((index ^ offset) == index + 1, edge, behind)
        rest.append(piece)
    return before, behind, rest


def join_halves(pieces):
    index = lax.axis_index("shard")
    upper = lax.axis_index("rep") % 2 != 0
    full = pieces[0].shape[1]
    count = len(pieces)
    if count > 2:
        mine = jnp.concatenate(pieces[2:], axis=0)
        other = swap_rep(mine, 1)
        halves = jnp.concatenate(
            [jnp.where(upper, other, mine), jnp.where(upper, mine, other)], axis=1
        )
        pieces = pieces[:2] + [halves[i : i + 1] for i in range(count - 2)]
    result = jnp.zeros((count,) + pieces[0].shape[1:], pieces[0].dtype)
    for offset, piece in enumerate(pieces):
        result = lax.dynamic_update_slice_in_dim(result, piece, index ^ offset, 0)
    return result


def visible_part(scores, top, block, fill):
    rows = lax.broadcasted_iota(jnp.int32, (block, block), 0)
    cols = lax.broadcasted_iota(jnp.int32, (block, block), 1)
    last = jnp.where(rows <= cols, scores[top:], fill)
    if top == 0:
        return last
    return jnp.concatenate([scores[:top], last], axis=0)


def turn(values):
    return values.astype(f32).T


def forward_kernel(blocks, block, place, q_ref, k_ref, v_ref, o_ref, low_ref, log_ref, k_rows, v_cols):
    for i in range(blocks):
        here = pl.ds(pl.multiple_of(place[i] * block, block), block)
        there = pl.ds(i * block, block)
        k_rows[there, :] = turn(k_ref[:, here]).astype(low)
        v_cols[:, there] = v_ref[:, here]
    for i in range(blocks):
        here = pl.ds(pl.multiple_of(place[i] * block, block), block)
        top = i * block
        count = top + block
        q_cols = q_ref[:, here] * jnp.asarray(score_scale, low)
        scores = contract(k_rows[:count, :], q_cols, 1, 0)
        scores = visible_part(scores, top, block, -jnp.inf)
        peak = jnp.max(scores, axis=0, keepdims=True)
        weights = jnp.exp(scores - peak)
        total = jnp.sum(weights, axis=0, keepdims=True)
        mixed = contract(v_cols[:, :count], weights.astype(low), 1, 0) / total
        o_ref[:, here] = mixed
        low_ref[:, here] = mixed.astype(low)
        log_ref[0, :, here] = peak + jnp.log(total)


def backward_kernel(
    blocks,
    block,
    place,
    q_ref,
    k_ref,
    v_ref,
    g_ref,
    o_ref,
    log_ref,
    dq_ref,
    dk_ref,
    dv_ref,
    k_rows,
    v_rows,
    k_cols,
    dk_rows,
    dv_rows,
):
    for i in range(blocks):
        here = pl.ds(pl.multiple_of(place[i] * block, block), block)
        there = pl.ds(i * block, block)
        k_rows[there, :] = turn(k_ref[:, here]).astype(low)
        v_rows[there, :] = turn(v_ref[:, here]).astype(low)
        k_cols[:, there] = k_ref[:, here]
    for i in reversed(range(blocks)):
        here = pl.ds(pl.multiple_of(place[i] * block, block), block)
        top = i * block
        count = top + block
        q_cols = q_ref[:, here] * jnp.asarray(score_scale, low)
        g_cols = g_ref[:, here]
        q_rows = turn(q_cols).astype(low)
        g_rows = turn(g_cols).astype(low)
        correction = jnp.sum(g_cols.astype(f32) * o_ref[:, here], axis=0, keepdims=True)
        scores = contract(k_rows[:count, :], q_cols, 1, 0)
        probs = jnp.exp(scores - log_ref[0, :, here])
        probs = visible_part(probs, top, block, 0.0)
        grad_probs = contract(v_rows[:count, :], g_cols, 1, 0)
        grad_scores = (probs * (grad_probs - correction)).astype(low)
        dv_part = contract(probs.astype(low), g_rows, 1, 0)
        dk_part = contract(grad_scores, q_rows, 1, 0)
        if i == blocks - 1:
            dv_rows[:count, :] = dv_part
            dk_rows[:count, :] = dk_part
        else:
            dv_rows[:count, :] += dv_part
            dk_rows[:count, :] += dk_part
        dq = contract(k_cols[:, :count], grad_scores, 1, 0) * score_scale
        dq_ref[:, here] = dq.astype(low)
    for i in range(blocks):
        here = pl.ds(pl.multiple_of(place[i] * block, block), block)
        there = pl.ds(i * block, block)
        dk_ref[:, here] = dk_rows[there, :].T.astype(low)
        dv_ref[:, here] = dv_rows[there, :].T.astype(low)


def head_spec(size, length, first):
    return pl.BlockSpec((size, length), lambda h, place: (first + h, 0))


def attend_forward(place, projected, heads, block):
    size = projected.shape[0] // (3 * heads)
    length = projected.shape[1]
    blocks = length // block
    row = pl.BlockSpec((1, 1, length), lambda h, place: (h, 0, 0))
    return pl.pallas_call(
        functools.partial(forward_kernel, blocks, block),
        grid_spec=pltpu.PrefetchScalarGridSpec(
            num_scalar_prefetch=1,
            grid=(heads,),
            in_specs=[
                head_spec(size, length, 0),
                head_spec(size, length, heads),
                head_spec(size, length, 2 * heads),
            ],
            out_specs=[head_spec(size, length, 0), head_spec(size, length, 0), row],
            scratch_shapes=[
                pltpu.VMEM((length, size), low),
                pltpu.VMEM((size, length), low),
            ],
        ),
        out_shape=[
            jax.ShapeDtypeStruct((heads * size, length), f32),
            jax.ShapeDtypeStruct((heads * size, length), low),
            jax.ShapeDtypeStruct((heads, 1, length), f32),
        ],
        cost_estimate=pl.CostEstimate(
            flops=4 * heads * length * length * size,
            bytes_accessed=heads * length * size * 12,
            transcendentals=heads * length * length,
        ),
        compiler_params=pltpu.CompilerParams(vmem_limit_bytes=32 * 1024 * 1024),
        name="attend_forward",
    )(place, projected, projected, projected)


def attend_backward(place, projected, grad, mixed, log_total, heads, block):
    size = projected.shape[0] // (3 * heads)
    length = projected.shape[1]
    blocks = length // block
    row = pl.BlockSpec((1, 1, length), lambda h, place: (h, 0, 0))
    out = jax.ShapeDtypeStruct((heads * size, length), low)
    return pl.pallas_call(
        functools.partial(backward_kernel, blocks, block),
        grid_spec=pltpu.PrefetchScalarGridSpec(
            num_scalar_prefetch=1,
            grid=(heads,),
            in_specs=[
                head_spec(size, length, 0),
                head_spec(size, length, heads),
                head_spec(size, length, 2 * heads),
                head_spec(size, length, 0),
                head_spec(size, length, 0),
                row,
            ],
            out_specs=[head_spec(size, length, 0)] * 3,
            scratch_shapes=[
                pltpu.VMEM((length, size), low),
                pltpu.VMEM((length, size), low),
                pltpu.VMEM((size, length), low),
                pltpu.VMEM((length, size), f32),
                pltpu.VMEM((length, size), f32),
            ],
        ),
        out_shape=[out, out, out],
        cost_estimate=pl.CostEstimate(
            flops=10 * heads * length * length * size,
            bytes_accessed=heads * length * size * 20,
            transcendentals=heads * length * length,
        ),
        compiler_params=pltpu.CompilerParams(vmem_limit_bytes=32 * 1024 * 1024),
        name="attend_backward",
    )(place, projected, projected, projected, grad, mixed, log_total)


def local(
    block_input,
    first_gain,
    first_shift,
    query_key_value_weight,
    query_bias,
    value_bias,
    attention_output_weight,
    attention_output_bias,
    second_gain,
    second_shift,
    up_weight,
    up_bias,
    down_weight,
    down_bias,
    cotangent,
):
    shards = lax.axis_size("shard")
    index = lax.axis_index("shard")
    seqs, span, width = block_input.shape
    size = width // HEADS
    own = width // shards
    hidden = up_bias.shape[0]
    starts = [d * own // size for d in range(shards)]
    heads = max(-(-(d + 1) * own // size) - starts[d] for d in range(shards))
    window = heads * size
    pad = window - own
    start = index * own // size
    skew = index * own - start * size
    order = relative_order()
    inverse_order = jnp.asarray([order.index(o) for o in range(shards)], jnp.int32)
    place = inverse_order[jnp.arange(shards, dtype=jnp.int32) ^ index]

    own_input = block_input.reshape(seqs * span, width)
    inputs_all = gather_relative(own_input)
    vectors = gather_absolute(
        jnp.stack(
            [
                first_gain,
                first_shift,
                query_bias,
                value_bias,
                attention_output_bias,
                second_gain,
                second_shift,
                down_bias,
            ]
        )
    )
    vectors = vectors.transpose(1, 0, 2).reshape(8, width)
    gain_one, shift_one, bias_query, bias_value, bias_out, gain_two, shift_two, bias_down = (
        vectors[i] for i in range(8)
    )
    weight_in_chain = Chain(
        exchange_steps(
            jnp.stack(
            [
                jnp.concatenate(
                    [
                        query_key_value_weight[
                            :, part * width + s * size : part * width + s * size + window
                        ]
                        for part in range(3)
                    ],
                    axis=1,
                )
                for s in starts
            ]
        )
    ))
    rows = shards * seqs * span
    normed_all, _ = normalize(inputs_all.astype(f32))
    hidden_one = (normed_all * gain_one + shift_one).astype(low)
    up_blocks = jnp.stack([up_weight[:, s * hidden : (s + 1) * hidden] for s in range(shards)])
    own_branch = cotangent.reshape(seqs * span, width).astype(low)
    hidden_one, up_blocks, own_branch = weight_in_chain.advance(
        weight_in_chain, (hidden_one, up_blocks, own_branch)
    )
    weight_in = weight_in_chain.holds.reshape(width, 3 * window)
    up_pieces = send_halves(
        up_blocks, attention_output_weight[:pad], attention_output_weight[own - pad :]
    )
    far_branch = swap(own_branch, bits_far_first()[0])
    grad_out = cotangent.reshape(seqs * span, width)

    def own_rows(values):
        return lax.dynamic_slice_in_dim(values, skew, own, 0)

    bias_window = jnp.concatenate(
        [
            lax.dynamic_slice_in_dim(bias_query, start * size, window, 0),
            jnp.zeros((window,), low),
            lax.dynamic_slice_in_dim(bias_value, start * size, window, 0),
        ]
    ).astype(f32)
    projected = (contract(weight_in, hidden_one, 0, 1) + bias_window[:, None]).astype(low)

    def per_sequence(values):
        lead = values.shape[:-1]
        split = values.reshape(lead + (shards, seqs, span))
        return [split[..., :, s, :].reshape(lead + (shards * span,)) for s in range(seqs)]

    def join_sequences(parts):
        if seqs == 1:
            return parts[0]
        lead = parts[0].shape[:-1]
        joined = jnp.stack([p.reshape(lead + (shards, span)) for p in parts], axis=-2)
        return joined.reshape(lead + (rows,))

    projected_parts = per_sequence(projected) if seqs > 1 else [projected]
    forward_parts = [attend_forward(place, p, heads, span) for p in projected_parts]
    attended = join_sequences([p[1] for p in forward_parts])
    attended, (up_pieces, far_branch) = after(attended, (up_pieces, far_branch))
    branch = gather_relative(jnp.concatenate([own_branch, far_branch], axis=0), slice(1, None))
    before_rows, behind_rows, up_pieces = take_edges(up_pieces, (pad, width))
    weight_out_window = lax.dynamic_slice_in_dim(
        jnp.concatenate([before_rows, attention_output_weight, behind_rows], axis=0),
        pad - skew,
        window,
        0,
    )
    attended = own_rows(attended)
    weight_up = join_halves(up_pieces).reshape(width, hidden)
    mixed_sum = scatter_relative(
        contract(attended, attention_output_weight, 0, 0)
    )
    layer_input = own_input.astype(f32)
    middle = layer_input + mixed_sum + bias_out

    normed_two, inverse_two = normalize(middle)
    hidden_two = gather_relative((normed_two * gain_two + shift_two).astype(low))
    before = contract(hidden_two, weight_up, 1, 0) + up_bias
    activated, slope = gelu_parts(before)
    activated = activated.astype(low)
    grad_before = (contract(branch, down_weight, 1, 1) * slope).astype(low)
    hidden_two_sum = contract(grad_before, weight_up, 1, 1)
    hidden_two_sum, late_before, late_active = lax.optimization_barrier(
        (hidden_two_sum, grad_before, activated)
    )
    hidden_chain = Chain(shard_sum(hidden_two_sum))
    late_before = hidden_chain.advance(hidden_chain, late_before)
    while hidden_chain.waits is not None:
        hidden_chain.advance(hidden_chain)
    grad_hidden_two = hidden_chain.holds
    near, far = rep_bits(False), rep_bits(True)
    down_weight_grad = contract(late_active, branch, 0, 0).astype(low)[None]
    down_chain = Chain(plain_sum(down_weight_grad, near))
    up_weight_grad = contract(hidden_two, late_before, 0, 0).astype(low)
    up_weight_grad = up_weight_grad.reshape(shards, own, hidden)
    down_sum = contract(late_active, down_weight, 1, 0)
    grad_middle = grad_out + norm_back(grad_hidden_two, normed_two, inverse_two, gain_two)
    up_chain = Chain(turned_sum(up_weight_grad, far))
    late_middle = down_chain.advance(up_chain, grad_middle)

    grad_mixed = gather_relative(grad_middle.astype(low))
    up_chain.advance(down_chain)
    block_chain = Chain(shard_sum(down_sum))
    late_mixed = block_chain.advance(up_chain, grad_mixed)
    grad_attended = contract(weight_out_window, grad_mixed, 1, 1).astype(low)
    grad_attended, (down_chain.holds, up_chain.holds, block_chain.holds) = after(
        grad_attended, (down_chain.holds, up_chain.holds, block_chain.holds)
    )
    grad_parts = per_sequence(grad_attended) if seqs > 1 else [grad_attended]
    backward_parts = [
        attend_backward(place, p, g, f[0], f[2], heads, span)
        for p, g, f in zip(projected_parts, grad_parts, forward_parts)
    ]
    grad_query, grad_key, grad_value = (
        join_sequences([p[i] for p in backward_parts]) for i in range(3)
    )
    own_query, own_key, own_value = (own_rows(g) for g in (grad_query, grad_key, grad_value))
    output_weight_grad = contract(attended, grad_mixed, 1, 0).astype(low)
    late_query = block_chain.advance(up_chain, own_query)
    down_chain.advance(block_chain)
    up_chain.advance(down_chain)

    (grad_query, grad_key, grad_value), (down_chain.holds, up_chain.holds) = after(
        (grad_query, grad_key, grad_value), (down_chain.holds, up_chain.holds)
    )
    own_query, own_key, own_value = (own_rows(g) for g in (grad_query, grad_key, grad_value))
    own_projected = jnp.concatenate([own_query, own_key, own_value], axis=0)

    def by_owner(gradient):
        return gradient.reshape(shards, own, gradient.shape[1])

    first_part = by_owner(contract(hidden_one, own_projected[: 2 * own], 0, 1).astype(low))
    second_part = by_owner(contract(hidden_one, own_value, 0, 1).astype(low))
    output_blocks = jnp.stack(
        [output_weight_grad[:, s * own : (s + 1) * own] for s in range(shards)]
    )
    second_part = jnp.concatenate([second_part, output_blocks], axis=2)
    mixer_chain = Chain(mixer_sum(first_part, second_part, [near, far], own))
    line = jnp.arange(window)
    mine = ((line >= skew) & (line < skew + own))[:, None]
    grad_projected = jnp.concatenate(
        [jnp.where(mine, g, jnp.zeros_like(g)) for g in (grad_query, grad_key, grad_value)], axis=0
    )
    hidden_chain = Chain(shard_sum(contract(grad_projected, weight_in, 0, 1)))
    chain = up_chain
    for step in (
        [hidden_chain, down_chain, mixer_chain, up_chain, down_chain, hidden_chain]
        + [block_chain, hidden_chain] * shards
    ):
        step.advance(chain)
        chain = step
    block_output = middle + block_chain.holds + bias_down
    grad_hidden_one = hidden_chain.holds
    normed_one, inverse_one = normalize(layer_input)
    input_grad = late_middle + norm_back(grad_hidden_one, normed_one, inverse_one, gain_one)

    def own_part(values):
        return lax.dynamic_slice_in_dim(values, index * own, own, 0)

    partial = jnp.stack(
        [
            jnp.sum(grad_hidden_one * normed_one, axis=0),
            jnp.sum(grad_hidden_one, axis=0),
            jnp.sum(grad_hidden_two * normed_two, axis=0),
            jnp.sum(grad_hidden_two, axis=0),
        ]
    )
    vector_chain = Chain(
        vector_sum(
            partial,
            [
                jnp.sum(late_query.astype(f32), axis=1),
                jnp.sum(own_value.astype(f32), axis=1),
                own_part(jnp.sum(late_mixed.astype(f32), axis=0)),
                own_part(jnp.sum(branch.astype(f32), axis=0)),
                jnp.sum(grad_before.astype(f32), axis=0),
            ],
            own_part,
        )
    )
    down, up, mixer, vector = chains = [down_chain, up_chain, mixer_chain, vector_chain]
    chain = hidden_chain
    for step in (
        [up, vector, vector, vector, mixer, down, vector, vector, up]
        + [mixer, mixer, up, mixer, down, mixer, up]
        + [down, up, vector] * 8
    ):
        if step.waits is not None:
            step.advance(chain)
            chain = step
    grads = (down.holds[0].astype(f32), up.holds.astype(f32))
    while mixer.waits is not None:
        grads = mixer.advance(mixer, grads)
    down_weight_grad, up_weight_grad = grads
    complete = vector_chain.holds
    first_part, second_part = mixer_chain.holds
    input_weight_grad = jnp.concatenate([first_part, second_part[:, :width]], axis=1)
    output_weight_grad = second_part[:, width:]
    (
        first_gain_grad,
        first_shift_grad,
        second_gain_grad,
        second_shift_grad,
        query_bias_grad,
        value_bias_grad,
        output_bias_grad,
        down_bias_grad,
    ) = (complete[i * own : (i + 1) * own] for i in range(8))
    up_bias_grad = complete[8 * own :]
    return (
        block_output.reshape(seqs, span, width),
        input_grad.reshape(seqs, span, width),
        first_gain_grad,
        first_shift_grad,
        input_weight_grad.astype(f32),
        query_bias_grad,
        value_bias_grad,
        output_weight_grad.astype(f32),
        output_bias_grad,
        second_gain_grad,
        second_shift_grad,
        up_weight_grad,
        up_bias_grad,
        down_weight_grad,
        down_bias_grad,
    )


def solution(mesh):
    matrix, vector, tokens = P("shard", None), P("shard"), P("rep", "shard", None)
    return jax.shard_map(
        local,
        mesh=mesh,
        in_specs=(
            tokens,
            vector,
            vector,
            matrix,
            vector,
            vector,
            matrix,
            vector,
            vector,
            vector,
            matrix,
            vector,
            matrix,
            vector,
            tokens,
        ),
        out_specs=(
            tokens,
            tokens,
            vector,
            vector,
            matrix,
            vector,
            vector,
            matrix,
            vector,
            vector,
            vector,
            matrix,
            vector,
            matrix,
            vector,
        ),
        check_vma=False,
    )
```

```python
import functools

import jax
import jax.numpy as jnp
from jax import lax
from jax.experimental import pallas as pl
from jax.experimental.pallas import tpu as pltpu
from jax.sharding import PartitionSpec as P

HEADS = 17

epsilon = 1e-05
score_scale = 0.125
low = jnp.bfloat16
f32 = jnp.float32


def normalize(values):
    centre = jnp.mean(values, axis=-1, keepdims=True)
    centred = values - centre
    inverse = lax.rsqrt(jnp.mean(centred * centred, axis=-1, keepdims=True) + epsilon)
    return (centred * inverse, inverse)


def norm_back(grad, normed, inverse, gain):
    scaled = grad * gain
    first = jnp.mean(scaled, axis=-1, keepdims=True)
    second = jnp.mean(scaled * normed, axis=-1, keepdims=True)
    return inverse * (scaled - first - normed * second)


def gelu_parts(values):
    cumulative = 0.5 * (1.0 + lax.erf(values * 0.7071067811865476))
    density = jnp.exp(-0.5 * values * values) * 0.3989422804014327
    return values * cumulative, cumulative + values * density


def contract(left, right, left_dim, right_dim):
    return lax.dot_general(
        left, right, (((left_dim,), (right_dim,)), ((), ())), preferred_element_type=f32
    )


def swap(values, bit):
    size = lax.axis_size("shard")
    return lax.ppermute(values, "shard", [(i, i ^ bit) for i in range(size)])


def bits_far_first():
    bit = lax.axis_size("shard") // 2
    bits = []
    while bit:
        bits.append(bit)
        bit //= 2
    return bits


def relative_order():
    order = [0]
    for bit in bits_far_first():
        order = order + [o ^ bit for o in order]
    return order


def gather_relative(block, steps=slice(None)):
    for bit in bits_far_first()[steps]:
        block = jnp.concatenate([block, swap(block, bit)], axis=0)
    return block


def gather_absolute(block):
    index = lax.axis_index("shard")
    stack = block[None]
    for bit in bits_far_first():
        other = swap(stack, bit)
        upper = (index & bit) != 0
        pair = jnp.stack(
            [jnp.where(upper, other, stack), jnp.where(upper, stack, other)], axis=1
        )
        stack = pair.reshape((2 * stack.shape[0],) + block.shape)
    return stack


def scatter_relative(parts):
    for bit in reversed(bits_far_first()):
        half = parts.shape[0] // 2
        other = swap(parts[half:].astype(low), bit)
        parts = parts[:half] + other.astype(f32)
    return parts


def swap_rep(values, bit):
    size = lax.axis_size("rep")
    return lax.ppermute(values, "rep", [(i, i ^ bit) for i in range(size)])


def rep_bits(turned):
    bits, bit = [], 1
    while bit < lax.axis_size("rep"):
        bits.append(bit)
        bit *= 2
    return bits[1:2] + bits[:1] + bits[2:] if turned else bits


def after(values, gate):
    return lax.optimization_barrier((values, gate))


def half_window(rows):
    return min(rows, (rows + 15) // 16 * 8)


def half_of(values, index):
    rows = values.shape[1]
    window = half_window(rows)
    return lax.dynamic_slice_in_dim(values, index * (rows - window), window, 1)


def sent_half(values, bit):
    return swap_rep(half_of(values, 1 - (lax.axis_index("rep") // bit) % 2), bit)


def kept_half(values, bit):
    return half_of(values, (lax.axis_index("rep") // bit) % 2)


def add(keep, other):
    return (keep.astype(f32) + other.astype(f32)).astype(low)


def join(values, other, bit, rows):
    window = values.shape[1]
    upper = (lax.axis_index("rep") // bit) % 2 != 0
    first = jnp.where(upper, other, values)
    second = jnp.where(upper, values, other)
    return jnp.concatenate([first, second[:, 2 * window - rows :]], axis=1)


class Chain:
    def __init__(self, steps):
        self.steps = steps
        self.take(None)

    def take(self, got):
        try:
            self.waits, self.holds = self.steps.send(got)
        except StopIteration as end:
            self.waits, self.holds = None, end.value

    def advance(self, previous, gate=()):
        if self.waits is not None:
            if previous is self:
                waits, gate = after(self.waits, gate)
            else:
                waits, (previous.holds, gate) = after(self.waits, (previous.holds, gate))
            self.take((waits, self.holds))
        return gate


def scatter_steps(lanes, orders):
    sizes = []
    for step in range(len(orders[0])):
        sizes.append(lanes[0].shape[1])
        others, held = yield (
            tuple(sent_half(v, order[step]) for v, order in zip(lanes, orders)),
            tuple(lanes),
        )
        lanes = [
            add(kept_half(v, order[step]), other) for v, other, order in zip(held, others, orders)
        ]
    return list(lax.optimization_barrier(tuple(lanes))), sizes


def gather_steps(lanes, orders, sizes):
    for step in reversed(range(len(orders[0]))):
        others, lanes = yield (
            tuple(swap_rep(v, order[step]) for v, order in zip(lanes, orders)),
            tuple(lanes),
        )
        lanes = [
            join(v, other, order[step], sizes[step])
            for v, other, order in zip(lanes, others, orders)
        ]
    return lanes


def exchange_steps(blocks):
    size = lax.axis_size("shard")
    index = lax.axis_index("shard")
    pieces = [lax.dynamic_index_in_dim(blocks, index ^ o, 0, keepdims=True) for o in range(size)]
    others, first = yield tuple(swap(pieces[o], o) for o in range(1, size)), pieces[0]
    result = jnp.zeros_like(blocks)
    for o, piece in enumerate((first,) + tuple(others)):
        result = lax.dynamic_update_slice_in_dim(result, piece, index ^ o, 0)
    return result


def plain_sum(values, order):
    lanes, sizes = yield from scatter_steps([values], [order])
    lanes = yield from gather_steps(lanes, [order], sizes)
    return lanes[0]


def turned_sum(values, order):
    lanes, sizes = yield from scatter_steps([values], [order])
    blocks = yield from exchange_steps(lanes[0])
    columns = jnp.concatenate([blocks[i] for i in range(blocks.shape[0])], axis=1)
    lanes = yield from gather_steps([columns[None]], [order], sizes)
    return lanes[0][0]


def mixer_sum(first, second, orders, own):
    lanes, sizes = yield from scatter_steps([first, second], orders)
    blocks = yield from exchange_steps(
        jnp.concatenate([lanes[0], lanes[1][:, :, :own]], axis=2)
    )
    count = blocks.shape[0]
    parts = [
        jnp.concatenate([blocks[s, :, i * own : (i + 1) * own] for s in range(count)], axis=1)
        for i in range(3)
    ]
    output = jnp.concatenate([lanes[1][i, :, own:] for i in range(count)], axis=1)
    lanes = [
        jnp.concatenate(parts[:2], axis=1)[None],
        jnp.concatenate([parts[2], output], axis=1)[None],
    ]
    lanes = yield from gather_steps(lanes, orders, sizes)
    return lanes[0][0], lanes[1][0]


def shard_sum(parts):
    for bit in reversed(bits_far_first()):
        half = parts.shape[0] // 2
        (other,), kept = yield (swap(parts[half:].astype(low), bit),), parts[:half]
        parts = kept + other.astype(f32)
    return parts


def vector_sum(partial, complete, own_part):
    for bit in bits_far_first():
        (other,), partial = yield (swap(partial, bit),), partial
        partial = partial + other
    total = jnp.concatenate([own_part(p) for p in partial] + complete)
    for bit in rep_bits(False):
        (other,), total = yield (swap_rep(total, bit),), total
        total = total + other
    return total


def is_neighbour_offset(offset):
    return offset & (offset + 1) == 0


def send_halves(blocks, first, last):
    index = lax.axis_index("shard")
    size = lax.axis_size("shard")
    half = blocks.shape[1] // 2
    part = (lax.axis_index("rep") % 2) * half
    pieces = []
    for offset in range(size):
        piece = lax.dynamic_index_in_dim(blocks, index ^ offset, 0, keepdims=True)
        if offset >= 2:
            piece = lax.dynamic_slice_in_dim(piece, part, half, 1)
        if offset:
            if is_neighbour_offset(offset):
                edge = jnp.where((index ^ offset) == index + 1, last, first)
                edge = edge.reshape(1, -1, piece.shape[2])
                piece = jnp.concatenate([piece, edge], axis=1)
            piece = swap(piece, offset)
        pieces.append(piece)
    return pieces


def take_edges(pieces, shape):
    index = lax.axis_index("shard")
    before = behind = None
    rest = pieces[:1]
    count = shape[0] * shape[1] // pieces[0].shape[2]
    for offset in range(1, len(pieces)):
        piece = pieces[offset]
        if is_neighbour_offset(offset):
            edge = piece[0, piece.shape[1] - count :].reshape(shape)
            piece = piece[:, : piece.shape[1] - count]
            if before is None:
                before = behind = edge
            before = jnp.where((index ^ offset) == index - 1, edge, before)
            behind = jnp.where((index ^ offset) == index + 1, edge, behind)
        rest.append(piece)
    return before, behind, rest


def join_halves(pieces):
    index = lax.axis_index("shard")
    upper = lax.axis_index("rep") % 2 != 0
    full = pieces[0].shape[1]
    count = len(pieces)
    if count > 2:
        mine = jnp.concatenate(pieces[2:], axis=0)
        other = swap_rep(mine, 1)
        halves = jnp.concatenate(
            [jnp.where(upper, other, mine), jnp.where(upper, mine, other)], axis=1
        )
        pieces = pieces[:2] + [halves[i : i + 1] for i in range(count - 2)]
    result = jnp.zeros((count,) + pieces[0].shape[1:], pieces[0].dtype)
    for offset, piece in enumerate(pieces):
        result = lax.dynamic_update_slice_in_dim(result, piece, index ^ offset, 0)
    return result


def visible_part(scores, top, block, fill):
    rows = lax.broadcasted_iota(jnp.int32, (block, block), 0)
    cols = lax.broadcasted_iota(jnp.int32, (block, block), 1)
    last = jnp.where(rows <= cols, scores[top:], fill)
    if top == 0:
        return last
    return jnp.concatenate([scores[:top], last], axis=0)


def turn(values):
    return values.astype(f32).T


def forward_kernel(blocks, block, place, q_ref, k_ref, v_ref, o_ref, low_ref, log_ref, k_rows, v_cols):
    for i in range(blocks):
        here = pl.ds(pl.multiple_of(place[i] * block, block), block)
        there = pl.ds(i * block, block)
        k_rows[there, :] = turn(k_ref[:, here]).astype(low)
        v_cols[:, there] = v_ref[:, here]
    for i in range(blocks):
        here = pl.ds(pl.multiple_of(place[i] * block, block), block)
        top = i * block
        count = top + block
        q_cols = q_ref[:, here] * jnp.asarray(score_scale, low)
        scores = contract(k_rows[:count, :], q_cols, 1, 0)
        scores = visible_part(scores, top, block, -jnp.inf)
        peak = jnp.max(scores, axis=0, keepdims=True)
        weights = jnp.exp(scores - peak)
        total = jnp.sum(weights, axis=0, keepdims=True)
        mixed = contract(v_cols[:, :count], weights.astype(low), 1, 0) / total
        o_ref[:, here] = mixed
        low_ref[:, here] = mixed.astype(low)
        log_ref[0, :, here] = peak + jnp.log(total)


def backward_kernel(
    blocks,
    block,
    place,
    q_ref,
    k_ref,
    v_ref,
    g_ref,
    o_ref,
    log_ref,
    dq_ref,
    dk_ref,
    dv_ref,
    k_rows,
    v_rows,
    k_cols,
    dk_rows,
    dv_rows,
):
    for i in range(blocks):
        here = pl.ds(pl.multiple_of(place[i] * block, block), block)
        there = pl.ds(i * block, block)
        k_rows[there, :] = turn(k_ref[:, here]).astype(low)
        v_rows[there, :] = turn(v_ref[:, here]).astype(low)
        k_cols[:, there] = k_ref[:, here]
    for i in reversed(range(blocks)):
        here = pl.ds(pl.multiple_of(place[i] * block, block), block)
        top = i * block
        count = top + block
        q_cols = q_ref[:, here] * jnp.asarray(score_scale, low)
        g_cols = g_ref[:, here]
        q_rows = turn(q_cols).astype(low)
        g_rows = turn(g_cols).astype(low)
        correction = jnp.sum(g_cols.astype(f32) * o_ref[:, here], axis=0, keepdims=True)
        scores = contract(k_rows[:count, :], q_cols, 1, 0)
        probs = jnp.exp(scores - log_ref[0, :, here])
        probs = visible_part(probs, top, block, 0.0)
        grad_probs = contract(v_rows[:count, :], g_cols, 1, 0)
        grad_scores = (probs * (grad_probs - correction)).astype(low)
        dv_part = contract(probs.astype(low), g_rows, 1, 0)
        dk_part = contract(grad_scores, q_rows, 1, 0)
        if i == blocks - 1:
            dv_rows[:count, :] = dv_part
            dk_rows[:count, :] = dk_part
        else:
            dv_rows[:count, :] += dv_part
            dk_rows[:count, :] += dk_part
        dq = contract(k_cols[:, :count], grad_scores, 1, 0) * score_scale
        dq_ref[:, here] = dq.astype(low)
    for i in range(blocks):
        here = pl.ds(pl.multiple_of(place[i] * block, block), block)
        there = pl.ds(i * block, block)
        dk_ref[:, here] = dk_rows[there, :].T.astype(low)
        dv_ref[:, here] = dv_rows[there, :].T.astype(low)


def head_spec(size, length, first):
    return pl.BlockSpec((size, length), lambda h, place: (first + h, 0))


def attend_forward(place, projected, heads, block):
    size = projected.shape[0] // (3 * heads)
    length = projected.shape[1]
    blocks = length // block
    row = pl.BlockSpec((1, 1, length), lambda h, place: (h, 0, 0))
    return pl.pallas_call(
        functools.partial(forward_kernel, blocks, block),
        grid_spec=pltpu.PrefetchScalarGridSpec(
            num_scalar_prefetch=1,
            grid=(heads,),
            in_specs=[
                head_spec(size, length, 0),
                head_spec(size, length, heads),
                head_spec(size, length, 2 * heads),
            ],
            out_specs=[head_spec(size, length, 0), head_spec(size, length, 0), row],
            scratch_shapes=[
                pltpu.VMEM((length, size), low),
                pltpu.VMEM((size, length), low),
            ],
        ),
        out_shape=[
            jax.ShapeDtypeStruct((heads * size, length), f32),
            jax.ShapeDtypeStruct((heads * size, length), low),
            jax.ShapeDtypeStruct((heads, 1, length), f32),
        ],
        cost_estimate=pl.CostEstimate(
            flops=4 * heads * length * length * size,
            bytes_accessed=heads * length * size * 12,
            transcendentals=heads * length * length,
        ),
        compiler_params=pltpu.CompilerParams(vmem_limit_bytes=32 * 1024 * 1024),
        name="attend_forward",
    )(place, projected, projected, projected)


def attend_backward(place, projected, grad, mixed, log_total, heads, block):
    size = projected.shape[0] // (3 * heads)
    length = projected.shape[1]
    blocks = length // block
    row = pl.BlockSpec((1, 1, length), lambda h, place: (h, 0, 0))
    out = jax.ShapeDtypeStruct((heads * size, length), low)
    return pl.pallas_call(
        functools.partial(backward_kernel, blocks, block),
        grid_spec=pltpu.PrefetchScalarGridSpec(
            num_scalar_prefetch=1,
            grid=(heads,),
            in_specs=[
                head_spec(size, length, 0),
                head_spec(size, length, heads),
                head_spec(size, length, 2 * heads),
                head_spec(size, length, 0),
                head_spec(size, length, 0),
                row,
            ],
            out_specs=[head_spec(size, length, 0)] * 3,
            scratch_shapes=[
                pltpu.VMEM((length, size), low),
                pltpu.VMEM((length, size), low),
                pltpu.VMEM((size, length), low),
                pltpu.VMEM((length, size), f32),
                pltpu.VMEM((length, size), f32),
            ],
        ),
        out_shape=[out, out, out],
        cost_estimate=pl.CostEstimate(
            flops=10 * heads * length * length * size,
            bytes_accessed=heads * length * size * 20,
            transcendentals=heads * length * length,
        ),
        compiler_params=pltpu.CompilerParams(vmem_limit_bytes=32 * 1024 * 1024),
        name="attend_backward",
    )(place, projected, projected, projected, grad, mixed, log_total)


def local(
    block_input,
    first_gain,
    first_shift,
    query_key_value_weight,
    query_bias,
    value_bias,
    attention_output_weight,
    attention_output_bias,
    second_gain,
    second_shift,
    up_weight,
    up_bias,
    down_weight,
    down_bias,
    cotangent,
):
    shards = lax.axis_size("shard")
    index = lax.axis_index("shard")
    seqs, span, width = block_input.shape
    size = width // HEADS
    own = width // shards
    hidden = up_bias.shape[0]
    starts = [d * own // size for d in range(shards)]
    heads = max(-(-(d + 1) * own // size) - starts[d] for d in range(shards))
    window = heads * size
    pad = window - own
    start = index * own // size
    skew = index * own - start * size
    order = relative_order()
    inverse_order = jnp.asarray([order.index(o) for o in range(shards)], jnp.int32)
    place = inverse_order[jnp.arange(shards, dtype=jnp.int32) ^ index]

    own_input = block_input.reshape(seqs * span, width)
    inputs_all = gather_relative(own_input)
    vectors = gather_absolute(
        jnp.stack(
            [
                first_gain,
                first_shift,
                query_bias,
                value_bias,
                attention_output_bias,
                second_gain,
                second_shift,
                down_bias,
            ]
        )
    )
    vectors = vectors.transpose(1, 0, 2).reshape(8, width)
    gain_one, shift_one, bias_query, bias_value, bias_out, gain_two, shift_two, bias_down = (
        vectors[i] for i in range(8)
    )
    weight_in_chain = Chain(
        exchange_steps(
            jnp.stack(
            [
                jnp.concatenate(
                    [
                        query_key_value_weight[
                            :, part * width + s * size : part * width + s * size + window
                        ]
                        for part in range(3)
                    ],
                    axis=1,
                )
                for s in starts
            ]
        )
    ))
    rows = shards * seqs * span
    normed_all, _ = normalize(inputs_all.astype(f32))
    hidden_one = (normed_all * gain_one + shift_one).astype(low)
    up_blocks = jnp.stack([up_weight[:, s * hidden : (s + 1) * hidden] for s in range(shards)])
    own_branch = cotangent.reshape(seqs * span, width).astype(low)
    hidden_one, up_blocks, own_branch = weight_in_chain.advance(
        weight_in_chain, (hidden_one, up_blocks, own_branch)
    )
    weight_in = weight_in_chain.holds.reshape(width, 3 * window)
    up_pieces = send_halves(
        up_blocks, attention_output_weight[:pad], attention_output_weight[own - pad :]
    )
    far_branch = swap(own_branch, bits_far_first()[0])
    grad_out = cotangent.reshape(seqs * span, width)

    def own_rows(values):
        return lax.dynamic_slice_in_dim(values, skew, own, 0)

    bias_window = jnp.concatenate(
        [
            lax.dynamic_slice_in_dim(bias_query, start * size, window, 0),
            jnp.zeros((window,), low),
            lax.dynamic_slice_in_dim(bias_value, start * size, window, 0),
        ]
    ).astype(f32)
    projected = (contract(weight_in, hidden_one, 0, 1) + bias_window[:, None]).astype(low)

    def per_sequence(values):
        lead = values.shape[:-1]
        split = values.reshape(lead + (shards, seqs, span))
        return [split[..., :, s, :].reshape(lead + (shards * span,)) for s in range(seqs)]

    def join_sequences(parts):
        if seqs == 1:
            return parts[0]
        lead = parts[0].shape[:-1]
        joined = jnp.stack([p.reshape(lead + (shards, span)) for p in parts], axis=-2)
        return joined.reshape(lead + (rows,))

    projected_parts = per_sequence(projected) if seqs > 1 else [projected]
    forward_parts = [attend_forward(place, p, heads, span) for p in projected_parts]
    attended = join_sequences([p[1] for p in forward_parts])
    attended, (up_pieces, far_branch) = after(attended, (up_pieces, far_branch))
    branch = gather_relative(jnp.concatenate([own_branch, far_branch], axis=0), slice(1, None))
    before_rows, behind_rows, up_pieces = take_edges(up_pieces, (pad, width))
    weight_out_window = lax.dynamic_slice_in_dim(
        jnp.concatenate([before_rows, attention_output_weight, behind_rows], axis=0),
        pad - skew,
        window,
        0,
    )
    attended = own_rows(attended)
    weight_up = join_halves(up_pieces).reshape(width, hidden)
    mixed_sum = scatter_relative(
        contract(attended, attention_output_weight, 0, 0)
    )
    layer_input = own_input.astype(f32)
    middle = layer_input + mixed_sum + bias_out

    normed_two, inverse_two = normalize(middle)
    hidden_two = gather_relative((normed_two * gain_two + shift_two).astype(low))
    before = contract(hidden_two, weight_up, 1, 0) + up_bias
    activated, slope = gelu_parts(before)
    activated = activated.astype(low)
    grad_before = (contract(branch, down_weight, 1, 1) * slope).astype(low)
    hidden_two_sum = contract(grad_before, weight_up, 1, 1)
    hidden_two_sum, late_before, late_active = lax.optimization_barrier(
        (hidden_two_sum, grad_before, activated)
    )
    hidden_chain = Chain(shard_sum(hidden_two_sum))
    late_before = hidden_chain.advance(hidden_chain, late_before)
    while hidden_chain.waits is not None:
        hidden_chain.advance(hidden_chain)
    grad_hidden_two = hidden_chain.holds
    near, far = rep_bits(False), rep_bits(True)
    down_weight_grad = contract(late_active, branch, 0, 0).astype(low)[None]
    down_chain = Chain(plain_sum(down_weight_grad, near))
    up_weight_grad = contract(hidden_two, late_before, 0, 0).astype(low)
    up_weight_grad = up_weight_grad.reshape(shards, own, hidden)
    down_sum = contract(late_active, down_weight, 1, 0)
    grad_middle = grad_out + norm_back(grad_hidden_two, normed_two, inverse_two, gain_two)
    up_chain = Chain(turned_sum(up_weight_grad, far))
    late_middle = down_chain.advance(up_chain, grad_middle)

    grad_mixed = gather_relative(grad_middle.astype(low))
    up_chain.advance(down_chain)
    block_chain = Chain(shard_sum(down_sum))
    late_mixed = block_chain.advance(up_chain, grad_mixed)
    grad_attended = contract(weight_out_window, grad_mixed, 1, 1).astype(low)
    grad_attended, (down_chain.holds, up_chain.holds, block_chain.holds) = after(
        grad_attended, (down_chain.holds, up_chain.holds, block_chain.holds)
    )
    grad_parts = per_sequence(grad_attended) if seqs > 1 else [grad_attended]
    backward_parts = [
        attend_backward(place, p, g, f[0], f[2], heads, span)
        for p, g, f in zip(projected_parts, grad_parts, forward_parts)
    ]
    grad_query, grad_key, grad_value = (
        join_sequences([p[i] for p in backward_parts]) for i in range(3)
    )
    own_query, own_key, own_value = (own_rows(g) for g in (grad_query, grad_key, grad_value))
    output_weight_grad = contract(attended, grad_mixed, 1, 0).astype(low)
    late_query = block_chain.advance(up_chain, own_query)
    down_chain.advance(block_chain)
    up_chain.advance(down_chain)

    (grad_query, grad_key, grad_value), (down_chain.holds, up_chain.holds) = after(
        (grad_query, grad_key, grad_value), (down_chain.holds, up_chain.holds)
    )
    own_query, own_key, own_value = (own_rows(g) for g in (grad_query, grad_key, grad_value))
    own_projected = jnp.concatenate([own_query, own_key, own_value], axis=0)

    def by_owner(gradient):
        return gradient.reshape(shards, own, gradient.shape[1])

    first_part = by_owner(contract(hidden_one, own_projected[: 2 * own], 0, 1).astype(low))
    second_part = by_owner(contract(hidden_one, own_value, 0, 1).astype(low))
    output_blocks = jnp.stack(
        [output_weight_grad[:, s * own : (s + 1) * own] for s in range(shards)]
    )
    second_part = jnp.concatenate([second_part, output_blocks], axis=2)
    mixer_chain = Chain(mixer_sum(first_part, second_part, [near, far], own))
    line = jnp.arange(window)
    mine = ((line >= skew) & (line < skew + own))[:, None]
    grad_projected = jnp.concatenate(
        [jnp.where(mine, g, jnp.zeros_like(g)) for g in (grad_query, grad_key, grad_value)], axis=0
    )
    hidden_chain = Chain(shard_sum(contract(grad_projected, weight_in, 0, 1)))
    chain = up_chain
    for step in (
        [hidden_chain, down_chain, mixer_chain, up_chain, hidden_chain]
        + [block_chain, hidden_chain] * shards
    ):
        step.advance(chain)
        chain = step
    block_output = middle + block_chain.holds + bias_down
    grad_hidden_one = hidden_chain.holds
    normed_one, inverse_one = normalize(layer_input)
    input_grad = late_middle + norm_back(grad_hidden_one, normed_one, inverse_one, gain_one)

    def own_part(values):
        return lax.dynamic_slice_in_dim(values, index * own, own, 0)

    partial = jnp.stack(
        [
            jnp.sum(grad_hidden_one * normed_one, axis=0),
            jnp.sum(grad_hidden_one, axis=0),
            jnp.sum(grad_hidden_two * normed_two, axis=0),
            jnp.sum(grad_hidden_two, axis=0),
        ]
    )
    vector_chain = Chain(
        vector_sum(
            partial,
            [
                jnp.sum(late_query.astype(f32), axis=1),
                jnp.sum(own_value.astype(f32), axis=1),
                own_part(jnp.sum(late_mixed.astype(f32), axis=0)),
                own_part(jnp.sum(branch.astype(f32), axis=0)),
                jnp.sum(grad_before.astype(f32), axis=0),
            ],
            own_part,
        )
    )
    down, up, mixer, vector = chains = [down_chain, up_chain, mixer_chain, vector_chain]
    chain = hidden_chain
    for step in (
        [down, up, vector, vector, vector, mixer, vector, vector, up]
        + [mixer, down, mixer, up, mixer, mixer, down, up]
        + [down, up, vector] * 8
    ):
        if step.waits is not None:
            step.advance(chain)
            chain = step
    grads = (down.holds[0].astype(f32), up.holds.astype(f32))
    while mixer.waits is not None:
        grads = mixer.advance(mixer, grads)
    down_weight_grad, up_weight_grad = grads
    complete = vector_chain.holds
    first_part, second_part = mixer_chain.holds
    input_weight_grad = jnp.concatenate([first_part, second_part[:, :width]], axis=1)
    output_weight_grad = second_part[:, width:]
    (
        first_gain_grad,
        first_shift_grad,
        second_gain_grad,
        second_shift_grad,
        query_bias_grad,
        value_bias_grad,
        output_bias_grad,
        down_bias_grad,
    ) = (complete[i * own : (i + 1) * own] for i in range(8))
    up_bias_grad = complete[8 * own :]
    return (
        block_output.reshape(seqs, span, width),
        input_grad.reshape(seqs, span, width),
        first_gain_grad,
        first_shift_grad,
        input_weight_grad.astype(f32),
        query_bias_grad,
        value_bias_grad,
        output_weight_grad.astype(f32),
        output_bias_grad,
        second_gain_grad,
        second_shift_grad,
        up_weight_grad,
        up_bias_grad,
        down_weight_grad,
        down_bias_grad,
    )


def solution(mesh):
    matrix, vector, tokens = P("shard", None), P("shard"), P("rep", "shard", None)
    return jax.shard_map(
        local,
        mesh=mesh,
        in_specs=(
            tokens,
            vector,
            vector,
            matrix,
            vector,
            vector,
            matrix,
            vector,
            vector,
            vector,
            matrix,
            vector,
            matrix,
            vector,
            tokens,
        ),
        out_specs=(
            tokens,
            tokens,
            vector,
            vector,
            matrix,
            vector,
            vector,
            matrix,
            vector,
            vector,
            vector,
            matrix,
            vector,
            matrix,
            vector,
        ),
        check_vma=False,
    )
```
